256 devices in a mesh: row: 8 (over y, core), col: 32 (over z, x).
Axes of the slice: x: 4, y: 4, z: 8, core: 2. Of those that a mesh axis runs over, the one named last changes fastest.
Arguments:
- probes: bfloat16 [32, 8, 128, 4096], P(None, None, 'row', 'col'), may hold values from -8 to 8
- spread: float32 [8, 128, 4096], P(None, 'row', 'col'), may hold values from 0.05 to 6.5, as said below
- adv_x: float32 [8, 128, 4096], P(None, 'row', 'col'), may hold values from -0.6 to 0.6
- adv_y: float32 [8, 128, 4096], P(None, 'row', 'col'), may hold values from -0.6 to 0.6
- diffusivity: float32 [8, 128, 4096], P(None, 'row', 'col'), may hold values from 0.02 to 0.2
Outputs:
- basis: float32 [32, 8, 128, 4096], P(None, None, 'row', 'col')
- core_factor: float32 [32, 32], replicated
The draws below stay inside these ranges and needn't reach their ends.
Inputs may be any that keep to these rules, and one draw needn't show every extreme that they name: `spread`: positive everywhere; a rough factor times a scale that varies over the grid.
All inputs are finite; a program needn't handle non-finite values.
Results may differ from the reference program's by a relative error of at most 0.0003.
Values sent between devices are 32-bit elements; how exact they have to be, the bound alone decides.
A program may use at most 128 MiB of HBM per device.

```python
import math
import jax
import jax.numpy as jnp
from jax import lax

K = 32
L = 8
NX = 128
NY = 4096


def draw_spread(key, part):
    key = jax.random.fold_in(key, 3)
    rows = jnp.arange(NX, dtype=jnp.float32)[:, None] / NX
    cols = jnp.arange(NY, dtype=jnp.float32)[None, :] / NY
    ramp = 10.0 ** (0.5 * rows + 0.5 * cols)
    rough = jnp.exp(jax.random.uniform(key, (L, NX, NY), jnp.float32, -0.7, 0.7))
    return (0.3 * rough * ramp[None]).astype(jnp.float32)


def draw_probes(key, part):
    key = jax.random.fold_in(key, 5)
    key_shared = jax.random.fold_in(key, 0)
    key_base = jax.random.fold_in(key, 1)
    key_weight = jax.random.fold_in(key, 3)
    shared = jax.random.normal(key_shared, (4, L, NX, NY), jnp.float32)
    mixed = jax.random.normal(key_base, (K, L, NX, NY), jnp.float32)
    weights = 0.5 * jax.random.normal(key_weight, (K, 4), jnp.float32)
    for index in range(4):
        mixed = mixed + weights[:, index][:, None, None, None] * shared[index][None]
    return jnp.clip(mixed, -8.0, 8.0).astype(jnp.bfloat16)


def block_scale(stream_key, extent, cuts, low, high):
    gain = 1.0
    for axis_at, shards_of in cuts:
        draws = jax.random.uniform(jax.random.fold_in(jax.random.fold_in(stream_key, 6), axis_at), (shards_of,), jnp.float32, low / len(cuts), high / len(cuts))
        gain = gain * jnp.repeat(jnp.exp(draws), extent[axis_at] // shards_of).reshape((-1,) + (1,) * (len(extent) - 1 - axis_at))
    return gain


def setup_inputs(seed: int = 0) -> dict:
    key_list = jax.random.split(jax.random.key(seed), 6)
    return {
        "probes": draw_probes(jax.random.fold_in(key_list[5], 71), 0),
        "spread": draw_spread(jax.random.fold_in(key_list[5], 71), 0),
        "adv_x": jnp.clip(jax.random.uniform(key_list[2], (L, NX, NY), jnp.float32, -0.6, 0.6) * block_scale(key_list[2], (L, NX, NY), ((1, 8), (2, 32)), -0.4, 0.0), -0.6, 0.6),
        "adv_y": jnp.clip(jax.random.uniform(key_list[3], (L, NX, NY), jnp.float32, -0.6, 0.6) * block_scale(key_list[3], (L, NX, NY), ((1, 8), (2, 32)), -0.4, 0.0), -0.6, 0.6),
        "diffusivity": jnp.clip(jnp.exp(math.log(0.2) - 2.3025851 * jax.random.uniform(key_list[4], (L, NX, NY), jnp.float32) ** block_scale(key_list[4], (L, NX, NY), ((1, 8), (2, 32)), -0.2, 0.2)), 0.02, 0.2),
    }


def shifted(padded, dx, dy):
    nx = padded.shape[-2] - 4
    ny = padded.shape[-1] - 4
    return padded[..., 2 + dx:2 + dx + nx, 2 + dy:2 + dy + ny]

def first_diff(padded, axis_id):
    if axis_id == 0:
        return (-shifted(padded, 2, 0) + 8.0 * shifted(padded, 1, 0) - 8.0 * shifted(padded, -1, 0) + shifted(padded, -2, 0)) / 12.0
    return (-shifted(padded, 0, 2) + 8.0 * shifted(padded, 0, 1) - 8.0 * shifted(padded, 0, -1) + shifted(padded, 0, -2)) / 12.0

def laplace(padded):
    return shifted(padded, 1, 0) + shifted(padded, -1, 0) + shifted(padded, 0, 1) + shifted(padded, 0, -1) - 4.0 * shifted(padded, 0, 0)

def vertical(center):
    upper = jnp.concatenate([center[:, 1:], center[:, -1:]], axis=1)
    lower = jnp.concatenate([center[:, :1], center[:, :-1]], axis=1)
    return upper + lower - 2.0 * center

def tangent(padded, coef_x, coef_y, coef_d):
    center = shifted(padded, 0, 0)
    return center + coef_x * first_diff(padded, 0) + coef_y * first_diff(padded, 1) + coef_d * laplace(padded) + 0.2 * vertical(center)

def adjoint(padded, pad_x, pad_y, pad_d):
    center = shifted(padded, 0, 0)
    return center - first_diff(pad_x * padded, 0) - first_diff(pad_y * padded, 1) + laplace(pad_d * padded) + 0.2 * vertical(center)

def lower_chol(matrix):
    order = matrix.shape[0]
    lower = jnp.zeros_like(matrix)
    for col_id in range(order):
        resid = matrix[:, col_id] - jnp.dot(lower, lower[col_id, :], precision=lax.Precision.HIGHEST)
        pivot = jnp.sqrt(resid[col_id])
        below = jnp.arange(order) > col_id
        column = jnp.where(below, resid / pivot, jnp.float32(0.0))
        column = column.at[col_id].set(pivot)
        lower = lower.at[:, col_id].set(column)
    return lower

def lower_inverse(lower):
    order = lower.shape[0]
    eye = jnp.eye(order, dtype=jnp.float32)
    result = jnp.zeros_like(lower)
    for row_id in range(order):
        line = (eye[row_id] - jnp.dot(lower[row_id], result, precision=lax.Precision.HIGHEST)) / lower[row_id, row_id]
        result = result.at[row_id].set(line)
    return result

def factors(gram, core):
    gram = 0.5 * (gram + gram.T)
    core = 0.5 * (core + core.T)
    low_gram = lower_chol(gram)
    upper = low_gram.T
    inv_upper = lower_inverse(low_gram).T
    low_core = lower_chol(core)
    inv_low = lower_inverse(low_core)
    factor = jnp.dot(upper, inv_low.T, precision=lax.Precision.HIGHEST)
    return (inv_upper, factor)

def reference(probes, spread, adv_x, adv_y, diffusivity):

    def pad_cells(field):
        widths = [(0, 0)] * (field.ndim - 2) + [(2, 2), (2, 2)]
        return jnp.pad(field, widths)
    pad_x = pad_cells(adv_x)
    pad_y = pad_cells(adv_y)
    pad_d = pad_cells(diffusivity)

    def one_probe(probe):
        omega = probe.astype(jnp.float32)[None]
        scaled = spread * omega
        tang = tangent(pad_cells(scaled), adv_x, adv_y, diffusivity)
        back = adjoint(pad_cells(tang), pad_x, pad_y, pad_d)
        return (omega + spread * back)[0]
    sketch = lax.map(one_probe, probes)
    flat = sketch.reshape(K, -1)
    omega_flat = probes.astype(jnp.float32).reshape(K, -1)
    gram = jnp.dot(flat, flat.T, precision=lax.Precision.HIGHEST)
    core = jnp.dot(omega_flat, flat.T, precision=lax.Precision.HIGHEST)
    inv_upper, factor = factors(gram, core)
    count = float(L * NX * NY)
    basis = jnp.dot(inv_upper.T, flat, precision=lax.Precision.HIGHEST) * jnp.sqrt(jnp.float32(count))
    return (basis.reshape(K, L, NX, NY), factor)
```

```python
import functools

import jax
import jax.numpy as jnp
from jax import lax
from jax.experimental import pallas as pl
from jax.experimental.pallas import tpu as pltpu
from jax.sharding import PartitionSpec as P

MESH = pl.DeviceIdType.MESH
F32 = jnp.float32
BF16 = jnp.bfloat16
INNER = 4
NF = 8
SPR, CEN, XP, XM, XA, YP, YM, YA = range(NF)
LOW, HIGH, LEFT, RIGHT = range(4)


def lanes(shape):
    return lax.broadcasted_iota(jnp.int32, shape, 1)


def roll(x, shift):
    return pltpu.roll(x, shift % 128, 1)


def put_row(ref, r, value):
    n, rows, width = ref.shape
    ref.reshape(n * rows, width)[pl.ds(r, n, stride=rows), :] = value


def wide(coef, nprobe):
    return jnp.broadcast_to(coef[None], (nprobe // 8, 8, 128)).reshape(nprobe, 128)


def halo_kernel(
    dims,
    probes_hbm, spread_hbm, advx_hbm, advy_hbm, diff_hbm,
    z_hbm, g_ref,
    probes, coefs, turn, omega, scaled, tang, co, edge,
    pack, pack_l, pack_r, wrap, wrap_l, wrap_r,
    to_low, to_high, from_low, from_high,
    zbuf, gbuf, red0, red1, red2,
    in_sem, out_sem, send_sem, recv_sem, red_send, red_recv,
):
    nprobe, nlev, nrow, nrd, ncd = dims
    outer = ncd // INNER
    row = lax.axis_index("row")
    col = lax.axis_index("col")
    zi = col // INNER
    xi = lax.rem(col, INNER)
    half = nprobe // 2

    loads = []
    for i, src in enumerate((spread_hbm, advx_hbm, advy_hbm, diff_hbm)):
        loads.append(pltpu.make_async_copy(src, coefs.at[i], in_sem.at[i]))
    loads.append(pltpu.make_async_copy(probes_hbm, probes, in_sem.at[4]))
    for load in loads:
        load.start()

    barrier = pltpu.get_barrier_semaphore()
    for o in range(1, nrd):
        pl.semaphore_signal(barrier, inc=1, device_id=(lax.rem(row + o, nrd), col), device_id_type=MESH)
    for o in range(1, INNER):
        pl.semaphore_signal(
            barrier, inc=1, device_id=(row, zi * INNER + lax.rem(xi + o, INNER)), device_id_type=MESH
        )
    for o in range(1, outer):
        pl.semaphore_signal(
            barrier, inc=1, device_id=(row, lax.rem(zi + o, outer) * INNER + xi), device_id_type=MESH
        )
    for o in (1, ncd - 1):
        pl.semaphore_signal(barrier, inc=1, device_id=(row, lax.rem(col + o, ncd)), device_id_type=MESH)

    for load in loads[:4]:
        load.wait()

    def spread_coefs(l, carry):
        ax = coefs[1, l] * (1.0 / 12.0)
        ay = coefs[2, l] * (1.0 / 12.0)
        d = coefs[3, l]
        fields = (coefs[0, l], 0.6 - 4.0 * d, d + 8.0 * ax, d - 8.0 * ax, ax, d + 8.0 * ay, d - 8.0 * ay, ay)
        for f in range(NF):
            for r in range(nrow):
                co[f, l, r] = jnp.broadcast_to(fields[f][r : r + 1], (8, 128))
        return carry

    lax.fori_loop(0, nlev, spread_coefs, 0)

    lane16 = lanes((half, 128))
    quad = lax.rem(lane16, 4)
    lane_l = lanes((nlev, 128))
    quad_l = lax.rem(lane_l, 4)

    def packed(field):
        acc = jnp.zeros((nlev, 128), F32)
        for r in range(nrow):
            acc = jnp.where(lax.div(lane_l, 4) == r, roll(coefs[field, :, r, :], 4 * r + 2), acc)
        return jnp.where(lane_l < 64, acc, roll(acc, 64))

    pa = packed(2) * (1.0 / 12.0)
    pd = packed(3)
    edge[0] = jnp.where(quad_l == 1, pd + 8.0 * pa, jnp.where(quad_l == 2, pd - 8.0 * pa, 0.0))
    edge[1] = pa

    has = {LOW: row > 0, HIGH: row < nrd - 1, LEFT: col > 0, RIGHT: col < ncd - 1}
    target = {LOW: (row - 1, col), HIGH: (row + 1, col), LEFT: (row, col - 1), RIGHT: (row, col + 1)}
    rims = (
        {
            LOW: (lambda l: scaled.at[l, 2:4], lambda l: scaled.at[l, nrow + 2 : nrow + 4]),
            HIGH: (lambda l: scaled.at[l, nrow : nrow + 2], lambda l: scaled.at[l, 0:2]),
            LEFT: (lambda l: pack.at[l], lambda l: pack_r.at[l]),
            RIGHT: (lambda l: pack.at[l], lambda l: pack_l.at[l]),
        },
        {
            LOW: (lambda l: to_low.at[l], lambda l: from_high.at[l]),
            HIGH: (lambda l: to_high.at[l], lambda l: from_low.at[l]),
            LEFT: (lambda l: wrap.at[l], lambda l: wrap_r.at[l]),
            RIGHT: (lambda l: wrap.at[l], lambda l: wrap_l.at[l]),
        },
    )
    opposite = {LOW: HIGH, HIGH: LOW, LEFT: RIGHT, RIGHT: LEFT}

    def rim(phase, side, l):
        src, dst = rims[phase][side]
        return pltpu.make_async_remote_copy(
            src_ref=src(l),
            dst_ref=dst(l),
            send_sem=send_sem.at[phase, side, l],
            recv_sem=recv_sem.at[phase, side, l],
            device_id=target[side],
            device_id_type=MESH,
        )

    def send(phase, l):
        for side in (LOW, HIGH, LEFT, RIGHT):
            @pl.when(has[side])
            def _():
                rim(phase, side, l).start()

    def receive(phase, l):
        for side in (LEFT, RIGHT, LOW, HIGH):
            @pl.when(has[side])
            def _():
                rim(phase, opposite[side], l).wait_recv()

    def sent(phase, l):
        for side in (LOW, HIGH, LEFT, RIGHT):
            @pl.when(has[side])
            def _():
                rim(phase, side, l).wait_send()

    zero_rows = jnp.zeros((nlev, 2, nprobe, 128), F32)
    zero_pack = jnp.zeros((nlev, half, 128), F32)

    @pl.when(row == 0)
    def _():
        scaled[:, 0:2] = zero_rows
        from_low[...] = zero_rows

    @pl.when(row == nrd - 1)
    def _():
        scaled[:, nrow + 2 : nrow + 4] = zero_rows
        from_high[...] = zero_rows

    @pl.when(col == 0)
    def _():
        pack_l[...] = zero_pack
        wrap_l[...] = zero_pack

    @pl.when(col == ncd - 1)
    def _():
        pack_r[...] = zero_pack
        wrap_r[...] = zero_pack

    loads[4].wait()
    pl.semaphore_wait(barrier, (nrd - 1) + (INNER - 1) + (outer - 1) + 2)

    def put(acc, r, value):
        slot = lax.div(lane16, 4)
        acc = jnp.where(slot == r, roll(value[:half], 4 * r + 2), acc)
        return jnp.where(slot == r + 16, roll(value[half:], 4 * r + 66), acc)

    wide_lane = lanes((nprobe, 128))
    at_edge = jnp.logical_or(wide_lane < 2, wide_lane >= 126)

    def take(corr, r):
        both = jnp.concatenate([roll(corr, -(4 * r + 2)), roll(corr, -(4 * r + 66))], axis=0)
        return jnp.where(at_edge, both, 0.0)

    def scale_level(l, carry):
        for p in range(nprobe):
            turn[p * nrow : (p + 1) * nrow, :] = probes[p, l].astype(F32)
        acc = jnp.zeros((half, 128), F32)
        for r in range(nrow):
            om = turn[pl.ds(r, nprobe, stride=nrow), :]
            omega[l, r] = om.astype(BF16)
            v = om * wide(co[SPR, l, r], nprobe)
            scaled[l, r + 2] = v
            acc = put(acc, r, v)
        pack[l] = acc
        send(0, l)
        return carry

    lax.fori_loop(0, nlev, scale_level, 0)

    def tangent_level(l, carry):
        receive(0, l)
        above = jnp.minimum(l + 1, nlev - 1)
        below = jnp.maximum(l - 1, 0)
        e1 = edge[0, pl.ds(l, 1), :]
        ea = edge[1, pl.ds(l, 1), :]
        diff = jnp.where(quad < 2, pack_l[l], pack_r[l]) - pack[l]
        near = jnp.where(quad == 1, roll(diff, -1), roll(diff, 1))
        far = jnp.where(quad < 2, -roll(diff, -2), roll(diff, 2))
        corr = e1 * near + ea * far
        acc = jnp.zeros((half, 128), F32)
        rims_of = {}
        for r in range(nrow):
            c = [wide(co[f, l, r], nprobe) for f in range(NF)]
            v = scaled[l, r + 2]
            t = c[CEN] * v + 0.2 * (scaled[above, r + 2] + scaled[below, r + 2])
            t = t + c[XP] * scaled[l, r + 3] + c[XM] * scaled[l, r + 1]
            t = t + c[XA] * (scaled[l, r] - scaled[l, r + 4])
            t = t + c[YP] * roll(v, -1) + c[YM] * roll(v, 1) + c[YA] * (roll(v, 2) - roll(v, -2))
            t = t + take(corr, r)
            tang[l, r] = t
            acc = put(acc, r, t)
            if r == 0:
                to_low[l, 0] = c[XA] * t
                rims_of[r] = c[XM] * t
            if r == 1:
                to_low[l, 1] = rims_of[0] + c[XA] * t
            if r == nrow - 2:
                rims_of[r] = c[XA] * t
            if r == nrow - 1:
                to_high[l, 0] = c[XP] * t - rims_of[nrow - 2]
                to_high[l, 1] = -(c[XA] * t)
        u = ea * acc
        w = e1 * acc
        wrap[l] = jnp.where(quad < 2, roll(u, -2), -roll(u, 2)) + jnp.where(
            quad == 1, roll(w, -1), jnp.where(quad == 2, roll(w, 1), 0.0)
        )
        send(1, l)
        return carry

    lax.fori_loop(0, nlev, tangent_level, 0)

    def adjoint_level(l, gram):
        receive(1, l)
        above = jnp.minimum(l + 1, nlev - 1)
        below = jnp.maximum(l - 1, 0)
        corr = jnp.where(quad < 2, wrap_r[l], wrap_l[l]) - wrap[l]
        for r0 in range(0, nrow, 2):
            left, right = [], []
            for r in (r0, r0 + 1):
                c = [wide(co[f, l, r], nprobe) for f in (CEN, YP, YM, YA, SPR)]
                w = tang[l, r]
                b = c[0] * w + 0.2 * (tang[above, r] + tang[below, r])
                if r + 1 < nrow:
                    b = b + wide(co[XM, l, r + 1], nprobe) * tang[l, r + 1]
                if r >= 1:
                    b = b + wide(co[XP, l, r - 1], nprobe) * tang[l, r - 1]
                if r + 2 < nrow:
                    b = b + wide(co[XA, l, r + 2], nprobe) * tang[l, r + 2]
                if r >= 2:
                    b = b - wide(co[XA, l, r - 2], nprobe) * tang[l, r - 2]
                ya = c[3] * w
                b = b + roll(c[2] * w, -1) + roll(c[1] * w, 1) + (roll(ya, -2) - roll(ya, 2))
                if r < 2:
                    b = b + from_low[l, r]
                if r >= nrow - 2:
                    b = b + from_high[l, r - (nrow - 2)]
                b = b + take(corr, r)
                om = omega[l, r]
                sk = om.astype(F32) + c[4] * b
                hi = sk.astype(BF16)
                lo = (sk - hi.astype(F32)).astype(BF16)
                z = jnp.concatenate([hi, lo], axis=0)
                zbuf[l, r] = z
                right.append(z)
                left.append(jnp.concatenate([z, om], axis=0))
            gram = gram + lax.dot_general(
                jnp.concatenate(left, axis=1),
                jnp.concatenate(right, axis=1),
                (((1,), (1,)), ((), ())),
                preferred_element_type=F32,
            )
        pltpu.make_async_copy(zbuf.at[l], z_hbm.at[l], out_sem.at[l]).start()
        return gram

    gram = lax.fori_loop(0, nlev, adjoint_level, jnp.zeros((3 * nprobe, 2 * nprobe), F32))

    gbuf[...] = jnp.zeros(gbuf.shape, F32)
    gbuf[:, 0 : 2 * nprobe] = gram
    full = gbuf[...]
    full = full + roll(full, -nprobe)
    own = full[:nprobe] + full[nprobe : 2 * nprobe]
    both = jnp.where(wide_lane < nprobe, own, roll(full[2 * nprobe :], nprobe))
    part = jnp.where(lane16 < 64, both[:half], roll(both[half:], 64))

    stages = (
        (red0, nrd, row, lambda t: (t, col)),
        (red1, INNER, xi, lambda t: (row, zi * INNER + t)),
        (red2, outer, zi, lambda t: (row, t * INNER + xi)),
    )
    copies = []
    for s, (buf, count, me, at) in enumerate(stages):
        buf[me] = part
        stage = []
        for o in range(1, count):
            stage.append(
                pltpu.make_async_remote_copy(
                    src_ref=buf.at[me],
                    dst_ref=buf.at[me],
                    send_sem=red_send.at[s, o],
                    recv_sem=red_recv.at[s, o],
                    device_id=at(lax.rem(me + o, count)),
                    device_id_type=MESH,
                )
            )
            stage[-1].start()
        for copy in stage:
            copy.wait_recv()
        part = buf[0]
        for o in range(1, count):
            part = part + buf[o]
        copies += stage
    g_ref[...] = part

    for copy in copies:
        copy.wait_send()

    def finish(l, carry):
        sent(0, l)
        sent(1, l)
        pltpu.make_async_copy(zbuf.at[l], z_hbm.at[l], out_sem.at[l]).wait()
        return carry

    lax.fori_loop(0, nlev, finish, 0)


def basis_kernel(nprobe, nlev, nrow, scale, g_ref, z_hbm, basis_hbm, factor_ref, zbuf, obuf, in_sem, out_sem):
    def load(l):
        return pltpu.make_async_copy(z_hbm.at[l], zbuf.at[l], in_sem.at[l])

    def store(l):
        return pltpu.make_async_copy(obuf.at[l], basis_hbm.at[:, l], out_sem.at[l])

    for l in range(nlev):
        load(l).start()
    half = nprobe // 2
    g = g_ref[...]
    both = jnp.concatenate([g, roll(g, 64)], axis=0)
    flip = both.T
    lane = lanes((nprobe, 128))
    sub = lax.broadcasted_iota(jnp.int32, (nprobe, 128), 0)
    pad = jnp.zeros((nprobe, 128 - nprobe), F32)
    flip_g = jnp.concatenate([flip[:nprobe], pad], axis=1)
    flip_c = jnp.concatenate([flip[nprobe : 2 * nprobe], pad], axis=1)
    sym_g = 0.5 * (both + flip_g)
    sym_c = 0.5 * (roll(both, -nprobe) + flip_c)
    m = jnp.where(lane < nprobe, sym_g, jnp.where(jnp.logical_and(lane >= 64, lane < 64 + nprobe), roll(sym_c, 64), 0.0))
    m = jnp.where(jnp.logical_or(lane == sub + nprobe, lane == sub + 64 + nprobe), 1.0, m)
    first = lane < 64
    piv = jnp.ones((nprobe, 128), F32)
    for k in range(nprobe):
        col = jnp.where(first, m[:, k : k + 1], m[:, 64 + k : 65 + k])
        p = col[k : k + 1]
        line = m[k : k + 1] / p
        piv = jnp.where(sub == k, p, piv)
        m = jnp.where(sub > k, m - col * line, m)
    m = m * (1.0 / jnp.sqrt(piv))
    upper = jnp.where(jnp.logical_and(lane >= sub, lane < nprobe), m, 0.0)
    inv_g = jnp.where(lane <= sub, roll(m, -nprobe), 0.0)
    inv_c = jnp.where(lane <= sub, roll(m, -(64 + nprobe)), 0.0)
    factor = lax.dot_general(
        upper, inv_c, (((1,), (1,)), ((), ())), precision=lax.Precision.HIGHEST, preferred_element_type=F32
    )
    factor_ref[...] = factor
    a = inv_g * scale
    a_hi = a.astype(BF16)
    a_lo = (a - a_hi.astype(F32)).astype(BF16)
    twice = jnp.where(lane < nprobe, a_hi.astype(F32), roll(a_hi.astype(F32), nprobe))
    twice_lo = jnp.where(lane < nprobe, a_lo.astype(F32), roll(a_lo.astype(F32), nprobe))
    lhs = jnp.concatenate([twice, twice_lo], axis=0).astype(BF16)[:, : 2 * nprobe]

    def level(l, carry):
        load(l).wait()
        for r in range(nrow):
            out = lax.dot_general(
                lhs, zbuf[l, r], (((1,), (0,)), ((), ())), preferred_element_type=F32
            )
            put_row(obuf.at[l], r, out[:nprobe] + out[nprobe:])
        store(l).start()
        return carry

    lax.fori_loop(0, nlev, level, 0)

    def finish(l, carry):
        store(l).wait()
        return carry

    lax.fori_loop(0, nlev, finish, 0)


def shards(probes, spread, adv_x, adv_y, diffusivity):
    nprobe, nlev, nrow, ncol = probes.shape
    nrd = lax.axis_size("row")
    ncd = lax.axis_size("col")
    half = nprobe // 2
    any_spec = pl.BlockSpec(memory_space=pl.ANY)
    vmem_spec = pl.BlockSpec(memory_space=pltpu.VMEM)
    rows2 = pltpu.VMEM((nlev, 2, nprobe, ncol), F32)
    strip = pltpu.VMEM((nlev, half, ncol), F32)
    most = max(nrd, INNER, ncd // INNER)
    z, g = pl.pallas_call(
        functools.partial(halo_kernel, (nprobe, nlev, nrow, nrd, ncd)),
        out_shape=(
            jax.ShapeDtypeStruct((nlev, nrow, 2 * nprobe, ncol), BF16),
            jax.ShapeDtypeStruct((half, ncol), F32),
        ),
        in_specs=[any_spec] * 5,
        out_specs=(any_spec, vmem_spec),
        scratch_shapes=[
            pltpu.VMEM((nprobe, nlev, nrow, ncol), BF16),
            pltpu.VMEM((4, nlev, nrow, ncol), F32),
            pltpu.VMEM((nprobe * nrow, ncol), F32),
            pltpu.VMEM((nlev, nrow, nprobe, ncol), BF16),
            pltpu.VMEM((nlev, nrow + 4, nprobe, ncol), F32),
            pltpu.VMEM((nlev, nrow, nprobe, ncol), F32),
            pltpu.VMEM((NF, nlev, nrow, 8, ncol), F32),
            pltpu.VMEM((2, nlev, ncol), F32),
            strip, strip, strip, strip, strip, strip,
            rows2, rows2, rows2, rows2,
            pltpu.VMEM((nlev, nrow, 2 * nprobe, ncol), BF16),
            pltpu.VMEM((3 * nprobe, ncol), F32),
            pltpu.VMEM((nrd, half, ncol), F32),
            pltpu.VMEM((INNER, half, ncol), F32),
            pltpu.VMEM((ncd // INNER, half, ncol), F32),
            pltpu.SemaphoreType.DMA((5,)),
            pltpu.SemaphoreType.DMA((nlev,)),
            pltpu.SemaphoreType.DMA((2, 4, nlev)),
            pltpu.SemaphoreType.DMA((2, 4, nlev)),
            pltpu.SemaphoreType.DMA((3, most)),
            pltpu.SemaphoreType.DMA((3, most)),
        ],
        compiler_params=pltpu.CompilerParams(
            collective_id=0, has_side_effects=True, vmem_limit_bytes=40 * 1024 * 1024
        ),
        name="sketch_and_sums",
    )(probes, spread, adv_x, adv_y, diffusivity)
    scale = float(nlev * nrow * ncol * nrd * ncd) ** 0.5
    basis, factor = pl.pallas_call(
        functools.partial(basis_kernel, nprobe, nlev, nrow, scale),
        out_shape=(
            jax.ShapeDtypeStruct((nprobe, nlev, nrow, ncol), F32),
            jax.ShapeDtypeStruct((nprobe, nprobe), F32),
        ),
        in_specs=[vmem_spec, any_spec],
        out_specs=(any_spec, vmem_spec),
        scratch_shapes=[
            pltpu.VMEM((nlev, nrow, 2 * nprobe, ncol), BF16),
            pltpu.VMEM((nlev, nprobe, nrow, ncol), F32),
            pltpu.SemaphoreType.DMA((nlev,)),
            pltpu.SemaphoreType.DMA((nlev,)),
        ],
        compiler_params=pltpu.CompilerParams(vmem_limit_bytes=24 * 1024 * 1024),
        name="factors_and_basis",
    )(g, z)
    return basis, factor


def solution(mesh):
    return jax.shard_map(
        shards,
        mesh=mesh,
        in_specs=(
            P(None, None, "row", "col"),
            P(None, "row", "col"),
            P(None, "row", "col"),
            P(None, "row", "col"),
            P(None, "row", "col"),
        ),
        out_specs=(P(None, None, "row", "col"), P()),
        check_vma=False,
    )
```

```python
import functools

import jax
import jax.numpy as jnp
from jax import lax
from jax.experimental import pallas as pl
from jax.experimental.pallas import tpu as pltpu
from jax.sharding import PartitionSpec as P

MESH = pl.DeviceIdType.MESH
F32 = jnp.float32
BF16 = jnp.bfloat16
INNER = 4
NF = 8
SPR, CEN, XP, XM, XA, YP, YM, YA = range(NF)
LOW, HIGH, LEFT, RIGHT = range(4)


def lanes(shape):
    return lax.broadcasted_iota(jnp.int32, shape, 1)


def roll(x, shift):
    return pltpu.roll(x, shift % 128, 1)


def put_row(ref, r, value):
    n, rows, width = ref.shape
    ref.reshape(n * rows, width)[pl.ds(r, n, stride=rows), :] = value


def wide(coef, nprobe):
    return jnp.broadcast_to(coef[None], (nprobe // 8, 8, 128)).reshape(nprobe, 128)


def halo_kernel(
    dims,
    probes_hbm, spread_hbm, advx_hbm, advy_hbm, diff_hbm,
    z_hbm, g_ref,
    probes, coefs, turn, omega, scaled, tang, co, edge,
    pack, pack_l, pack_r, wrap, wrap_l, wrap_r,
    to_low, to_high, from_low, from_high,
    back, strip, zbuf, gbuf, red_a, red_b, red_c, total,
    in_sem, out_sem, send_sem, recv_sem, red_send, red_recv,
):
    nprobe, nlev, nrow, nrd, ncd = dims
    outer = ncd // INNER
    row = lax.axis_index("row")
    col = lax.axis_index("col")
    zi = col // INNER
    xi = lax.rem(col, INNER)
    half = nprobe // 2

    loads = []
    for i, src in enumerate((spread_hbm, advx_hbm, advy_hbm, diff_hbm)):
        loads.append(pltpu.make_async_copy(src, coefs.at[i], in_sem.at[i]))
    loads.append(pltpu.make_async_copy(probes_hbm, probes, in_sem.at[4]))
    for load in loads:
        load.start()

    core = lax.rem(row, 2)
    chip = (row // 2) * INNER + xi
    plane = (nrd // 2) * INNER

    def in_plane(t):
        return ((t // INNER) * 2 + core, zi * INNER + lax.rem(t, INNER))

    def in_line(t):
        return (row, t * INNER + xi)

    other = (row + 1 - 2 * core, col)
    barrier = pltpu.get_barrier_semaphore()
    greet = [other]
    greet += [(lax.rem(row + o, nrd), col) for o in (1, nrd - 1)]
    greet += [(row, lax.rem(col + o, ncd)) for o in (1, ncd - 1)]
    greet += [in_plane(lax.rem(chip + o, plane)) for o in range(1, plane)]
    greet += [in_line(lax.rem(zi + o, outer)) for o in range(1, outer)]
    for device in greet:
        pl.semaphore_signal(barrier, inc=1, device_id=device, device_id_type=MESH)
    signals = len(greet)

    for load in loads[:4]:
        load.wait()

    def spread_coefs(l, carry):
        ax = coefs[1, l] * (1.0 / 12.0)
        ay = coefs[2, l] * (1.0 / 12.0)
        d = coefs[3, l]
        fields = (coefs[0, l], 0.6 - 4.0 * d, d + 8.0 * ax, d - 8.0 * ax, ax, d + 8.0 * ay, d - 8.0 * ay, ay)
        for f in range(NF):
            for r in range(nrow):
                co[f, l, r] = jnp.broadcast_to(fields[f][r : r + 1], (8, 128))
        return carry

    lax.fori_loop(0, nlev, spread_coefs, 0)

    lane16 = lanes((half, 128))
    quad = lax.rem(lane16, 4)
    lane_l = lanes((nlev, 128))
    quad_l = lax.rem(lane_l, 4)

    def packed(field):
        acc = jnp.zeros((nlev, 128), F32)
        for r in range(nrow):
            acc = jnp.where(lax.div(lane_l, 4) == r, roll(coefs[field, :, r, :], 4 * r + 2), acc)
        return jnp.where(lane_l < 64, acc, roll(acc, 64))

    pa = packed(2) * (1.0 / 12.0)
    pd = packed(3)
    edge[0] = jnp.where(quad_l == 1, pd + 8.0 * pa, jnp.where(quad_l == 2, pd - 8.0 * pa, 0.0))
    edge[1] = pa

    has = {LOW: row > 0, HIGH: row < nrd - 1, LEFT: col > 0, RIGHT: col < ncd - 1}
    target = {LOW: (row - 1, col), HIGH: (row + 1, col), LEFT: (row, col - 1), RIGHT: (row, col + 1)}
    rims = (
        {
            LOW: (lambda l: scaled.at[l, 2:4], lambda l: scaled.at[l, nrow + 2 : nrow + 4]),
            HIGH: (lambda l: scaled.at[l, nrow : nrow + 2], lambda l: scaled.at[l, 0:2]),
            LEFT: (lambda l: pack.at[l], lambda l: pack_r.at[l]),
            RIGHT: (lambda l: pack.at[l], lambda l: pack_l.at[l]),
        },
        {
            LOW: (lambda l: to_low.at[l], lambda l: from_high.at[l]),
            HIGH: (lambda l: to_high.at[l], lambda l: from_low.at[l]),
            LEFT: (lambda l: wrap.at[l], lambda l: wrap_r.at[l]),
            RIGHT: (lambda l: wrap.at[l], lambda l: wrap_l.at[l]),
        },
    )
    opposite = {LOW: HIGH, HIGH: LOW, LEFT: RIGHT, RIGHT: LEFT}

    def rim(phase, side, l):
        src, dst = rims[phase][side]
        return pltpu.make_async_remote_copy(
            src_ref=src(l),
            dst_ref=dst(l),
            send_sem=send_sem.at[phase, side, l],
            recv_sem=recv_sem.at[phase, side, l],
            device_id=target[side],
            device_id_type=MESH,
        )

    def send(phase, l):
        for side in (LOW, HIGH, LEFT, RIGHT):
            @pl.when(has[side])
            def _():
                rim(phase, side, l).start()

    def receive(phase, l):
        for side in (LEFT, RIGHT, LOW, HIGH):
            @pl.when(has[side])
            def _():
                rim(phase, opposite[side], l).wait_recv()

    def sent(phase, l):
        for side in (LOW, HIGH, LEFT, RIGHT):
            @pl.when(has[side])
            def _():
                rim(phase, side, l).wait_send()

    zero_rows = jnp.zeros((nlev, 2, nprobe, 128), F32)
    zero_pack = jnp.zeros((nlev, half, 128), F32)

    @pl.when(row == 0)
    def _():
        scaled[:, 0:2] = zero_rows
        from_low[...] = zero_rows

    @pl.when(row == nrd - 1)
    def _():
        scaled[:, nrow + 2 : nrow + 4] = zero_rows
        from_high[...] = zero_rows

    @pl.when(col == 0)
    def _():
        pack_l[...] = zero_pack
        wrap_l[...] = zero_pack

    @pl.when(col == ncd - 1)
    def _():
        pack_r[...] = zero_pack
        wrap_r[...] = zero_pack

    loads[4].wait()

    def put(acc, r, value):
        slot = lax.div(lane16, 4)
        acc = jnp.where(slot == r, roll(value[:half], 4 * r + 2), acc)
        return jnp.where(slot == r + 16, roll(value[half:], 4 * r + 66), acc)

    wide_lane = lanes((nprobe, 128))
    at_edge = jnp.logical_or(wide_lane < 2, wide_lane >= 126)

    def take(corr, r):
        both = jnp.concatenate([roll(corr, -(4 * r + 2)), roll(corr, -(4 * r + 66))], axis=0)
        return jnp.where(at_edge, both, 0.0)

    def scale_level(l, carry):
        for p in range(nprobe):
            turn[p * nrow : (p + 1) * nrow, :] = probes[p, l].astype(F32)
        acc = jnp.zeros((half, 128), F32)
        for r in range(nrow):
            om = turn[pl.ds(r, nprobe, stride=nrow), :]
            omega[l, r] = om.astype(BF16)
            v = om * wide(co[SPR, l, r], nprobe)
            scaled[l, r + 2] = v
            acc = put(acc, r, v)
        pack[l] = acc
        return carry

    lax.fori_loop(0, nlev, scale_level, 0)

    pl.semaphore_wait(barrier, signals)

    def send_level(l, carry):
        send(0, l)
        return carry

    lax.fori_loop(0, nlev, send_level, 0)

    def tangent_row(l, r):
        above = jnp.minimum(l + 1, nlev - 1)
        below = jnp.maximum(l - 1, 0)
        c = [wide(co[f, l, r], nprobe) for f in range(NF)]
        v = scaled[l, r + 2]
        t = c[CEN] * v + 0.2 * (scaled[above, r + 2] + scaled[below, r + 2])
        t = t + c[XP] * scaled[l, r + 3] + c[XM] * scaled[l, r + 1]
        t = t + c[XA] * (scaled[l, r] - scaled[l, r + 4])
        return t + c[YP] * roll(v, -1) + c[YM] * roll(v, 1) + c[YA] * (roll(v, 2) - roll(v, -2))

    def tangent_inner(l, carry):
        for r in range(2, nrow - 2):
            tang[l, r] = tangent_row(l, r)

        def gather(h, carry):
            lane8 = lax.div(lanes((8, 128)), 4)
            acc = jnp.zeros((8, 128), F32)
            for r in range(2, nrow - 2):
                a = tang[l, r, pl.ds(h * 8, 8), :]
                b = tang[l, r, pl.ds(h * 8 + half, 8), :]
                acc = jnp.where(lane8 == r, roll(a, 4 * r + 2), acc)
                acc = jnp.where(lane8 == r + 16, roll(b, 4 * r + 66), acc)
            strip[l, pl.ds(h * 8, 8), :] = acc
            return carry

        lax.fori_loop(0, half // 8, gather, 0)
        return carry

    lax.fori_loop(0, nlev, tangent_inner, 0)

    def tangent_outer(l, carry):
        receive(0, l)
        e1 = edge[0, pl.ds(l, 1), :]
        ea = edge[1, pl.ds(l, 1), :]
        diff = jnp.where(quad < 2, pack_l[l], pack_r[l]) - pack[l]
        near = jnp.where(quad == 1, roll(diff, -1), roll(diff, 1))
        far = jnp.where(quad < 2, -roll(diff, -2), roll(diff, 2))
        corr = e1 * near + ea * far
        acc = strip[l] + corr
        ends = {}
        for r in (0, 1, nrow - 2, nrow - 1):
            t = tangent_row(l, r) + take(corr, r)
            tang[l, r] = t
            ends[r] = t
            acc = put(acc, r, t)
        last = nrow - 1

        def coef(f, r):
            return wide(co[f, l, r], nprobe)

        to_low[l, 0] = coef(XA, 0) * ends[0]
        to_low[l, 1] = coef(XM, 0) * ends[0] + coef(XA, 1) * ends[1]
        to_high[l, 0] = coef(XP, last) * ends[last] - coef(XA, last - 1) * ends[last - 1]
        to_high[l, 1] = -(coef(XA, last) * ends[last])
        u = ea * acc
        w = e1 * acc
        wrap[l] = jnp.where(quad < 2, roll(u, -2), -roll(u, 2)) + jnp.where(
            quad == 1, roll(w, -1), jnp.where(quad == 2, roll(w, 1), 0.0)
        )
        send(1, l)
        for r in range(2, nrow - 2):
            tang[l, r] = tang[l, r] + take(corr, r)
        return carry

    lax.fori_loop(0, nlev, tangent_outer, 0)

    def adjoint_own(l, carry):
        above = jnp.minimum(l + 1, nlev - 1)
        below = jnp.maximum(l - 1, 0)
        for r in range(nrow):
            c = [wide(co[f, l, r], nprobe) for f in (CEN, YP, YM, YA)]
            w = tang[l, r]
            b = c[0] * w + 0.2 * (tang[above, r] + tang[below, r])
            if r + 1 < nrow:
                b = b + wide(co[XM, l, r + 1], nprobe) * tang[l, r + 1]
            if r >= 1:
                b = b + wide(co[XP, l, r - 1], nprobe) * tang[l, r - 1]
            if r + 2 < nrow:
                b = b + wide(co[XA, l, r + 2], nprobe) * tang[l, r + 2]
            if r >= 2:
                b = b - wide(co[XA, l, r - 2], nprobe) * tang[l, r - 2]
            ya = c[3] * w
            back[l, r] = b + roll(c[2] * w, -1) + roll(c[1] * w, 1) + (roll(ya, -2) - roll(ya, 2))
        return carry

    lax.fori_loop(0, nlev, adjoint_own, 0)

    def sketch_level(l, gram):
        receive(1, l)
        corr = jnp.where(quad < 2, wrap_r[l], wrap_l[l]) - wrap[l]
        for r0 in range(0, nrow, 2):
            left, right = [], []
            for r in (r0, r0 + 1):
                b = back[l, r] + take(corr, r)
                if r < 2:
                    b = b + from_low[l, r]
                if r >= nrow - 2:
                    b = b + from_high[l, r - (nrow - 2)]
                om = omega[l, r]
                sk = om.astype(F32) + wide(co[SPR, l, r], nprobe) * b
                hi = sk.astype(BF16)
                lo = (sk - hi.astype(F32)).astype(BF16)
                z = jnp.concatenate([hi, lo], axis=0)
                zbuf[l, r] = z
                right.append(z)
                left.append(jnp.concatenate([z, om], axis=0))
            gram = gram + lax.dot_general(
                jnp.concatenate(left, axis=1),
                jnp.concatenate(right, axis=1),
                (((1,), (1,)), ((), ())),
                preferred_element_type=F32,
            )
        pltpu.make_async_copy(zbuf.at[l], z_hbm.at[l], out_sem.at[l]).start()
        return gram

    gram = lax.fori_loop(0, nlev, sketch_level, jnp.zeros((3 * nprobe, 2 * nprobe), F32))

    gbuf[...] = jnp.zeros(gbuf.shape, F32)
    gbuf[:, 0 : 2 * nprobe] = gram
    full = gbuf[...]
    full = full + roll(full, -nprobe)
    own = full[:nprobe] + full[nprobe : 2 * nprobe]
    both = jnp.where(wide_lane < nprobe, own, roll(full[2 * nprobe :], nprobe))
    part = jnp.where(lane16 < 64, both[:half], roll(both[half:], 64))

    pair_part = red_a
    pair_part[0] = part
    swap = pltpu.make_async_remote_copy(
        src_ref=pair_part.at[0], dst_ref=pair_part.at[1], send_sem=red_send.at[0, 0], recv_sem=red_recv.at[0, 0],
        device_id=other, device_id_type=MESH,
    )
    swap.start()
    swap.wait_recv()
    quarter = half // 2
    mine = pl.ds(pl.multiple_of(core * quarter, quarter), quarter)
    part = pair_part[0, mine] + pair_part[1, mine]
    copies = [swap]
    for s, (buf, count, me, at) in enumerate(((red_b, plane, chip, in_plane), (red_c, outer, zi, in_line))):
        buf[me] = part
        stage = []
        for o in range(1, count):
            stage.append(
                pltpu.make_async_remote_copy(
                    src_ref=buf.at[me],
                    dst_ref=buf.at[me],
                    send_sem=red_send.at[s + 1, o],
                    recv_sem=red_recv.at[s + 1, o],
                    device_id=at(lax.rem(me + o, count)),
                    device_id_type=MESH,
                )
            )
            stage[-1].start()
        for copy in stage:
            copy.wait_recv()
        terms = [buf[o] for o in range(count)]
        while len(terms) > 1:
            terms = [sum(terms[i : i + 2][1:], terms[i]) for i in range(0, len(terms), 2)]
        part = terms[0]
        copies += stage
    total[mine] = part
    join = pltpu.make_async_remote_copy(
        src_ref=total.at[mine], dst_ref=total.at[mine], send_sem=red_send.at[0, 1], recv_sem=red_recv.at[0, 1],
        device_id=other, device_id_type=MESH,
    )
    join.start()
    join.wait_recv()
    copies.append(join)
    g_ref[...] = total[...]

    for copy in copies:
        copy.wait_send()

    def finish(l, carry):
        sent(0, l)
        sent(1, l)
        pltpu.make_async_copy(zbuf.at[l], z_hbm.at[l], out_sem.at[l]).wait()
        return carry

    lax.fori_loop(0, nlev, finish, 0)


def basis_kernel(nprobe, nlev, nrow, scale, g_ref, z_hbm, basis_hbm, factor_ref, zbuf, obuf, in_sem, out_sem):
    def load(l):
        return pltpu.make_async_copy(z_hbm.at[l], zbuf.at[l], in_sem.at[l])

    def store(l):
        return pltpu.make_async_copy(obuf.at[l], basis_hbm.at[:, l], out_sem.at[l])

    for l in range(nlev):
        load(l).start()
    half = nprobe // 2
    g = g_ref[...]
    both = jnp.concatenate([g, roll(g, 64)], axis=0)
    flip = both.T
    lane = lanes((nprobe, 128))
    sub = lax.broadcasted_iota(jnp.int32, (nprobe, 128), 0)
    pad = jnp.zeros((nprobe, 128 - nprobe), F32)
    flip_g = jnp.concatenate([flip[:nprobe], pad], axis=1)
    flip_c = jnp.concatenate([flip[nprobe : 2 * nprobe], pad], axis=1)
    sym_g = 0.5 * (both + flip_g)
    sym_c = 0.5 * (roll(both, -nprobe) + flip_c)
    m = jnp.where(lane < nprobe, sym_g, jnp.where(jnp.logical_and(lane >= 64, lane < 64 + nprobe), roll(sym_c, 64), 0.0))
    m = jnp.where(jnp.logical_or(lane == sub + nprobe, lane == sub + 64 + nprobe), 1.0, m)
    first = lane < 64
    piv = jnp.ones((nprobe, 128), F32)
    for k in range(nprobe):
        col = jnp.where(first, m[:, k : k + 1], m[:, 64 + k : 65 + k])
        p = col[k : k + 1]
        line = m[k : k + 1] / p
        piv = jnp.where(sub == k, p, piv)
        m = jnp.where(sub > k, m - col * line, m)
    m = m * (1.0 / jnp.sqrt(piv))
    upper = jnp.where(jnp.logical_and(lane >= sub, lane < nprobe), m, 0.0)
    inv_g = jnp.where(lane <= sub, roll(m, -nprobe), 0.0)
    inv_c = jnp.where(lane <= sub, roll(m, -(64 + nprobe)), 0.0)
    factor = lax.dot_general(
        upper, inv_c, (((1,), (1,)), ((), ())), precision=lax.Precision.HIGHEST, preferred_element_type=F32
    )
    factor_ref[...] = factor
    a = inv_g * scale
    a_hi = a.astype(BF16)
    a_lo = (a - a_hi.astype(F32)).astype(BF16)
    twice = jnp.where(lane < nprobe, a_hi.astype(F32), roll(a_hi.astype(F32), nprobe))
    twice_lo = jnp.where(lane < nprobe, a_lo.astype(F32), roll(a_lo.astype(F32), nprobe))
    lhs = jnp.concatenate([twice, twice_lo], axis=0).astype(BF16)[:, : 2 * nprobe]

    def level(l, carry):
        load(l).wait()
        for r in range(nrow):
            out = lax.dot_general(
                lhs, zbuf[l, r], (((1,), (0,)), ((), ())), preferred_element_type=F32
            )
            put_row(obuf.at[l], r, out[:nprobe] + out[nprobe:])
        store(l).start()
        return carry

    lax.fori_loop(0, nlev, level, 0)

    def finish(l, carry):
        store(l).wait()
        return carry

    lax.fori_loop(0, nlev, finish, 0)


def shards(probes, spread, adv_x, adv_y, diffusivity):
    nprobe, nlev, nrow, ncol = probes.shape
    nrd = lax.axis_size("row")
    ncd = lax.axis_size("col")
    half = nprobe // 2
    inputs = [pltpu.with_memory_space_constraint(x, pltpu.HBM) for x in (probes, spread, adv_x, adv_y, diffusivity)]
    any_spec = pl.BlockSpec(memory_space=pltpu.HBM)
    vmem_spec = pl.BlockSpec(memory_space=pltpu.VMEM)
    rows2 = pltpu.VMEM((nlev, 2, nprobe, ncol), F32)
    strip = pltpu.VMEM((nlev, half, ncol), F32)
    plane = (nrd // 2) * INNER
    most = max(2, plane, ncd // INNER)
    z, g = pl.pallas_call(
        functools.partial(halo_kernel, (nprobe, nlev, nrow, nrd, ncd)),
        out_shape=(
            jax.ShapeDtypeStruct((nlev, nrow, 2 * nprobe, ncol), BF16),
            jax.ShapeDtypeStruct((half, ncol), F32),
        ),
        in_specs=[any_spec] * 5,
        out_specs=(any_spec, vmem_spec),
        scratch_shapes=[
            pltpu.VMEM((nprobe, nlev, nrow, ncol), BF16),
            pltpu.VMEM((4, nlev, nrow, ncol), F32),
            pltpu.VMEM((nprobe * nrow, ncol), F32),
            pltpu.VMEM((nlev, nrow, nprobe, ncol), BF16),
            pltpu.VMEM((nlev, nrow + 4, nprobe, ncol), F32),
            pltpu.VMEM((nlev, nrow, nprobe, ncol), F32),
            pltpu.VMEM((NF, nlev, nrow, 8, ncol), F32),
            pltpu.VMEM((2, nlev, ncol), F32),
            strip, strip, strip, strip, strip, strip,
            rows2, rows2, rows2, rows2,
            pltpu.VMEM((nlev, nrow, nprobe, ncol), F32),
            strip,
            pltpu.VMEM((nlev, nrow, 2 * nprobe, ncol), BF16),
            pltpu.VMEM((3 * nprobe, ncol), F32),
            pltpu.VMEM((2, half, ncol), F32),
            pltpu.VMEM((plane, half // 2, ncol), F32),
            pltpu.VMEM((ncd // INNER, half // 2, ncol), F32),
            pltpu.VMEM((half, ncol), F32),
            pltpu.SemaphoreType.DMA((5,)),
            pltpu.SemaphoreType.DMA((nlev,)),
            pltpu.SemaphoreType.DMA((2, 4, nlev)),
            pltpu.SemaphoreType.DMA((2, 4, nlev)),
            pltpu.SemaphoreType.DMA((3, most)),
            pltpu.SemaphoreType.DMA((3, most)),
        ],
        compiler_params=pltpu.CompilerParams(
            collective_id=0, has_side_effects=True, vmem_limit_bytes=40 * 1024 * 1024
        ),
        name="sketch_and_sums",
    )(*inputs)
    scale = float(nlev * nrow * ncol * nrd * ncd) ** 0.5
    basis, factor = pl.pallas_call(
        functools.partial(basis_kernel, nprobe, nlev, nrow, scale),
        out_shape=(
            jax.ShapeDtypeStruct((nprobe, nlev, nrow, ncol), F32),
            jax.ShapeDtypeStruct((nprobe, nprobe), F32),
        ),
        in_specs=[vmem_spec, any_spec],
        out_specs=(any_spec, vmem_spec),
        scratch_shapes=[
            pltpu.VMEM((nlev, nrow, 2 * nprobe, ncol), BF16),
            pltpu.VMEM((nlev, nprobe, nrow, ncol), F32),
            pltpu.SemaphoreType.DMA((nlev,)),
            pltpu.SemaphoreType.DMA((nlev,)),
        ],
        compiler_params=pltpu.CompilerParams(vmem_limit_bytes=24 * 1024 * 1024),
        name="factors_and_basis",
    )(g, z)
    return basis, factor


def solution(mesh):
    return jax.shard_map(
        shards,
        mesh=mesh,
        in_specs=(
            P(None, None, "row", "col"),
            P(None, "row", "col"),
            P(None, "row", "col"),
            P(None, "row", "col"),
            P(None, "row", "col"),
        ),
        out_specs=(P(None, None, "row", "col"), P()),
        check_vma=False,
    )
```

```python
import functools

import jax
import jax.numpy as jnp
from jax import lax
from jax.experimental import pallas as pl
from jax.experimental.pallas import tpu as pltpu
from jax.sharding import PartitionSpec as P

MESH = pl.DeviceIdType.MESH
F32 = jnp.float32
BF16 = jnp.bfloat16
INNER = 4
WIDTH = 8
GROUP = 2
NF = 8
SPR, CEN, XP, XM, XA, YP, YM, YA = range(NF)
LOW, HIGH, LEFT, RIGHT = range(4)


def lanes(shape):
    return lax.broadcasted_iota(jnp.int32, shape, 1)


def roll(x, shift):
    return pltpu.roll(x, shift % 128, 1)


def put_row(ref, r, value):
    n, rows, width = ref.shape
    ref.reshape(n * rows, width)[pl.ds(r, n, stride=rows), :] = value


def wide(coef, nprobe):
    return jnp.broadcast_to(coef[None], (nprobe // 8, 8, 128)).reshape(nprobe, 128)


def halo_kernel(
    dims,
    probes_hbm, spread_hbm, advx_hbm, advy_hbm, diff_hbm,
    z_hbm, g_ref,
    probes, coefs, turn, omega, scaled, tang, co, edge,
    pack, pack_l, pack_r, wrap, wrap_l, wrap_r,
    to_low, to_high, from_low, from_high,
    back, strip, zbuf, gbuf, red_a, red_b, red_c, total,
    in_sem, out_sem, send_sem, recv_sem, red_send, red_recv,
):
    nprobe, nlev, nrow, nrd, ncd = dims
    outer = ncd // INNER
    row = lax.axis_index("row")
    col = lax.axis_index("col")
    zi = col // INNER
    xi = lax.rem(col, INNER)
    half = nprobe // 2

    loads = []
    for i, src in enumerate((spread_hbm, advx_hbm, advy_hbm, diff_hbm)):
        loads.append(pltpu.make_async_copy(src, coefs.at[i], in_sem.at[i]))
    loads.append(pltpu.make_async_copy(probes_hbm, probes, in_sem.at[4]))
    for load in loads:
        load.start()

    core = lax.rem(row, 2)
    chip = (row // 2) * INNER + xi
    plane = (nrd // 2) * INNER

    def in_plane(t):
        return ((t // INNER) * 2 + core, zi * INNER + lax.rem(t, INNER))

    def in_line(t):
        return (row, t * INNER + xi)

    other = (row + 1 - 2 * core, col)
    barrier = pltpu.get_barrier_semaphore()
    greet = [other]
    greet += [(lax.rem(row + o, nrd), col) for o in (1, nrd - 1)]
    greet += [(row, lax.rem(col + o, ncd)) for o in (1, ncd - 1)]
    greet += [in_plane(lax.rem(chip + o, plane)) for o in range(1, plane)]
    greet += [in_line(lax.rem(zi + o, outer)) for o in range(1, outer)]
    for device in greet:
        pl.semaphore_signal(barrier, inc=1, device_id=device, device_id_type=MESH)
    signals = len(greet)

    for load in loads[:4]:
        load.wait()

    def spread_coefs(l, carry):
        ax = coefs[1, l] * (1.0 / 12.0)
        ay = coefs[2, l] * (1.0 / 12.0)
        d = coefs[3, l]
        fields = (coefs[0, l], 0.6 - 4.0 * d, d + 8.0 * ax, d - 8.0 * ax, ax, d + 8.0 * ay, d - 8.0 * ay, ay)
        for f in range(NF):
            for r in range(nrow):
                co[f, l, r] = jnp.broadcast_to(fields[f][r : r + 1], (8, 128))
        return carry

    lax.fori_loop(0, nlev, spread_coefs, 0)

    lane16 = lanes((half, 128))
    quad = lax.rem(lane16, 4)
    lane_l = lanes((nlev, 128))
    quad_l = lax.rem(lane_l, 4)

    def packed(field):
        acc = jnp.zeros((nlev, 128), F32)
        for r in range(nrow):
            acc = jnp.where(lax.div(lane_l, 4) == r, roll(coefs[field, :, r, :], 4 * r + 2), acc)
        return jnp.where(lane_l < 64, acc, roll(acc, 64))

    pa = packed(2) * (1.0 / 12.0)
    pd = packed(3)
    edge[0] = jnp.where(quad_l == 1, pd + 8.0 * pa, jnp.where(quad_l == 2, pd - 8.0 * pa, 0.0))
    edge[1] = pa

    has = {LOW: row > 0, HIGH: row < nrd - 1, LEFT: col > 0, RIGHT: col < ncd - 1}
    target = {LOW: (row - 1, col), HIGH: (row + 1, col), LEFT: (row, col - 1), RIGHT: (row, col + 1)}
    rims = (
        {
            LOW: (lambda l: scaled.at[l, 2:4], lambda l: scaled.at[l, nrow + 2 : nrow + 4]),
            HIGH: (lambda l: scaled.at[l, nrow : nrow + 2], lambda l: scaled.at[l, 0:2]),
            LEFT: (lambda l: pack.at[l], lambda l: pack_r.at[l]),
            RIGHT: (lambda l: pack.at[l], lambda l: pack_l.at[l]),
        },
        {
            LOW: (lambda l: to_low.at[l], lambda l: from_high.at[l]),
            HIGH: (lambda l: to_high.at[l], lambda l: from_low.at[l]),
            LEFT: (lambda l: wrap.at[l], lambda l: wrap_r.at[l]),
            RIGHT: (lambda l: wrap.at[l], lambda l: wrap_l.at[l]),
        },
    )
    opposite = {LOW: HIGH, HIGH: LOW, LEFT: RIGHT, RIGHT: LEFT}

    def rim(phase, side, l):
        src, dst = rims[phase][side]
        return pltpu.make_async_remote_copy(
            src_ref=src(l),
            dst_ref=dst(l),
            send_sem=send_sem.at[phase, side, l],
            recv_sem=recv_sem.at[phase, side, l],
            device_id=target[side],
            device_id_type=MESH,
        )

    def send(phase, l):
        for side in (LOW, HIGH, LEFT, RIGHT):
            @pl.when(has[side])
            def _():
                rim(phase, side, l).start()

    def receive(phase, l):
        for side in (LEFT, RIGHT, LOW, HIGH):
            @pl.when(has[side])
            def _():
                rim(phase, opposite[side], l).wait_recv()

    def sent(phase, l):
        for side in (LOW, HIGH, LEFT, RIGHT):
            @pl.when(has[side])
            def _():
                rim(phase, side, l).wait_send()

    zero_rows = jnp.zeros((nlev, 2, nprobe, 128), F32)
    zero_pack = jnp.zeros((nlev, half, 128), F32)

    @pl.when(row == 0)
    def _():
        scaled[:, 0:2] = zero_rows
        from_low[...] = zero_rows

    @pl.when(row == nrd - 1)
    def _():
        scaled[:, nrow + 2 : nrow + 4] = zero_rows
        from_high[...] = zero_rows

    @pl.when(col == 0)
    def _():
        pack_l[...] = zero_pack
        wrap_l[...] = zero_pack

    @pl.when(col == ncd - 1)
    def _():
        pack_r[...] = zero_pack
        wrap_r[...] = zero_pack

    loads[4].wait()

    def put(acc, r, value):
        slot = lax.div(lane16, 4)
        acc = jnp.where(slot == r, roll(value[:half], 4 * r + 2), acc)
        return jnp.where(slot == r + 16, roll(value[half:], 4 * r + 66), acc)

    wide_lane = lanes((nprobe, 128))
    at_edge = jnp.logical_or(wide_lane < 2, wide_lane >= 126)

    def take(corr, r):
        both = jnp.concatenate([roll(corr, -(4 * r + 2)), roll(corr, -(4 * r + 66))], axis=0)
        return jnp.where(at_edge, both, 0.0)

    def scale_level(l, carry):
        for p in range(nprobe):
            turn[p * nrow : (p + 1) * nrow, :] = probes[p, l].astype(F32)
        acc = jnp.zeros((half, 128), F32)
        for r in range(nrow):
            om = turn[pl.ds(r, nprobe, stride=nrow), :]
            omega[l, r] = om.astype(BF16)
            v = om * wide(co[SPR, l, r], nprobe)
            scaled[l, r + 2] = v
            acc = put(acc, r, v)
        pack[l] = acc
        return carry

    lax.fori_loop(0, nlev, scale_level, 0)

    pl.semaphore_wait(barrier, signals)

    def send_level(l, carry):
        send(0, l)
        return carry

    lax.fori_loop(0, nlev, send_level, 0)

    def tangent_row(l, r):
        above = jnp.minimum(l + 1, nlev - 1)
        below = jnp.maximum(l - 1, 0)
        c = [wide(co[f, l, r], nprobe) for f in range(NF)]
        v = scaled[l, r + 2]
        t = c[CEN] * v + 0.2 * (scaled[above, r + 2] + scaled[below, r + 2])
        t = t + c[XP] * scaled[l, r + 3] + c[XM] * scaled[l, r + 1]
        t = t + c[XA] * (scaled[l, r] - scaled[l, r + 4])
        return t + c[YP] * roll(v, -1) + c[YM] * roll(v, 1) + c[YA] * (roll(v, 2) - roll(v, -2))

    def tangent_inner(l, carry):
        for r in range(2, nrow - 2):
            tang[l, r] = tangent_row(l, r)
        return carry

    def gather(l, carry):
        acc = jnp.zeros((half, 128), F32)
        for r in range(2, nrow - 2):
            acc = put(acc, r, tang[l, r])
        strip[l] = acc
        return carry

    lax.fori_loop(0, nlev, tangent_inner, 0)
    lax.fori_loop(0, nlev, gather, 0)

    def tangent_outer(l):
        e1 = edge[0, pl.ds(l, 1), :]
        ea = edge[1, pl.ds(l, 1), :]
        diff = jnp.where(quad < 2, pack_l[l], pack_r[l]) - pack[l]
        near = jnp.where(quad == 1, roll(diff, -1), roll(diff, 1))
        far = jnp.where(quad < 2, -roll(diff, -2), roll(diff, 2))
        corr = e1 * near + ea * far
        acc = strip[l] + corr
        ends = {}
        for r in (0, 1, nrow - 2, nrow - 1):
            t = tangent_row(l, r) + take(corr, r)
            tang[l, r] = t
            ends[r] = t
            acc = put(acc, r, t)
        last = nrow - 1

        def coef(f, r):
            return wide(co[f, l, r], nprobe)

        to_low[l, 0] = coef(XA, 0) * ends[0]
        to_low[l, 1] = coef(XM, 0) * ends[0] + coef(XA, 1) * ends[1]
        to_high[l, 0] = coef(XP, last) * ends[last] - coef(XA, last - 1) * ends[last - 1]
        to_high[l, 1] = -(coef(XA, last) * ends[last])
        u = ea * acc
        w = e1 * acc
        wrap[l] = jnp.where(quad < 2, roll(u, -2), -roll(u, 2)) + jnp.where(
            quad == 1, roll(w, -1), jnp.where(quad == 2, roll(w, 1), 0.0)
        )
        for r in range(2, nrow - 2):
            tang[l, r] = tang[l, r] + take(corr, r)

    def tangent_rims(g, carry):
        group = [g * GROUP + i for i in range(GROUP)]
        for l in group:
            receive(0, l)
        for l in group:
            tangent_outer(l)
        for l in group:
            send(1, l)
        return carry

    lax.fori_loop(0, nlev // GROUP, tangent_rims, 0)

    def adjoint_own(l, carry):
        above = jnp.minimum(l + 1, nlev - 1)
        below = jnp.maximum(l - 1, 0)
        for r in range(nrow):
            c = [wide(co[f, l, r], nprobe) for f in (CEN, YP, YM, YA)]
            w = tang[l, r]
            b = c[0] * w + 0.2 * (tang[above, r] + tang[below, r])
            if r + 1 < nrow:
                b = b + wide(co[XM, l, r + 1], nprobe) * tang[l, r + 1]
            if r >= 1:
                b = b + wide(co[XP, l, r - 1], nprobe) * tang[l, r - 1]
            if r + 2 < nrow:
                b = b + wide(co[XA, l, r + 2], nprobe) * tang[l, r + 2]
            if r >= 2:
                b = b - wide(co[XA, l, r - 2], nprobe) * tang[l, r - 2]
            ya = c[3] * w
            back[l, r] = b + roll(c[2] * w, -1) + roll(c[1] * w, 1) + (roll(ya, -2) - roll(ya, 2))
        return carry

    lax.fori_loop(0, nlev, adjoint_own, 0)

    def sketch_level(l):
        corr = jnp.where(quad < 2, wrap_r[l], wrap_l[l]) - wrap[l]
        left, right = [], []
        for r in range(nrow):
            b = back[l, r] + take(corr, r)
            if r < 2:
                b = b + from_low[l, r]
            if r >= nrow - 2:
                b = b + from_high[l, r - (nrow - 2)]
            om = omega[l, r]
            sk = om.astype(F32) + wide(co[SPR, l, r], nprobe) * b
            hi = sk.astype(BF16)
            lo = (sk - hi.astype(F32)).astype(BF16)
            z = jnp.concatenate([hi, lo], axis=0)
            zbuf[l, r] = z
            right.append(z)
            left.append(jnp.concatenate([hi, om], axis=0))
        return lax.dot_general(
            jnp.concatenate(left, axis=1),
            jnp.concatenate(right, axis=1),
            (((1,), (1,)), ((), ())),
            preferred_element_type=F32,
        )

    def sketch_rims(g, gram):
        group = [g * GROUP + i for i in range(GROUP)]
        for l in group:
            receive(1, l)
        for l in group:
            gram = gram + sketch_level(l)
        for l in group:
            pltpu.make_async_copy(zbuf.at[l], z_hbm.at[l], out_sem.at[l]).start()
        return gram

    gram = lax.fori_loop(0, nlev // GROUP, sketch_rims, jnp.zeros((2 * nprobe, 2 * nprobe), F32))

    gbuf[...] = jnp.zeros(gbuf.shape, F32)
    gbuf[:, 0 : 2 * nprobe] = gram
    full = gbuf[...]
    high, probe = full[:nprobe], full[nprobe:]
    own = high + 2.0 * roll(high, -nprobe)
    both = jnp.where(wide_lane < nprobe, own, roll(probe, nprobe) + probe)
    part = jnp.where(lane16 < 64, both[:half], roll(both[half:], 64))

    pair_part = red_a
    pair_part[0] = part
    swap = pltpu.make_async_remote_copy(
        src_ref=pair_part.at[0], dst_ref=pair_part.at[1], send_sem=red_send.at[0, 0], recv_sem=red_recv.at[0, 0],
        device_id=other, device_id_type=MESH,
    )
    swap.start()
    swap.wait_recv()
    quarter = half // 2
    mine = pl.ds(pl.multiple_of(core * quarter, quarter), quarter)
    part = pair_part[0, mine] + pair_part[1, mine]
    copies = [swap]
    for s, (buf, count, me, at) in enumerate(((red_b, plane, chip, in_plane), (red_c, outer, zi, in_line))):
        buf[me] = part
        stage = []
        for o in range(1, count):
            stage.append(
                pltpu.make_async_remote_copy(
                    src_ref=buf.at[me],
                    dst_ref=buf.at[me],
                    send_sem=red_send.at[s + 1, o],
                    recv_sem=red_recv.at[s + 1, o],
                    device_id=at(lax.rem(me + o, count)),
                    device_id_type=MESH,
                )
            )
            stage[-1].start()
        for copy in stage:
            copy.wait_recv()
        terms = [buf[o] for o in range(count)]
        while len(terms) > 1:
            terms = [sum(terms[i : i + 2][1:], terms[i]) for i in range(0, len(terms), 2)]
        part = terms[0]
        copies += stage
    total[mine] = part
    join = pltpu.make_async_remote_copy(
        src_ref=total.at[mine], dst_ref=total.at[mine], send_sem=red_send.at[0, 1], recv_sem=red_recv.at[0, 1],
        device_id=other, device_id_type=MESH,
    )
    join.start()
    join.wait_recv()
    copies.append(join)
    g_ref[...] = total[...]

    for copy in copies:
        copy.wait_send()

    def finish(l, carry):
        sent(0, l)
        sent(1, l)
        pltpu.make_async_copy(zbuf.at[l], z_hbm.at[l], out_sem.at[l]).wait()
        return carry

    lax.fori_loop(0, nlev, finish, 0)


def basis_kernel(nprobe, nlev, nrow, scale, g_ref, z_hbm, basis_hbm, factor_ref, zbuf, obuf, in_sem, out_sem):
    def load(l):
        return pltpu.make_async_copy(z_hbm.at[l], zbuf.at[l], in_sem.at[l])

    def store(l):
        return pltpu.make_async_copy(obuf.at[l], basis_hbm.at[:, l], out_sem.at[l])

    for l in range(nlev):
        load(l).start()
    half = nprobe // 2
    g = g_ref[...]
    both = jnp.concatenate([g, roll(g, 64)], axis=0)
    flip = both.T
    lane = lanes((nprobe, 128))
    sub = lax.broadcasted_iota(jnp.int32, (nprobe, 128), 0)
    pad = jnp.zeros((nprobe, 128 - nprobe), F32)
    flip_g = jnp.concatenate([flip[:nprobe], pad], axis=1)
    flip_c = jnp.concatenate([flip[nprobe : 2 * nprobe], pad], axis=1)
    sym_g = 0.5 * (both + flip_g)
    sym_c = 0.5 * (roll(both, -nprobe) + flip_c)
    m = jnp.where(lane < nprobe, sym_g, jnp.where(jnp.logical_and(lane >= 64, lane < 64 + nprobe), roll(sym_c, 64), 0.0))
    m = jnp.where(jnp.logical_or(lane == sub + nprobe, lane == sub + 64 + nprobe), 1.0, m)
    first = lane < 64
    piv = jnp.ones((nprobe, 128), F32)
    for k0 in range(0, nprobe, WIDTH):
        cols = [
            jnp.where(
                first,
                jnp.broadcast_to(m[:, k : k + 1], (nprobe, 128)),
                jnp.broadcast_to(m[:, 64 + k : 65 + k], (nprobe, 128)),
            )
            for k in range(k0, k0 + WIDTH)
        ]
        for j in range(WIDTH):
            k = k0 + j
            p = cols[j][k : k + 1]
            inv = 1.0 / p
            piv = jnp.where(sub == k, p, piv)
            below = jnp.where(sub > k, cols[j], 0.0)
            for i in range(j + 1, WIDTH):
                cols[i] = cols[i] - below * (cols[i][k : k + 1] * inv)
            m = m - below * (m[k : k + 1] * inv)
    m = m * (1.0 / jnp.sqrt(piv))
    upper = jnp.where(jnp.logical_and(lane >= sub, lane < nprobe), m, 0.0)
    inv_g = jnp.where(lane <= sub, roll(m, -nprobe), 0.0)
    inv_c = jnp.where(lane <= sub, roll(m, -(64 + nprobe)), 0.0)
    factor = lax.dot_general(
        upper, inv_c, (((1,), (1,)), ((), ())), precision=lax.Precision.HIGHEST, preferred_element_type=F32
    )
    factor_ref[...] = factor
    a = inv_g * scale
    a_hi = a.astype(BF16)
    a_lo = (a - a_hi.astype(F32)).astype(BF16)
    twice = jnp.where(lane < nprobe, a_hi.astype(F32), roll(a_hi.astype(F32), nprobe))
    twice_lo = jnp.where(lane < nprobe, a_lo.astype(F32), roll(a_lo.astype(F32), nprobe))
    lhs = jnp.concatenate([twice, twice_lo], axis=0).astype(BF16)[:, : 2 * nprobe]

    def level(l, carry):
        load(l).wait()
        for r in range(0, nrow, 2):
            out = lax.dot_general(
                lhs,
                jnp.concatenate([zbuf[l, r], zbuf[l, r + 1]], axis=1),
                (((1,), (0,)), ((), ())),
                preferred_element_type=F32,
            )
            out = out[:nprobe] + out[nprobe:]
            put_row(obuf.at[l], r, out[:, :128])
            put_row(obuf.at[l], r + 1, out[:, 128:])
        store(l).start()
        return carry

    lax.fori_loop(0, nlev, level, 0)

    def finish(l, carry):
        store(l).wait()
        return carry

    lax.fori_loop(0, nlev, finish, 0)


def shards(probes, spread, adv_x, adv_y, diffusivity):
    nprobe, nlev, nrow, ncol = probes.shape
    nrd = lax.axis_size("row")
    ncd = lax.axis_size("col")
    half = nprobe // 2
    inputs = [pltpu.with_memory_space_constraint(x, pltpu.HBM) for x in (probes, spread, adv_x, adv_y, diffusivity)]
    any_spec = pl.BlockSpec(memory_space=pltpu.HBM)
    vmem_spec = pl.BlockSpec(memory_space=pltpu.VMEM)
    rows2 = pltpu.VMEM((nlev, 2, nprobe, ncol), F32)
    strip = pltpu.VMEM((nlev, half, ncol), F32)
    plane = (nrd // 2) * INNER
    most = max(2, plane, ncd // INNER)
    z, g = pl.pallas_call(
        functools.partial(halo_kernel, (nprobe, nlev, nrow, nrd, ncd)),
        out_shape=(
            jax.ShapeDtypeStruct((nlev, nrow, 2 * nprobe, ncol), BF16),
            jax.ShapeDtypeStruct((half, ncol), F32),
        ),
        in_specs=[any_spec] * 5,
        out_specs=(any_spec, vmem_spec),
        scratch_shapes=[
            pltpu.VMEM((nprobe, nlev, nrow, ncol), BF16),
            pltpu.VMEM((4, nlev, nrow, ncol), F32),
            pltpu.VMEM((nprobe * nrow, ncol), F32),
            pltpu.VMEM((nlev, nrow, nprobe, ncol), BF16),
            pltpu.VMEM((nlev, nrow + 4, nprobe, ncol), F32),
            pltpu.VMEM((nlev, nrow, nprobe, ncol), F32),
            pltpu.VMEM((NF, nlev, nrow, 8, ncol), F32),
            pltpu.VMEM((2, nlev, ncol), F32),
            strip, strip, strip, strip, strip, strip,
            rows2, rows2, rows2, rows2,
            pltpu.VMEM((nlev, nrow, nprobe, ncol), F32),
            strip,
            pltpu.VMEM((nlev, nrow, 2 * nprobe, ncol), BF16),
            pltpu.VMEM((2 * nprobe, ncol), F32),
            pltpu.VMEM((2, half, ncol), F32),
            pltpu.VMEM((plane, half // 2, ncol), F32),
            pltpu.VMEM((ncd // INNER, half // 2, ncol), F32),
            pltpu.VMEM((half, ncol), F32),
            pltpu.SemaphoreType.DMA((5,)),
            pltpu.SemaphoreType.DMA((nlev,)),
            pltpu.SemaphoreType.DMA((2, 4, nlev)),
            pltpu.SemaphoreType.DMA((2, 4, nlev)),
            pltpu.SemaphoreType.DMA((3, most)),
            pltpu.SemaphoreType.DMA((3, most)),
        ],
        compiler_params=pltpu.CompilerParams(
            collective_id=0, has_side_effects=True, vmem_limit_bytes=40 * 1024 * 1024
        ),
        name="sketch_and_sums",
    )(*inputs)
    scale = float(nlev * nrow * ncol * nrd * ncd) ** 0.5
    basis, factor = pl.pallas_call(
        functools.partial(basis_kernel, nprobe, nlev, nrow, scale),
        out_shape=(
            jax.ShapeDtypeStruct((nprobe, nlev, nrow, ncol), F32),
            jax.ShapeDtypeStruct((nprobe, nprobe), F32),
        ),
        in_specs=[vmem_spec, any_spec],
        out_specs=(any_spec, vmem_spec),
        scratch_shapes=[
            pltpu.VMEM((nlev, nrow, 2 * nprobe, ncol), BF16),
            pltpu.VMEM((nlev, nprobe, nrow, ncol), F32),
            pltpu.SemaphoreType.DMA((nlev,)),
            pltpu.SemaphoreType.DMA((nlev,)),
        ],
        compiler_params=pltpu.CompilerParams(vmem_limit_bytes=24 * 1024 * 1024),
        name="factors_and_basis",
    )(g, z)
    return basis, factor


def solution(mesh):
    return jax.shard_map(
        shards,
        mesh=mesh,
        in_specs=(
            P(None, None, "row", "col"),
            P(None, "row", "col"),
            P(None, "row", "col"),
            P(None, "row", "col"),
            P(None, "row", "col"),
        ),
        out_specs=(P(None, None, "row", "col"), P()),
        check_vma=False,
    )
```

```python
import functools

import jax
import jax.numpy as jnp
from jax import lax
from jax.experimental import pallas as pl
from jax.experimental.pallas import tpu as pltpu
from jax.sharding import PartitionSpec as P

MESH = pl.DeviceIdType.MESH
F32 = jnp.float32
BF16 = jnp.bfloat16
INNER = 4
WIDTH = 8
CHUNK = 8
GROUP = 2
NF = 7
SPR, CEN, XP, XM, XA, YA, DIF = range(NF)
LOW, HIGH, LEFT, RIGHT = range(4)


def lanes(shape):
    return lax.broadcasted_iota(jnp.int32, shape, 1)


def roll(x, shift):
    return pltpu.roll(x, shift % 128, 1)


def put_row(ref, r, value):
    n, rows, width = ref.shape
    ref.reshape(n * rows, width)[pl.ds(r, n, stride=rows), :] = value


def wide(coef, nprobe):
    return jnp.broadcast_to(coef[None], (nprobe // 8, 8, 128)).reshape(nprobe, 128)


def halo_kernel(
    dims,
    probes_hbm, spread_hbm, advx_hbm, advy_hbm, diff_hbm,
    z_hbm, g_ref,
    probes, coefs, turn, omega, scaled, tang, co, edge, ring, ring_t,
    pack, pack_l, pack_r, wrap, wrap_l, wrap_r,
    to_low, to_high, from_low, from_high,
    back, strip, zbuf, gbuf, red_a, red_b, red_c, total,
    in_sem, out_sem, send_sem, recv_sem, red_send, red_recv,
):
    nprobe, nlev, nrow, nrd, ncd = dims
    outer = ncd // INNER
    row = lax.axis_index("row")
    col = lax.axis_index("col")
    zi = col // INNER
    xi = lax.rem(col, INNER)
    half = nprobe // 2

    loads = []
    for i, src in enumerate((spread_hbm, advx_hbm, advy_hbm, diff_hbm)):
        loads.append(pltpu.make_async_copy(src, coefs.at[i], in_sem.at[i]))
    loads.append(pltpu.make_async_copy(probes_hbm, probes, in_sem.at[4]))
    for load in loads:
        load.start()

    core = lax.rem(row, 2)
    chip = (row // 2) * INNER + xi
    plane = (nrd // 2) * INNER

    def in_plane(t):
        return ((t // INNER) * 2 + core, zi * INNER + lax.rem(t, INNER))

    def in_line(t):
        return (row, t * INNER + xi)

    other = (row + 1 - 2 * core, col)
    barrier = pltpu.get_barrier_semaphore()
    greet = [other]
    greet += [(lax.rem(row + o, nrd), col) for o in (1, nrd - 1)]
    greet += [(row, lax.rem(col + o, ncd)) for o in (1, ncd - 1)]
    greet += [in_plane(lax.rem(chip + o, plane)) for o in range(1, plane)]
    greet += [in_line(lax.rem(zi + o, outer)) for o in range(1, outer)]
    for device in greet:
        pl.semaphore_signal(barrier, inc=1, device_id=device, device_id_type=MESH)
    signals = len(greet)

    for load in loads[:4]:
        load.wait()

    def spread_coefs(l, carry):
        ax = coefs[1, l] * (1.0 / 12.0)
        ay = coefs[2, l] * (1.0 / 12.0)
        d = coefs[3, l]
        fields = (coefs[0, l], 0.6 - 4.0 * d, d + 8.0 * ax, d - 8.0 * ax, ax, ay, d)
        for f in range(NF):
            for r in range(nrow):
                co[f, l, r] = jnp.broadcast_to(fields[f][r : r + 1], (8, 128))
        return carry

    lax.fori_loop(0, nlev, spread_coefs, 0)

    lane16 = lanes((half, 128))
    quad = lax.rem(lane16, 4)
    lane_l = lanes((nlev, 128))
    quad_l = lax.rem(lane_l, 4)

    def packed(field):
        acc = jnp.zeros((nlev, 128), F32)
        for r in range(nrow):
            acc = jnp.where(lax.div(lane_l, 4) == r, roll(coefs[field, :, r, :], 4 * r + 2), acc)
        return jnp.where(lane_l < 64, acc, roll(acc, 64))

    pa = packed(2) * (1.0 / 12.0)
    pd = packed(3)
    edge[0] = jnp.where(quad_l == 1, pd + 8.0 * pa, jnp.where(quad_l == 2, pd - 8.0 * pa, 0.0))
    edge[1] = pa

    for k, shape in enumerate(((256, 256), (512, 128))):
        src_lane = lax.rem(lax.broadcasted_iota(jnp.int32, shape, 0), 128)
        src_part = lax.div(lax.broadcasted_iota(jnp.int32, shape, 0), 128)
        out_col = lax.broadcasted_iota(jnp.int32, shape, 1)
        step = lax.rem(src_lane - lax.rem(out_col, 128) + 128, 128)
        first = jnp.where(step == 1, 8.0, jnp.where(step == 127, -8.0, jnp.where(step == 2, -1.0, jnp.where(step == 126, 1.0, 0.0))))
        both = jnp.where(jnp.logical_or(step == 1, step == 127), 1.0, 0.0)
        if k == 0:
            ring[...] = jnp.where(out_col < 128, first, both).astype(BF16)
        else:
            ring_t[...] = jnp.where(src_part < 2, both, -first).astype(BF16)

    has = {LOW: row > 0, HIGH: row < nrd - 1, LEFT: col > 0, RIGHT: col < ncd - 1}
    target = {LOW: (row - 1, col), HIGH: (row + 1, col), LEFT: (row, col - 1), RIGHT: (row, col + 1)}
    rims = (
        {
            LOW: (lambda l: scaled.at[l, 2:4], lambda l: scaled.at[l, nrow + 2 : nrow + 4]),
            HIGH: (lambda l: scaled.at[l, nrow : nrow + 2], lambda l: scaled.at[l, 0:2]),
            LEFT: (lambda l: pack.at[l], lambda l: pack_r.at[l]),
            RIGHT: (lambda l: pack.at[l], lambda l: pack_l.at[l]),
        },
        {
            LOW: (lambda l: to_low.at[l], lambda l: from_high.at[l]),
            HIGH: (lambda l: to_high.at[l], lambda l: from_low.at[l]),
            LEFT: (lambda l: wrap.at[l], lambda l: wrap_r.at[l]),
            RIGHT: (lambda l: wrap.at[l], lambda l: wrap_l.at[l]),
        },
    )
    opposite = {LOW: HIGH, HIGH: LOW, LEFT: RIGHT, RIGHT: LEFT}

    def rim(phase, side, l):
        src, dst = rims[phase][side]
        return pltpu.make_async_remote_copy(
            src_ref=src(l),
            dst_ref=dst(l),
            send_sem=send_sem.at[phase, side, l],
            recv_sem=recv_sem.at[phase, side, l],
            device_id=target[side],
            device_id_type=MESH,
        )

    def send(phase, l):
        for side in (LOW, HIGH, LEFT, RIGHT):
            @pl.when(has[side])
            def _():
                rim(phase, side, l).start()

    def receive(phase, l):
        for side in (LEFT, RIGHT, LOW, HIGH):
            @pl.when(has[side])
            def _():
                rim(phase, opposite[side], l).wait_recv()

    def sent(phase, l):
        for side in (LOW, HIGH, LEFT, RIGHT):
            @pl.when(has[side])
            def _():
                rim(phase, side, l).wait_send()

    zero_rows = jnp.zeros((nlev, 2, nprobe, 128), F32)
    zero_pack = jnp.zeros((nlev, half, 128), F32)

    @pl.when(row == 0)
    def _():
        scaled[:, 0:2] = zero_rows
        from_low[...] = zero_rows

    @pl.when(row == nrd - 1)
    def _():
        scaled[:, nrow + 2 : nrow + 4] = zero_rows
        from_high[...] = zero_rows

    @pl.when(col == 0)
    def _():
        pack_l[...] = zero_pack
        wrap_l[...] = zero_pack

    @pl.when(col == ncd - 1)
    def _():
        pack_r[...] = zero_pack
        wrap_r[...] = zero_pack

    loads[4].wait()
    pl.semaphore_wait(barrier, signals)

    def put(acc, r, value):
        slot = lax.div(lane16, 4)
        acc = jnp.where(slot == r, roll(value[:half], 4 * r + 2), acc)
        return jnp.where(slot == r + 16, roll(value[half:], 4 * r + 66), acc)

    wide_lane = lanes((nprobe, 128))
    at_edge = jnp.logical_or(wide_lane < 2, wide_lane >= 126)

    def take(corr, r):
        both = jnp.concatenate([roll(corr, -(4 * r + 2)), roll(corr, -(4 * r + 66))], axis=0)
        return jnp.where(at_edge, both, 0.0)

    def scale_level(l, turn):
        for p in range(nprobe):
            turn[p * nrow : (p + 1) * nrow, :] = probes[p, l].astype(F32)
        acc = jnp.zeros((half, 128), F32)
        for r in range(nrow):
            om = turn[pl.ds(r, nprobe, stride=nrow), :]
            omega[l, r] = om.astype(BF16)
            v = om * wide(co[SPR, l, r], nprobe)
            scaled[l, r + 2] = v
            acc = put(acc, r, v)
        pack[l] = acc

    def scale_group(g, carry):
        group = [g * GROUP + i for i in range(GROUP)]
        for i, l in enumerate(group):
            scale_level(l, turn.at[i])
        for l in group:
            send(0, l)
        return carry

    lax.fori_loop(0, nlev // GROUP, scale_group, 0)

    def halves(x):
        high = x.astype(BF16)
        return high, (x - high.astype(F32)).astype(BF16)

    def tangent_own(l, carry):
        above = jnp.minimum(l + 1, nlev - 1)
        below = jnp.maximum(l - 1, 0)
        acc = jnp.zeros((half, 128), F32)
        for r0 in range(0, nrow, CHUNK):
            v = scaled[l, r0 + 2 : r0 + 2 + CHUNK].reshape(CHUNK * nprobe, 128)
            cols = lax.dot_general(
                jnp.concatenate(halves(v), axis=1), ring[...], (((1,), (0,)), ((), ())), preferred_element_type=F32
            )
            for r in range(r0, r0 + CHUNK):
                at = slice((r - r0) * nprobe, (r - r0 + 1) * nprobe)
                c = [wide(co[f, l, r], nprobe) for f in range(NF)]
                t = c[CEN] * scaled[l, r + 2] + 0.2 * (scaled[above, r + 2] + scaled[below, r + 2])
                if r + 1 < nrow:
                    t = t + c[XP] * scaled[l, r + 3]
                if r >= 1:
                    t = t + c[XM] * scaled[l, r + 1]
                if r >= 2 and r + 2 < nrow:
                    t = t + c[XA] * (scaled[l, r] - scaled[l, r + 4])
                elif r >= 2:
                    t = t + c[XA] * scaled[l, r]
                else:
                    t = t - c[XA] * scaled[l, r + 4]
                t = t + c[YA] * cols[at, :128] + c[DIF] * cols[at, 128:]
                tang[l, r] = t
                if 2 <= r < nrow - 2:
                    acc = put(acc, r, t)
        strip[l] = acc
        return carry

    lax.fori_loop(0, nlev, tangent_own, 0, unroll=2)

    def tangent_outer(l):
        e1 = edge[0, pl.ds(l, 1), :]
        ea = edge[1, pl.ds(l, 1), :]
        diff = jnp.where(quad < 2, pack_l[l], pack_r[l]) - pack[l]
        near = jnp.where(quad == 1, roll(diff, -1), roll(diff, 1))
        far = jnp.where(quad < 2, -roll(diff, -2), roll(diff, 2))
        corr = e1 * near + ea * far
        acc = strip[l] + corr
        ends = {}
        last = nrow - 1

        def coef(f, r):
            return wide(co[f, l, r], nprobe)

        rim_terms = {
            0: coef(XM, 0) * scaled[l, 1] + coef(XA, 0) * scaled[l, 0],
            1: coef(XA, 1) * scaled[l, 1],
            last - 1: -(coef(XA, last - 1) * scaled[l, nrow + 2]),
            last: coef(XP, last) * scaled[l, nrow + 2] - coef(XA, last) * scaled[l, nrow + 3],
        }
        for r in rim_terms:
            t = tang[l, r] + rim_terms[r] + take(corr, r)
            tang[l, r] = t
            ends[r] = t
            acc = put(acc, r, t)

        to_low[l, 0] = coef(XA, 0) * ends[0]
        to_low[l, 1] = coef(XM, 0) * ends[0] + coef(XA, 1) * ends[1]
        to_high[l, 0] = coef(XP, last) * ends[last] - coef(XA, last - 1) * ends[last - 1]
        to_high[l, 1] = -(coef(XA, last) * ends[last])
        u = ea * acc
        w = e1 * acc
        wrap[l] = jnp.where(quad < 2, roll(u, -2), -roll(u, 2)) + jnp.where(
            quad == 1, roll(w, -1), jnp.where(quad == 2, roll(w, 1), 0.0)
        )
        for r in range(2, nrow - 2):
            tang[l, r] = tang[l, r] + take(corr, r)

    def tangent_rims(g, carry):
        group = [g * GROUP + i for i in range(GROUP)]
        for l in group:
            receive(0, l)
        for l in group:
            tangent_outer(l)
        for l in group:
            send(1, l)
        return carry

    lax.fori_loop(0, nlev // GROUP, tangent_rims, 0)

    def adjoint_own(l, carry):
        above = jnp.minimum(l + 1, nlev - 1)
        below = jnp.maximum(l - 1, 0)
        for r0 in range(0, nrow, CHUNK):
            parts = []
            for r in range(r0, r0 + CHUNK):
                w = tang[l, r]
                parts.append(
                    jnp.concatenate(
                        halves(wide(co[DIF, l, r], nprobe) * w) + halves(wide(co[YA, l, r], nprobe) * w), axis=1
                    )
                )
            cols = lax.dot_general(
                jnp.concatenate(parts, axis=0), ring_t[...], (((1,), (0,)), ((), ())), preferred_element_type=F32
            )
            for r in range(r0, r0 + CHUNK):
                b = cols[(r - r0) * nprobe : (r - r0 + 1) * nprobe]
                b = b + wide(co[CEN, l, r], nprobe) * tang[l, r] + 0.2 * (tang[above, r] + tang[below, r])
                if r + 1 < nrow:
                    b = b + wide(co[XM, l, r + 1], nprobe) * tang[l, r + 1]
                if r >= 1:
                    b = b + wide(co[XP, l, r - 1], nprobe) * tang[l, r - 1]
                if r + 2 < nrow:
                    b = b + wide(co[XA, l, r + 2], nprobe) * tang[l, r + 2]
                if r >= 2:
                    b = b - wide(co[XA, l, r - 2], nprobe) * tang[l, r - 2]
                back[l, r] = b
        return carry

    lax.fori_loop(0, nlev, adjoint_own, 0, unroll=2)

    def sketch_level(l):
        corr = jnp.where(quad < 2, wrap_r[l], wrap_l[l]) - wrap[l]
        left, right = [], []
        for r in range(nrow):
            b = back[l, r] + take(corr, r)
            if r < 2:
                b = b + from_low[l, r]
            if r >= nrow - 2:
                b = b + from_high[l, r - (nrow - 2)]
            om = omega[l, r]
            sk = om.astype(F32) + wide(co[SPR, l, r], nprobe) * b
            hi = sk.astype(BF16)
            lo = (sk - hi.astype(F32)).astype(BF16)
            z = jnp.concatenate([hi, lo], axis=0)
            zbuf[l, r] = z
            right.append(z)
            left.append(jnp.concatenate([hi, om], axis=0))
        return lax.dot_general(
            jnp.concatenate(left, axis=1),
            jnp.concatenate(right, axis=1),
            (((1,), (1,)), ((), ())),
            preferred_element_type=F32,
        )

    def sketch_rims(g, gram):
        group = [g * GROUP + i for i in range(GROUP)]
        for l in group:
            receive(1, l)
        for l in group:
            gram = gram + sketch_level(l)
        for l in group:
            pltpu.make_async_copy(zbuf.at[l], z_hbm.at[l], out_sem.at[l]).start()
        return gram

    gram = lax.fori_loop(0, nlev // GROUP, sketch_rims, jnp.zeros((2 * nprobe, 2 * nprobe), F32))

    gbuf[...] = jnp.zeros(gbuf.shape, F32)
    gbuf[:, 0 : 2 * nprobe] = gram
    full = gbuf[...]
    high, probe = full[:nprobe], full[nprobe:]
    own = high + 2.0 * roll(high, -nprobe)
    both = jnp.where(wide_lane < nprobe, own, roll(probe, nprobe) + probe)
    part = jnp.where(lane16 < 64, both[:half], roll(both[half:], 64))

    pair_part = red_a
    pair_part[0] = part
    swap = pltpu.make_async_remote_copy(
        src_ref=pair_part.at[0], dst_ref=pair_part.at[1], send_sem=red_send.at[0, 0], recv_sem=red_recv.at[0, 0],
        device_id=other, device_id_type=MESH,
    )
    swap.start()
    swap.wait_recv()
    quarter = half // 2
    mine = pl.ds(pl.multiple_of(core * quarter, quarter), quarter)
    part = pair_part[0, mine] + pair_part[1, mine]
    copies = [swap]
    for s, (buf, count, me, at) in enumerate(((red_b, plane, chip, in_plane), (red_c, outer, zi, in_line))):
        buf[me] = part
        stage = []
        for o in range(1, count):
            stage.append(
                pltpu.make_async_remote_copy(
                    src_ref=buf.at[me],
                    dst_ref=buf.at[me],
                    send_sem=red_send.at[s + 1, o],
                    recv_sem=red_recv.at[s + 1, o],
                    device_id=at(lax.rem(me + o, count)),
                    device_id_type=MESH,
                )
            )
            stage[-1].start()
        for copy in stage:
            copy.wait_recv()
        terms = [buf[o] for o in range(count)]
        while len(terms) > 1:
            terms = [sum(terms[i : i + 2][1:], terms[i]) for i in range(0, len(terms), 2)]
        part = terms[0]
        copies += stage
    total[mine] = part
    join = pltpu.make_async_remote_copy(
        src_ref=total.at[mine], dst_ref=total.at[mine], send_sem=red_send.at[0, 1], recv_sem=red_recv.at[0, 1],
        device_id=other, device_id_type=MESH,
    )
    join.start()
    join.wait_recv()
    copies.append(join)
    g_ref[...] = total[...]

    for copy in copies:
        copy.wait_send()

    def finish(l, carry):
        sent(0, l)
        sent(1, l)
        pltpu.make_async_copy(zbuf.at[l], z_hbm.at[l], out_sem.at[l]).wait()
        return carry

    lax.fori_loop(0, nlev, finish, 0)


def basis_kernel(nprobe, nlev, nrow, scale, g_ref, z_hbm, basis_hbm, factor_ref, zbuf, obuf, in_sem, out_sem):
    def load(l):
        return pltpu.make_async_copy(z_hbm.at[l], zbuf.at[l], in_sem.at[l])

    def store(l):
        return pltpu.make_async_copy(obuf.at[l], basis_hbm.at[:, l], out_sem.at[l])

    for l in range(nlev):
        load(l).start()
    half = nprobe // 2
    g = g_ref[...]
    both = jnp.concatenate([g, roll(g, 64)], axis=0)
    flip = both.T
    lane = lanes((nprobe, 128))
    sub = lax.broadcasted_iota(jnp.int32, (nprobe, 128), 0)
    pad = jnp.zeros((nprobe, 128 - nprobe), F32)
    flip_g = jnp.concatenate([flip[:nprobe], pad], axis=1)
    flip_c = jnp.concatenate([flip[nprobe : 2 * nprobe], pad], axis=1)
    sym_g = 0.5 * (both + flip_g)
    sym_c = 0.5 * (roll(both, -nprobe) + flip_c)
    m = jnp.where(lane < nprobe, sym_g, jnp.where(jnp.logical_and(lane >= 64, lane < 64 + nprobe), roll(sym_c, 64), 0.0))
    m = jnp.where(jnp.logical_or(lane == sub + nprobe, lane == sub + 64 + nprobe), 1.0, m)
    first = lane < 64
    piv = jnp.ones((nprobe, 128), F32)
    for k0 in range(0, nprobe, WIDTH):
        cols = [
            jnp.where(
                first,
                jnp.broadcast_to(m[:, k : k + 1], (nprobe, 128)),
                jnp.broadcast_to(m[:, 64 + k : 65 + k], (nprobe, 128)),
            )
            for k in range(k0, k0 + WIDTH)
        ]
        for j in range(WIDTH):
            k = k0 + j
            p = cols[j][k : k + 1]
            inv = 1.0 / p
            piv = jnp.where(sub == k, p, piv)
            below = jnp.where(sub > k, cols[j], 0.0)
            for i in range(j + 1, WIDTH):
                cols[i] = cols[i] - below * (cols[i][k : k + 1] * inv)
            m = m - below * (m[k : k + 1] * inv)
    m = m * (1.0 / jnp.sqrt(piv))
    upper = jnp.where(jnp.logical_and(lane >= sub, lane < nprobe), m, 0.0)
    inv_g = jnp.where(lane <= sub, roll(m, -nprobe), 0.0)
    inv_c = jnp.where(lane <= sub, roll(m, -(64 + nprobe)), 0.0)
    factor = lax.dot_general(
        upper, inv_c, (((1,), (1,)), ((), ())), precision=lax.Precision.HIGHEST, preferred_element_type=F32
    )
    factor_ref[...] = factor
    a = inv_g * scale
    a_hi = a.astype(BF16)
    a_lo = (a - a_hi.astype(F32)).astype(BF16)
    twice = jnp.where(lane < nprobe, a_hi.astype(F32), roll(a_hi.astype(F32), nprobe))
    twice_lo = jnp.where(lane < nprobe, a_lo.astype(F32), roll(a_lo.astype(F32), nprobe))
    lhs = jnp.concatenate([twice, twice_lo], axis=0).astype(BF16)[:, : 2 * nprobe]

    def level(l, carry):
        load(l).wait()
        for r in range(0, nrow, 2):
            out = lax.dot_general(
                lhs,
                jnp.concatenate([zbuf[l, r], zbuf[l, r + 1]], axis=1),
                (((1,), (0,)), ((), ())),
                preferred_element_type=F32,
            )
            out = out[:nprobe] + out[nprobe:]
            put_row(obuf.at[l], r, out[:, :128])
            put_row(obuf.at[l], r + 1, out[:, 128:])
        store(l).start()
        return carry

    lax.fori_loop(0, nlev, level, 0)

    def finish(l, carry):
        store(l).wait()
        return carry

    lax.fori_loop(0, nlev, finish, 0)


def shards(probes, spread, adv_x, adv_y, diffusivity):
    nprobe, nlev, nrow, ncol = probes.shape
    nrd = lax.axis_size("row")
    ncd = lax.axis_size("col")
    half = nprobe // 2
    inputs = [pltpu.with_memory_space_constraint(x, pltpu.HBM) for x in (probes, spread, adv_x, adv_y, diffusivity)]
    any_spec = pl.BlockSpec(memory_space=pltpu.HBM)
    vmem_spec = pl.BlockSpec(memory_space=pltpu.VMEM)
    rows2 = pltpu.VMEM((nlev, 2, nprobe, ncol), F32)
    strip = pltpu.VMEM((nlev, half, ncol), F32)
    plane = (nrd // 2) * INNER
    most = max(2, plane, ncd // INNER)
    z, g = pl.pallas_call(
        functools.partial(halo_kernel, (nprobe, nlev, nrow, nrd, ncd)),
        out_shape=(
            jax.ShapeDtypeStruct((nlev, nrow, 2 * nprobe, ncol), BF16),
            jax.ShapeDtypeStruct((half, ncol), F32),
        ),
        in_specs=[any_spec] * 5,
        out_specs=(any_spec, vmem_spec),
        scratch_shapes=[
            pltpu.VMEM((nprobe, nlev, nrow, ncol), BF16),
            pltpu.VMEM((4, nlev, nrow, ncol), F32),
            pltpu.VMEM((GROUP, nprobe * nrow, ncol), F32),
            pltpu.VMEM((nlev, nrow, nprobe, ncol), BF16),
            pltpu.VMEM((nlev, nrow + 4, nprobe, ncol), F32),
            pltpu.VMEM((nlev, nrow, nprobe, ncol), F32),
            pltpu.VMEM((NF, nlev, nrow, 8, ncol), F32),
            pltpu.VMEM((2, nlev, ncol), F32),
            pltpu.VMEM((256, 256), BF16),
            pltpu.VMEM((512, 128), BF16),
            strip, strip, strip, strip, strip, strip,
            rows2, rows2, rows2, rows2,
            pltpu.VMEM((nlev, nrow, nprobe, ncol), F32),
            strip,
            pltpu.VMEM((nlev, nrow, 2 * nprobe, ncol), BF16),
            pltpu.VMEM((2 * nprobe, ncol), F32),
            pltpu.VMEM((2, half, ncol), F32),
            pltpu.VMEM((plane, half // 2, ncol), F32),
            pltpu.VMEM((ncd // INNER, half // 2, ncol), F32),
            pltpu.VMEM((half, ncol), F32),
            pltpu.SemaphoreType.DMA((5,)),
            pltpu.SemaphoreType.DMA((nlev,)),
            pltpu.SemaphoreType.DMA((2, 4, nlev)),
            pltpu.SemaphoreType.DMA((2, 4, nlev)),
            pltpu.SemaphoreType.DMA((3, most)),
            pltpu.SemaphoreType.DMA((3, most)),
        ],
        compiler_params=pltpu.CompilerParams(
            collective_id=0, has_side_effects=True, vmem_limit_bytes=40 * 1024 * 1024
        ),
        name="sketch_and_sums",
    )(*inputs)
    scale = float(nlev * nrow * ncol * nrd * ncd) ** 0.5
    basis, factor = pl.pallas_call(
        functools.partial(basis_kernel, nprobe, nlev, nrow, scale),
        out_shape=(
            jax.ShapeDtypeStruct((nprobe, nlev, nrow, ncol), F32),
            jax.ShapeDtypeStruct((nprobe, nprobe), F32),
        ),
        in_specs=[vmem_spec, any_spec],
        out_specs=(any_spec, vmem_spec),
        scratch_shapes=[
            pltpu.VMEM((nlev, nrow, 2 * nprobe, ncol), BF16),
            pltpu.VMEM((nlev, nprobe, nrow, ncol), F32),
            pltpu.SemaphoreType.DMA((nlev,)),
            pltpu.SemaphoreType.DMA((nlev,)),
        ],
        compiler_params=pltpu.CompilerParams(vmem_limit_bytes=24 * 1024 * 1024),
        name="factors_and_basis",
    )(g, z)
    return basis, factor


def solution(mesh):
    return jax.shard_map(
        shards,
        mesh=mesh,
        in_specs=(
            P(None, None, "row", "col"),
            P(None, "row", "col"),
            P(None, "row", "col"),
            P(None, "row", "col"),
            P(None, "row", "col"),
        ),
        out_specs=(P(None, None, "row", "col"), P()),
        check_vma=False,
    )
```

```python
import functools

import jax
import jax.numpy as jnp
from jax import lax
from jax.experimental import pallas as pl
from jax.experimental.pallas import tpu as pltpu
from jax.sharding import PartitionSpec as P

MESH = pl.DeviceIdType.MESH
F32 = jnp.float32
BF16 = jnp.bfloat16
INNER = 4
WIDTH = 8
CHUNK = 8
GROUP = 2
NF = 7
SPR, CEN, XP, XM, XA, YA, DIF = range(NF)
LOW, HIGH, LEFT, RIGHT = range(4)


def lanes(shape):
    return lax.broadcasted_iota(jnp.int32, shape, 1)


def roll(x, shift):
    return pltpu.roll(x, shift % 128, 1)


def put_row(ref, r, value):
    n, rows, width = ref.shape
    ref.reshape(n * rows, width)[pl.ds(r, n, stride=rows), :] = value


def wide(coef, nprobe):
    return jnp.broadcast_to(coef[None], (nprobe // 8, 8, 128)).reshape(nprobe, 128)


def halo_kernel(
    dims,
    probes_hbm, spread_hbm, advx_hbm, advy_hbm, diff_hbm,
    z_hbm, g_ref,
    probes, coefs, turn, omega, scaled, tang, co, edge, ring, ring_t,
    pack, pack_l, pack_r, wrap, wrap_l, wrap_r,
    to_low, to_high, from_low, from_high,
    back, strip, zbuf, gbuf, red_a, red_b, red_c, total,
    in_sem, out_sem, send_sem, recv_sem, red_send, red_recv,
):
    nprobe, nlev, nrow, nrd, ncd = dims
    outer = ncd // INNER
    row = lax.axis_index("row")
    col = lax.axis_index("col")
    zi = col // INNER
    xi = lax.rem(col, INNER)
    half = nprobe // 2

    loads = []
    for i, src in enumerate((spread_hbm, advx_hbm, advy_hbm, diff_hbm)):
        loads.append(pltpu.make_async_copy(src, coefs.at[i], in_sem.at[i]))
    loads.append(pltpu.make_async_copy(probes_hbm, probes, in_sem.at[4]))
    for load in loads:
        load.start()

    core = lax.rem(row, 2)
    chip = (row // 2) * INNER + xi
    plane = (nrd // 2) * INNER

    def far(o, count):
        return min(o, count - o)

    yi = row // 2
    tall = nrd // 2
    steps = [(dy, dx) for dy in range(tall) for dx in range(INNER)][1:]
    steps.sort(key=lambda st: -(far(st[0], tall) + far(st[1], INNER)))
    in_plane = [
        (lax.rem(yi + dy, tall) * 2 + core, zi * INNER + lax.rem(xi + dx, INNER)) for dy, dx in steps
    ]
    in_line = [
        (row, lax.rem(zi + o, outer) * INNER + xi) for o in sorted(range(1, outer), key=lambda o: -far(o, outer))
    ]
    other = (row + 1 - 2 * core, col)
    barrier = pltpu.get_barrier_semaphore()
    greet = [other]
    greet += [(lax.rem(row + o, nrd), col) for o in (1, nrd - 1)]
    greet += [(row, lax.rem(col + o, ncd)) for o in (1, ncd - 1)]
    greet += in_plane + in_line
    for device in greet:
        pl.semaphore_signal(barrier, inc=1, device_id=device, device_id_type=MESH)
    signals = len(greet)

    for load in loads[:4]:
        load.wait()

    def spread_coefs(l, carry):
        ax = coefs[1, l] * (1.0 / 12.0)
        ay = coefs[2, l] * (1.0 / 12.0)
        d = coefs[3, l]
        fields = (coefs[0, l], 0.6 - 4.0 * d, d + 8.0 * ax, d - 8.0 * ax, ax, ay, d)
        for f in range(NF):
            for r in range(nrow):
                co[f, l, r] = jnp.broadcast_to(fields[f][r : r + 1], (8, 128))
        return carry

    lax.fori_loop(0, nlev, spread_coefs, 0)

    lane16 = lanes((half, 128))
    quad = lax.rem(lane16, 4)
    lane_l = lanes((nlev, 128))
    quad_l = lax.rem(lane_l, 4)

    def packed(field):
        acc = jnp.zeros((nlev, 128), F32)
        for r in range(nrow):
            acc = jnp.where(lax.div(lane_l, 4) == r, roll(coefs[field, :, r, :], 4 * r + 2), acc)
        return jnp.where(lane_l < 64, acc, roll(acc, 64))

    pa = packed(2) * (1.0 / 12.0)
    pd = packed(3)
    edge[0] = jnp.where(quad_l == 1, pd + 8.0 * pa, jnp.where(quad_l == 2, pd - 8.0 * pa, 0.0))
    edge[1] = pa

    for k, shape in enumerate(((256, 256), (512, 128))):
        src_lane = lax.rem(lax.broadcasted_iota(jnp.int32, shape, 0), 128)
        src_part = lax.div(lax.broadcasted_iota(jnp.int32, shape, 0), 128)
        out_col = lax.broadcasted_iota(jnp.int32, shape, 1)
        step = lax.rem(src_lane - lax.rem(out_col, 128) + 128, 128)
        first = jnp.where(step == 1, 8.0, jnp.where(step == 127, -8.0, jnp.where(step == 2, -1.0, jnp.where(step == 126, 1.0, 0.0))))
        both = jnp.where(jnp.logical_or(step == 1, step == 127), 1.0, 0.0)
        if k == 0:
            ring[...] = jnp.where(out_col < 128, first, both).astype(BF16)
        else:
            ring_t[...] = jnp.where(src_part < 2, both, -first).astype(BF16)

    has = {LOW: row > 0, HIGH: row < nrd - 1, LEFT: col > 0, RIGHT: col < ncd - 1}
    target = {LOW: (row - 1, col), HIGH: (row + 1, col), LEFT: (row, col - 1), RIGHT: (row, col + 1)}
    def some(g):
        return pl.ds(g * GROUP, GROUP)

    rims = (
        {
            LOW: (lambda g: scaled.at[some(g), 2:4], lambda g: scaled.at[some(g), nrow + 2 : nrow + 4]),
            HIGH: (lambda g: scaled.at[some(g), nrow : nrow + 2], lambda g: scaled.at[some(g), 0:2]),
            LEFT: (lambda g: pack.at[some(g)], lambda g: pack_r.at[some(g)]),
            RIGHT: (lambda g: pack.at[some(g)], lambda g: pack_l.at[some(g)]),
        },
        {
            LOW: (lambda g: to_low.at[some(g)], lambda g: from_high.at[some(g)]),
            HIGH: (lambda g: to_high.at[some(g)], lambda g: from_low.at[some(g)]),
            LEFT: (lambda g: wrap.at[some(g)], lambda g: wrap_r.at[some(g)]),
            RIGHT: (lambda g: wrap.at[some(g)], lambda g: wrap_l.at[some(g)]),
        },
    )
    opposite = {LOW: HIGH, HIGH: LOW, LEFT: RIGHT, RIGHT: LEFT}

    def rim(phase, side, g):
        src, dst = rims[phase][side]
        return pltpu.make_async_remote_copy(
            src_ref=src(g),
            dst_ref=dst(g),
            send_sem=send_sem.at[phase, side, g],
            recv_sem=recv_sem.at[phase, side, g],
            device_id=target[side],
            device_id_type=MESH,
        )

    def send(phase, g):
        for side in (LOW, HIGH, LEFT, RIGHT):
            @pl.when(has[side])
            def _():
                rim(phase, side, g).start()

    def receive(phase, g):
        for side in (LEFT, RIGHT, LOW, HIGH):
            @pl.when(has[side])
            def _():
                rim(phase, opposite[side], g).wait_recv()

    def sent(phase, g):
        for side in (LOW, HIGH, LEFT, RIGHT):
            @pl.when(has[side])
            def _():
                rim(phase, side, g).wait_send()

    zero_rows = jnp.zeros((nlev, 2, nprobe, 128), F32)
    zero_pack = jnp.zeros((nlev, half, 128), F32)

    @pl.when(row == 0)
    def _():
        scaled[:, 0:2] = zero_rows
        from_low[...] = zero_rows

    @pl.when(row == nrd - 1)
    def _():
        scaled[:, nrow + 2 : nrow + 4] = zero_rows
        from_high[...] = zero_rows

    @pl.when(col == 0)
    def _():
        pack_l[...] = zero_pack
        wrap_l[...] = zero_pack

    @pl.when(col == ncd - 1)
    def _():
        pack_r[...] = zero_pack
        wrap_r[...] = zero_pack

    loads[4].wait()
    pl.semaphore_wait(barrier, signals)

    def put(acc, r, value):
        slot = lax.div(lane16, 4)
        acc = jnp.where(slot == r, roll(value[:half], 4 * r + 2), acc)
        return jnp.where(slot == r + 16, roll(value[half:], 4 * r + 66), acc)

    wide_lane = lanes((nprobe, 128))
    at_edge = jnp.logical_or(wide_lane < 2, wide_lane >= 126)

    def take(corr, r):
        both = jnp.concatenate([roll(corr, -(4 * r + 2)), roll(corr, -(4 * r + 66))], axis=0)
        return jnp.where(at_edge, both, 0.0)

    def scale_level(l, turn):
        for p in range(nprobe):
            turn[p * nrow : (p + 1) * nrow, :] = probes[p, l].astype(F32)
        acc = jnp.zeros((half, 128), F32)
        for r in range(nrow):
            om = turn[pl.ds(r, nprobe, stride=nrow), :]
            omega[l, r] = om.astype(BF16)
            v = om * wide(co[SPR, l, r], nprobe)
            scaled[l, r + 2] = v
            acc = put(acc, r, v)
        pack[l] = acc

    def scale_group(g, carry):
        group = [g * GROUP + i for i in range(GROUP)]
        for i, l in enumerate(group):
            scale_level(l, turn.at[i])
        send(0, g)
        return carry

    lax.fori_loop(0, nlev // GROUP, scale_group, 0)

    def halves(x):
        high = x.astype(BF16)
        return high, (x - high.astype(F32)).astype(BF16)

    def tangent_own(l, carry):
        above = jnp.minimum(l + 1, nlev - 1)
        below = jnp.maximum(l - 1, 0)
        acc = jnp.zeros((half, 128), F32)
        for r0 in range(0, nrow, CHUNK):
            v = scaled[l, r0 + 2 : r0 + 2 + CHUNK].reshape(CHUNK * nprobe, 128)
            cols = lax.dot_general(
                jnp.concatenate(halves(v), axis=1), ring[...], (((1,), (0,)), ((), ())), preferred_element_type=F32
            )
            for r in range(r0, r0 + CHUNK):
                at = slice((r - r0) * nprobe, (r - r0 + 1) * nprobe)
                c = [wide(co[f, l, r], nprobe) for f in range(NF)]
                t = c[CEN] * scaled[l, r + 2] + 0.2 * (scaled[above, r + 2] + scaled[below, r + 2])
                if r + 1 < nrow:
                    t = t + c[XP] * scaled[l, r + 3]
                if r >= 1:
                    t = t + c[XM] * scaled[l, r + 1]
                if r >= 2 and r + 2 < nrow:
                    t = t + c[XA] * (scaled[l, r] - scaled[l, r + 4])
                elif r >= 2:
                    t = t + c[XA] * scaled[l, r]
                else:
                    t = t - c[XA] * scaled[l, r + 4]
                t = t + c[YA] * cols[at, :128] + c[DIF] * cols[at, 128:]
                tang[l, r] = t
                if 2 <= r < nrow - 2:
                    acc = put(acc, r, t)
        strip[l] = acc
        return carry

    lax.fori_loop(0, nlev, tangent_own, 0, unroll=2)

    def tangent_outer(l):
        e1 = edge[0, pl.ds(l, 1), :]
        ea = edge[1, pl.ds(l, 1), :]
        diff = jnp.where(quad < 2, pack_l[l], pack_r[l]) - pack[l]
        near = jnp.where(quad == 1, roll(diff, -1), roll(diff, 1))
        far = jnp.where(quad < 2, -roll(diff, -2), roll(diff, 2))
        corr = e1 * near + ea * far
        acc = strip[l] + corr
        ends = {}
        last = nrow - 1

        def coef(f, r):
            return wide(co[f, l, r], nprobe)

        rim_terms = {
            0: coef(XM, 0) * scaled[l, 1] + coef(XA, 0) * scaled[l, 0],
            1: coef(XA, 1) * scaled[l, 1],
            last - 1: -(coef(XA, last - 1) * scaled[l, nrow + 2]),
            last: coef(XP, last) * scaled[l, nrow + 2] - coef(XA, last) * scaled[l, nrow + 3],
        }
        for r in rim_terms:
            t = tang[l, r] + rim_terms[r] + take(corr, r)
            tang[l, r] = t
            ends[r] = t
            acc = put(acc, r, t)

        to_low[l, 0] = coef(XA, 0) * ends[0]
        to_low[l, 1] = coef(XM, 0) * ends[0] + coef(XA, 1) * ends[1]
        to_high[l, 0] = coef(XP, last) * ends[last] - coef(XA, last - 1) * ends[last - 1]
        to_high[l, 1] = -(coef(XA, last) * ends[last])
        u = ea * acc
        w = e1 * acc
        wrap[l] = jnp.where(quad < 2, roll(u, -2), -roll(u, 2)) + jnp.where(
            quad == 1, roll(w, -1), jnp.where(quad == 2, roll(w, 1), 0.0)
        )
        for r in range(2, nrow - 2):
            tang[l, r] = tang[l, r] + take(corr, r)

    def tangent_rims(g, carry):
        group = [g * GROUP + i for i in range(GROUP)]
        receive(0, g)
        for l in group:
            tangent_outer(l)
        send(1, g)
        return carry

    lax.fori_loop(0, nlev // GROUP, tangent_rims, 0)

    def adjoint_own(l, carry):
        above = jnp.minimum(l + 1, nlev - 1)
        below = jnp.maximum(l - 1, 0)
        for r0 in range(0, nrow, CHUNK):
            parts = []
            for r in range(r0, r0 + CHUNK):
                w = tang[l, r]
                parts.append(
                    jnp.concatenate(
                        halves(wide(co[DIF, l, r], nprobe) * w) + halves(wide(co[YA, l, r], nprobe) * w), axis=1
                    )
                )
            cols = lax.dot_general(
                jnp.concatenate(parts, axis=0), ring_t[...], (((1,), (0,)), ((), ())), preferred_element_type=F32
            )
            for r in range(r0, r0 + CHUNK):
                b = cols[(r - r0) * nprobe : (r - r0 + 1) * nprobe]
                b = b + wide(co[CEN, l, r], nprobe) * tang[l, r] + 0.2 * (tang[above, r] + tang[below, r])
                if r + 1 < nrow:
                    b = b + wide(co[XM, l, r + 1], nprobe) * tang[l, r + 1]
                if r >= 1:
                    b = b + wide(co[XP, l, r - 1], nprobe) * tang[l, r - 1]
                if r + 2 < nrow:
                    b = b + wide(co[XA, l, r + 2], nprobe) * tang[l, r + 2]
                if r >= 2:
                    b = b - wide(co[XA, l, r - 2], nprobe) * tang[l, r - 2]
                back[l, r] = b
        return carry

    lax.fori_loop(0, nlev, adjoint_own, 0, unroll=2)

    def sketch_level(l):
        corr = jnp.where(quad < 2, wrap_r[l], wrap_l[l]) - wrap[l]
        left, right = [], []
        for r in range(nrow):
            b = back[l, r] + take(corr, r)
            if r < 2:
                b = b + from_low[l, r]
            if r >= nrow - 2:
                b = b + from_high[l, r - (nrow - 2)]
            om = omega[l, r]
            sk = om.astype(F32) + wide(co[SPR, l, r], nprobe) * b
            hi = sk.astype(BF16)
            lo = (sk - hi.astype(F32)).astype(BF16)
            z = jnp.concatenate([hi, lo], axis=0)
            zbuf[l, r] = z
            right.append(z)
            left.append(jnp.concatenate([hi, om], axis=0))
        return lax.dot_general(
            jnp.concatenate(left, axis=1),
            jnp.concatenate(right, axis=1),
            (((1,), (1,)), ((), ())),
            preferred_element_type=F32,
        )

    def sketch_rims(g, gram):
        group = [g * GROUP + i for i in range(GROUP)]
        receive(1, g)
        for l in group:
            gram = gram + sketch_level(l)
        pltpu.make_async_copy(zbuf.at[some(g)], z_hbm.at[some(g)], out_sem.at[g]).start()
        return gram

    gram = lax.fori_loop(0, nlev // GROUP, sketch_rims, jnp.zeros((2 * nprobe, 2 * nprobe), F32))

    gbuf[...] = jnp.zeros(gbuf.shape, F32)
    gbuf[:, 0 : 2 * nprobe] = gram
    full = gbuf[...]
    high, probe = full[:nprobe], full[nprobe:]
    own = high + 2.0 * roll(high, -nprobe)
    both = jnp.where(wide_lane < nprobe, own, roll(probe, nprobe) + probe)
    part = jnp.where(lane16 < 64, both[:half], roll(both[half:], 64))

    pair_part = red_a
    pair_part[0] = part
    swap = pltpu.make_async_remote_copy(
        src_ref=pair_part.at[0], dst_ref=pair_part.at[1], send_sem=red_send.at[0, 0], recv_sem=red_recv.at[0, 0],
        device_id=other, device_id_type=MESH,
    )
    swap.start()
    swap.wait_recv()
    quarter = half // 2
    mine = pl.ds(pl.multiple_of(core * quarter, quarter), quarter)
    part = pair_part[0, mine] + pair_part[1, mine]

    def finish(g, carry):
        sent(0, g)
        sent(1, g)
        pltpu.make_async_copy(zbuf.at[some(g)], z_hbm.at[some(g)], out_sem.at[g]).wait()
        return carry

    pending = [swap]
    for s, (buf, count, me, reach) in enumerate(((red_b, plane, chip, in_plane), (red_c, outer, zi, in_line))):
        buf[me] = part
        stage = []
        for o, device in enumerate(reach):
            stage.append(
                pltpu.make_async_remote_copy(
                    src_ref=buf.at[me],
                    dst_ref=buf.at[me],
                    send_sem=red_send.at[s + 1, o],
                    recv_sem=red_recv.at[s + 1, o],
                    device_id=device,
                    device_id_type=MESH,
                )
            )
            stage[-1].start()
        if s == 0:
            lax.fori_loop(0, nlev // GROUP, finish, 0)
        for copy in pending:
            copy.wait_send()
        pending = stage
        for copy in reversed(stage):
            copy.wait_recv()
        terms = [buf[o] for o in range(count)]
        while len(terms) > 1:
            terms = [sum(terms[i : i + 2][1:], terms[i]) for i in range(0, len(terms), 2)]
        part = terms[0]
    total[mine] = part
    join = pltpu.make_async_remote_copy(
        src_ref=total.at[mine], dst_ref=total.at[mine], send_sem=red_send.at[0, 1], recv_sem=red_recv.at[0, 1],
        device_id=other, device_id_type=MESH,
    )
    join.start()
    for copy in pending:
        copy.wait_send()
    join.wait_recv()
    g_ref[...] = total[...]
    join.wait_send()


def basis_kernel(nprobe, nlev, nrow, scale, g_ref, z_hbm, basis_hbm, factor_ref, zbuf, obuf, in_sem, out_sem):
    def load(l):
        return pltpu.make_async_copy(z_hbm.at[l], zbuf.at[l], in_sem.at[l])

    def store(l):
        return pltpu.make_async_copy(obuf.at[l], basis_hbm.at[:, l], out_sem.at[l])

    for l in range(nlev):
        load(l).start()
    half = nprobe // 2
    g = g_ref[...]
    both = jnp.concatenate([g, roll(g, 64)], axis=0)
    flip = both.T
    lane = lanes((nprobe, 128))
    sub = lax.broadcasted_iota(jnp.int32, (nprobe, 128), 0)
    pad = jnp.zeros((nprobe, 128 - nprobe), F32)
    flip_g = jnp.concatenate([flip[:nprobe], pad], axis=1)
    flip_c = jnp.concatenate([flip[nprobe : 2 * nprobe], pad], axis=1)
    sym_g = 0.5 * (both + flip_g)
    sym_c = 0.5 * (roll(both, -nprobe) + flip_c)
    m = jnp.where(lane < nprobe, sym_g, jnp.where(jnp.logical_and(lane >= 64, lane < 64 + nprobe), roll(sym_c, 64), 0.0))
    m = jnp.where(jnp.logical_or(lane == sub + nprobe, lane == sub + 64 + nprobe), 1.0, m)
    first = lane < 64
    piv = jnp.ones((nprobe, 128), F32)
    for k0 in range(0, nprobe, WIDTH):
        cols = [
            jnp.where(
                first,
                jnp.broadcast_to(m[:, k : k + 1], (nprobe, 128)),
                jnp.broadcast_to(m[:, 64 + k : 65 + k], (nprobe, 128)),
            )
            for k in range(k0, k0 + WIDTH)
        ]
        for j in range(WIDTH):
            k = k0 + j
            p = cols[j][k : k + 1]
            inv = 1.0 / p
            piv = jnp.where(sub == k, p, piv)
            below = jnp.where(sub > k, cols[j], 0.0)
            for i in range(j + 1, WIDTH):
                cols[i] = cols[i] - below * (cols[i][k : k + 1] * inv)
            m = m - below * (m[k : k + 1] * inv)
    m = m * (1.0 / jnp.sqrt(piv))
    upper = jnp.where(jnp.logical_and(lane >= sub, lane < nprobe), m, 0.0)
    inv_g = jnp.where(lane <= sub, roll(m, -nprobe), 0.0)
    inv_c = jnp.where(lane <= sub, roll(m, -(64 + nprobe)), 0.0)
    factor = lax.dot_general(
        upper, inv_c, (((1,), (1,)), ((), ())), precision=lax.Precision.HIGHEST, preferred_element_type=F32
    )
    factor_ref[...] = factor
    a = inv_g * scale
    a_hi = a.astype(BF16)
    a_lo = (a - a_hi.astype(F32)).astype(BF16)
    twice = jnp.where(lane < nprobe, a_hi.astype(F32), roll(a_hi.astype(F32), nprobe))
    twice_lo = jnp.where(lane < nprobe, a_lo.astype(F32), roll(a_lo.astype(F32), nprobe))
    lhs = jnp.concatenate([twice, twice_lo], axis=0).astype(BF16)[:, : 2 * nprobe]

    def level(l, carry):
        load(l).wait()
        for r in range(0, nrow, 2):
            out = lax.dot_general(
                lhs,
                jnp.concatenate([zbuf[l, r], zbuf[l, r + 1]], axis=1),
                (((1,), (0,)), ((), ())),
                preferred_element_type=F32,
            )
            out = out[:nprobe] + out[nprobe:]
            put_row(obuf.at[l], r, out[:, :128])
            put_row(obuf.at[l], r + 1, out[:, 128:])
        store(l).start()
        return carry

    lax.fori_loop(0, nlev, level, 0)

    def finish(l, carry):
        store(l).wait()
        return carry

    lax.fori_loop(0, nlev, finish, 0)


def shards(probes, spread, adv_x, adv_y, diffusivity):
    nprobe, nlev, nrow, ncol = probes.shape
    nrd = lax.axis_size("row")
    ncd = lax.axis_size("col")
    half = nprobe // 2
    inputs = [pltpu.with_memory_space_constraint(x, pltpu.HBM) for x in (probes, spread, adv_x, adv_y, diffusivity)]
    any_spec = pl.BlockSpec(memory_space=pltpu.HBM)
    vmem_spec = pl.BlockSpec(memory_space=pltpu.VMEM)
    rows2 = pltpu.VMEM((nlev, 2, nprobe, ncol), F32)
    strip = pltpu.VMEM((nlev, half, ncol), F32)
    plane = (nrd // 2) * INNER
    most = max(2, plane, ncd // INNER)
    z, g = pl.pallas_call(
        functools.partial(halo_kernel, (nprobe, nlev, nrow, nrd, ncd)),
        out_shape=(
            jax.ShapeDtypeStruct((nlev, nrow, 2 * nprobe, ncol), BF16),
            jax.ShapeDtypeStruct((half, ncol), F32),
        ),
        in_specs=[any_spec] * 5,
        out_specs=(any_spec, vmem_spec),
        scratch_shapes=[
            pltpu.VMEM((nprobe, nlev, nrow, ncol), BF16),
            pltpu.VMEM((4, nlev, nrow, ncol), F32),
            pltpu.VMEM((GROUP, nprobe * nrow, ncol), F32),
            pltpu.VMEM((nlev, nrow, nprobe, ncol), BF16),
            pltpu.VMEM((nlev, nrow + 4, nprobe, ncol), F32),
            pltpu.VMEM((nlev, nrow, nprobe, ncol), F32),
            pltpu.VMEM((NF, nlev, nrow, 8, ncol), F32),
            pltpu.VMEM((2, nlev, ncol), F32),
            pltpu.VMEM((256, 256), BF16),
            pltpu.VMEM((512, 128), BF16),
            strip, strip, strip, strip, strip, strip,
            rows2, rows2, rows2, rows2,
            pltpu.VMEM((nlev, nrow, nprobe, ncol), F32),
            strip,
            pltpu.VMEM((nlev, nrow, 2 * nprobe, ncol), BF16),
            pltpu.VMEM((2 * nprobe, ncol), F32),
            pltpu.VMEM((2, half, ncol), F32),
            pltpu.VMEM((plane, half // 2, ncol), F32),
            pltpu.VMEM((ncd // INNER, half // 2, ncol), F32),
            pltpu.VMEM((half, ncol), F32),
            pltpu.SemaphoreType.DMA((5,)),
            pltpu.SemaphoreType.DMA((nlev // GROUP,)),
            pltpu.SemaphoreType.DMA((2, 4, nlev // GROUP)),
            pltpu.SemaphoreType.DMA((2, 4, nlev // GROUP)),
            pltpu.SemaphoreType.DMA((3, most)),
            pltpu.SemaphoreType.DMA((3, most)),
        ],
        compiler_params=pltpu.CompilerParams(
            collective_id=0, has_side_effects=True, vmem_limit_bytes=40 * 1024 * 1024
        ),
        name="sketch_and_sums",
    )(*inputs)
    scale = float(nlev * nrow * ncol * nrd * ncd) ** 0.5
    basis, factor = pl.pallas_call(
        functools.partial(basis_kernel, nprobe, nlev, nrow, scale),
        out_shape=(
            jax.ShapeDtypeStruct((nprobe, nlev, nrow, ncol), F32),
            jax.ShapeDtypeStruct((nprobe, nprobe), F32),
        ),
        in_specs=[vmem_spec, any_spec],
        out_specs=(any_spec, vmem_spec),
        scratch_shapes=[
            pltpu.VMEM((nlev, nrow, 2 * nprobe, ncol), BF16),
            pltpu.VMEM((nlev, nprobe, nrow, ncol), F32),
            pltpu.SemaphoreType.DMA((nlev,)),
            pltpu.SemaphoreType.DMA((nlev,)),
        ],
        compiler_params=pltpu.CompilerParams(vmem_limit_bytes=24 * 1024 * 1024),
        name="factors_and_basis",
    )(g, z)
    return basis, factor


def solution(mesh):
    return jax.shard_map(
        shards,
        mesh=mesh,
        in_specs=(
            P(None, None, "row", "col"),
            P(None, "row", "col"),
            P(None, "row", "col"),
            P(None, "row", "col"),
            P(None, "row", "col"),
        ),
        out_specs=(P(None, None, "row", "col"), P()),
        check_vma=False,
    )
```

```python
import functools

import jax
import jax.numpy as jnp
from jax import lax
from jax.experimental import pallas as pl
from jax.experimental.pallas import tpu as pltpu
from jax.sharding import PartitionSpec as P

MESH = pl.DeviceIdType.MESH
F32 = jnp.float32
BF16 = jnp.bfloat16
INNER = 4
WIDTH = 8
CHUNK = 8
GROUP = 2
NF = 7
SPR, CEN, XP, XM, XA, YA, DIF = range(NF)
LOW, HIGH, LEFT, RIGHT = range(4)


def lanes(shape):
    return lax.broadcasted_iota(jnp.int32, shape, 1)


def roll(x, shift):
    return pltpu.roll(x, shift % 128, 1)


def put_row(ref, r, value):
    n, rows, width = ref.shape
    ref.reshape(n * rows, width)[pl.ds(r, n, stride=rows), :] = value


def wide(coef, nprobe):
    return jnp.broadcast_to(coef[None], (nprobe // 8, 8, 128)).reshape(nprobe, 128)


def halo_kernel(
    dims,
    probes_hbm, spread_hbm, advx_hbm, advy_hbm, diff_hbm,
    z_hbm, g_hbm,
    probes, coefs, turn, omega, scaled, tang, co, edge, ring, ring_t,
    pack, pack_l, pack_r, wrap, wrap_l, wrap_r,
    to_low, to_high, from_low, from_high,
    back, strip, zbuf, gbuf, red_a, red_b, red_c, total,
    in_sem, out_sem, send_sem, recv_sem, red_send, red_recv, news,
):
    nprobe, nlev, nrow, nrd, ncd = dims
    outer = ncd // INNER
    row = lax.axis_index("row")
    col = lax.axis_index("col")
    zi = col // INNER
    xi = lax.rem(col, INNER)
    half = nprobe // 2

    loads = []
    for i, src in enumerate((spread_hbm, advx_hbm, advy_hbm, diff_hbm)):
        loads.append(pltpu.make_async_copy(src, coefs.at[i], in_sem.at[i]))
    loads.append(pltpu.make_async_copy(probes_hbm, probes, in_sem.at[4]))
    for load in loads:
        load.start()

    core = lax.rem(row, 2)
    chip = (row // 2) * INNER + xi
    plane = (nrd // 2) * INNER

    def far(o, count):
        return min(o, count - o)

    yi = row // 2
    tall = nrd // 2
    steps = [(dy, dx) for dy in range(tall) for dx in range(INNER)][1:]
    steps.sort(key=lambda st: -(far(st[0], tall) + far(st[1], INNER)))
    in_plane = [
        (lax.rem(yi + dy, tall) * 2 + core, zi * INNER + lax.rem(xi + dx, INNER)) for dy, dx in steps
    ]
    in_line = [
        (row, lax.rem(zi + o, outer) * INNER + xi) for o in sorted(range(1, outer), key=lambda o: -far(o, outer))
    ]
    other = (row + 1 - 2 * core, col)
    barrier = pltpu.get_barrier_semaphore()
    greet = [other]
    greet += [(lax.rem(row + o, nrd), col) for o in (1, nrd - 1)]
    greet += [(row, lax.rem(col + o, ncd)) for o in (1, ncd - 1)]
    next_x = [(row, zi * INNER + lax.rem(xi + o, INNER)) for o in (1, INNER - 1)]
    next_y = [(lax.rem(yi + o, tall) * 2 + core, col) for o in (1, tall - 1)]
    next_z = [(row, lax.rem(zi + o, outer) * INNER + xi) for o in (1, outer - 1)]
    skip_z = [(row, lax.rem(zi + o, outer) * INNER + xi) for o in (2, outer - 2)]
    greet += next_x + next_y + next_z
    for device in greet:
        pl.semaphore_signal(barrier, inc=1, device_id=device, device_id_type=MESH)
    signals = len(greet)

    def tell(n, devices):
        for device in devices:
            pl.semaphore_signal(news.at[n], inc=1, device_id=device, device_id_type=MESH)

    def hear(n):
        pl.semaphore_wait(news.at[n], 2)


    for load in loads[:4]:
        load.wait()

    def spread_coefs(l, carry):
        ax = coefs[1, l] * (1.0 / 12.0)
        ay = coefs[2, l] * (1.0 / 12.0)
        d = coefs[3, l]
        fields = (coefs[0, l], 0.6 - 4.0 * d, d + 8.0 * ax, d - 8.0 * ax, ax, ay, d)
        for f in range(NF):
            for r in range(nrow):
                co[f, l, r] = jnp.broadcast_to(fields[f][r : r + 1], (8, 128))
        return carry

    lax.fori_loop(0, nlev, spread_coefs, 0)

    lane16 = lanes((half, 128))
    quad = lax.rem(lane16, 4)
    lane_l = lanes((nlev, 128))
    quad_l = lax.rem(lane_l, 4)

    def packed(field):
        acc = jnp.zeros((nlev, 128), F32)
        for r in range(nrow):
            acc = jnp.where(lax.div(lane_l, 4) == r, roll(coefs[field, :, r, :], 4 * r + 2), acc)
        return jnp.where(lane_l < 64, acc, roll(acc, 64))

    pa = packed(2) * (1.0 / 12.0)
    pd = packed(3)
    edge[0] = jnp.where(quad_l == 1, pd + 8.0 * pa, jnp.where(quad_l == 2, pd - 8.0 * pa, 0.0))
    edge[1] = pa

    for k, shape in enumerate(((256, 256), (512, 128))):
        src_lane = lax.rem(lax.broadcasted_iota(jnp.int32, shape, 0), 128)
        src_part = lax.div(lax.broadcasted_iota(jnp.int32, shape, 0), 128)
        out_col = lax.broadcasted_iota(jnp.int32, shape, 1)
        step = lax.rem(src_lane - lax.rem(out_col, 128) + 128, 128)
        first = jnp.where(step == 1, 8.0, jnp.where(step == 127, -8.0, jnp.where(step == 2, -1.0, jnp.where(step == 126, 1.0, 0.0))))
        both = jnp.where(jnp.logical_or(step == 1, step == 127), 1.0, 0.0)
        if k == 0:
            ring[...] = jnp.where(out_col < 128, first, both).astype(BF16)
        else:
            ring_t[...] = jnp.where(src_part < 2, both, -first).astype(BF16)

    has = {LOW: row > 0, HIGH: row < nrd - 1, LEFT: col > 0, RIGHT: col < ncd - 1}
    target = {LOW: (row - 1, col), HIGH: (row + 1, col), LEFT: (row, col - 1), RIGHT: (row, col + 1)}
    def some(g):
        return pl.ds(g * GROUP, GROUP)

    rims = (
        {
            LOW: (lambda g: scaled.at[some(g), 2:4], lambda g: scaled.at[some(g), nrow + 2 : nrow + 4]),
            HIGH: (lambda g: scaled.at[some(g), nrow : nrow + 2], lambda g: scaled.at[some(g), 0:2]),
            LEFT: (lambda g: pack.at[some(g)], lambda g: pack_r.at[some(g)]),
            RIGHT: (lambda g: pack.at[some(g)], lambda g: pack_l.at[some(g)]),
        },
        {
            LOW: (lambda g: to_low.at[some(g)], lambda g: from_high.at[some(g)]),
            HIGH: (lambda g: to_high.at[some(g)], lambda g: from_low.at[some(g)]),
            LEFT: (lambda g: wrap.at[some(g)], lambda g: wrap_r.at[some(g)]),
            RIGHT: (lambda g: wrap.at[some(g)], lambda g: wrap_l.at[some(g)]),
        },
    )
    opposite = {LOW: HIGH, HIGH: LOW, LEFT: RIGHT, RIGHT: LEFT}

    def rim(phase, side, g):
        src, dst = rims[phase][side]
        return pltpu.make_async_remote_copy(
            src_ref=src(g),
            dst_ref=dst(g),
            send_sem=send_sem.at[phase, side, g],
            recv_sem=recv_sem.at[phase, side, g],
            device_id=target[side],
            device_id_type=MESH,
        )

    def send(phase, g):
        for side in (LOW, HIGH, LEFT, RIGHT):
            @pl.when(has[side])
            def _():
                rim(phase, side, g).start()

    def receive(phase, g):
        for side in (LEFT, RIGHT, LOW, HIGH):
            @pl.when(has[side])
            def _():
                rim(phase, opposite[side], g).wait_recv()

    def sent(phase, g):
        for side in (LOW, HIGH, LEFT, RIGHT):
            @pl.when(has[side])
            def _():
                rim(phase, side, g).wait_send()

    zero_rows = jnp.zeros((nlev, 2, nprobe, 128), F32)
    zero_pack = jnp.zeros((nlev, half, 128), F32)

    @pl.when(row == 0)
    def _():
        scaled[:, 0:2] = zero_rows
        from_low[...] = zero_rows

    @pl.when(row == nrd - 1)
    def _():
        scaled[:, nrow + 2 : nrow + 4] = zero_rows
        from_high[...] = zero_rows

    @pl.when(col == 0)
    def _():
        pack_l[...] = zero_pack
        wrap_l[...] = zero_pack

    @pl.when(col == ncd - 1)
    def _():
        pack_r[...] = zero_pack
        wrap_r[...] = zero_pack

    loads[4].wait()
    pl.semaphore_wait(barrier, signals)

    def put(acc, r, value):
        slot = lax.div(lane16, 4)
        acc = jnp.where(slot == r, roll(value[:half], 4 * r + 2), acc)
        return jnp.where(slot == r + 16, roll(value[half:], 4 * r + 66), acc)

    wide_lane = lanes((nprobe, 128))
    at_edge = jnp.logical_or(wide_lane < 2, wide_lane >= 126)

    def take(corr, r):
        both = jnp.concatenate([roll(corr, -(4 * r + 2)), roll(corr, -(4 * r + 66))], axis=0)
        return jnp.where(at_edge, both, 0.0)

    def scale_level(l, turn):
        for p in range(nprobe):
            turn[p * nrow : (p + 1) * nrow, :] = probes[p, l].astype(F32)
        acc = jnp.zeros((half, 128), F32)
        for r in range(nrow):
            om = turn[pl.ds(r, nprobe, stride=nrow), :]
            omega[l, r] = om.astype(BF16)
            v = om * wide(co[SPR, l, r], nprobe)
            scaled[l, r + 2] = v
            acc = put(acc, r, v)
        pack[l] = acc

    def scale_group(g, carry):
        group = [g * GROUP + i for i in range(GROUP)]
        for i, l in enumerate(group):
            scale_level(l, turn.at[i])
        send(0, g)
        return carry

    lax.fori_loop(0, nlev // GROUP, scale_group, 0)
    tell(0, next_x)
    tell(1, next_z)

    def halves(x):
        high = x.astype(BF16)
        return high, (x - high.astype(F32)).astype(BF16)

    def tangent_own(l, carry):
        above = jnp.minimum(l + 1, nlev - 1)
        below = jnp.maximum(l - 1, 0)
        acc = jnp.zeros((half, 128), F32)
        for r0 in range(0, nrow, CHUNK):
            v = scaled[l, r0 + 2 : r0 + 2 + CHUNK].reshape(CHUNK * nprobe, 128)
            cols = lax.dot_general(
                jnp.concatenate(halves(v), axis=1), ring[...], (((1,), (0,)), ((), ())), preferred_element_type=F32
            )
            for r in range(r0, r0 + CHUNK):
                at = slice((r - r0) * nprobe, (r - r0 + 1) * nprobe)
                c = [wide(co[f, l, r], nprobe) for f in range(NF)]
                t = c[CEN] * scaled[l, r + 2] + 0.2 * (scaled[above, r + 2] + scaled[below, r + 2])
                if r + 1 < nrow:
                    t = t + c[XP] * scaled[l, r + 3]
                if r >= 1:
                    t = t + c[XM] * scaled[l, r + 1]
                if r >= 2 and r + 2 < nrow:
                    t = t + c[XA] * (scaled[l, r] - scaled[l, r + 4])
                elif r >= 2:
                    t = t + c[XA] * scaled[l, r]
                else:
                    t = t - c[XA] * scaled[l, r + 4]
                t = t + c[YA] * cols[at, :128] + c[DIF] * cols[at, 128:]
                tang[l, r] = t
                if 2 <= r < nrow - 2:
                    acc = put(acc, r, t)
        strip[l] = acc
        return carry

    lax.fori_loop(0, nlev, tangent_own, 0, unroll=2)
    hear(0)
    hear(1)
    tell(2, next_y)
    tell(3, skip_z)

    def tangent_outer(l):
        e1 = edge[0, pl.ds(l, 1), :]
        ea = edge[1, pl.ds(l, 1), :]
        diff = jnp.where(quad < 2, pack_l[l], pack_r[l]) - pack[l]
        near = jnp.where(quad == 1, roll(diff, -1), roll(diff, 1))
        far = jnp.where(quad < 2, -roll(diff, -2), roll(diff, 2))
        corr = e1 * near + ea * far
        acc = strip[l] + corr
        ends = {}
        last = nrow - 1

        def coef(f, r):
            return wide(co[f, l, r], nprobe)

        rim_terms = {
            0: coef(XM, 0) * scaled[l, 1] + coef(XA, 0) * scaled[l, 0],
            1: coef(XA, 1) * scaled[l, 1],
            last - 1: -(coef(XA, last - 1) * scaled[l, nrow + 2]),
            last: coef(XP, last) * scaled[l, nrow + 2] - coef(XA, last) * scaled[l, nrow + 3],
        }
        for r in rim_terms:
            t = tang[l, r] + rim_terms[r] + take(corr, r)
            tang[l, r] = t
            ends[r] = t
            acc = put(acc, r, t)

        to_low[l, 0] = coef(XA, 0) * ends[0]
        to_low[l, 1] = coef(XM, 0) * ends[0] + coef(XA, 1) * ends[1]
        to_high[l, 0] = coef(XP, last) * ends[last] - coef(XA, last - 1) * ends[last - 1]
        to_high[l, 1] = -(coef(XA, last) * ends[last])
        u = ea * acc
        w = e1 * acc
        wrap[l] = jnp.where(quad < 2, roll(u, -2), -roll(u, 2)) + jnp.where(
            quad == 1, roll(w, -1), jnp.where(quad == 2, roll(w, 1), 0.0)
        )
        for r in range(2, nrow - 2):
            tang[l, r] = tang[l, r] + take(corr, r)

    def tangent_rims(g, carry):
        group = [g * GROUP + i for i in range(GROUP)]
        receive(0, g)
        for l in group:
            tangent_outer(l)
        send(1, g)
        return carry

    lax.fori_loop(0, nlev // GROUP, tangent_rims, 0)
    hear(2)
    hear(3)
    tell(4, next_y)

    def adjoint_own(l, carry):
        above = jnp.minimum(l + 1, nlev - 1)
        below = jnp.maximum(l - 1, 0)
        for r0 in range(0, nrow, CHUNK):
            parts = []
            for r in range(r0, r0 + CHUNK):
                w = tang[l, r]
                parts.append(
                    jnp.concatenate(
                        halves(wide(co[DIF, l, r], nprobe) * w) + halves(wide(co[YA, l, r], nprobe) * w), axis=1
                    )
                )
            cols = lax.dot_general(
                jnp.concatenate(parts, axis=0), ring_t[...], (((1,), (0,)), ((), ())), preferred_element_type=F32
            )
            for r in range(r0, r0 + CHUNK):
                b = cols[(r - r0) * nprobe : (r - r0 + 1) * nprobe]
                b = b + wide(co[CEN, l, r], nprobe) * tang[l, r] + 0.2 * (tang[above, r] + tang[below, r])
                if r + 1 < nrow:
                    b = b + wide(co[XM, l, r + 1], nprobe) * tang[l, r + 1]
                if r >= 1:
                    b = b + wide(co[XP, l, r - 1], nprobe) * tang[l, r - 1]
                if r + 2 < nrow:
                    b = b + wide(co[XA, l, r + 2], nprobe) * tang[l, r + 2]
                if r >= 2:
                    b = b - wide(co[XA, l, r - 2], nprobe) * tang[l, r - 2]
                back[l, r] = b
        return carry

    lax.fori_loop(0, nlev, adjoint_own, 0, unroll=2)
    hear(4)

    def sketch_level(l):
        corr = jnp.where(quad < 2, wrap_r[l], wrap_l[l]) - wrap[l]
        left, right = [], []
        for r in range(nrow):
            b = back[l, r] + take(corr, r)
            if r < 2:
                b = b + from_low[l, r]
            if r >= nrow - 2:
                b = b + from_high[l, r - (nrow - 2)]
            om = omega[l, r]
            sk = om.astype(F32) + wide(co[SPR, l, r], nprobe) * b
            hi = sk.astype(BF16)
            lo = (sk - hi.astype(F32)).astype(BF16)
            z = jnp.concatenate([hi, lo], axis=0)
            zbuf[l, r] = z
            right.append(z)
            left.append(jnp.concatenate([hi, om], axis=0))
        return lax.dot_general(
            jnp.concatenate(left, axis=1),
            jnp.concatenate(right, axis=1),
            (((1,), (1,)), ((), ())),
            preferred_element_type=F32,
        )

    def sketch_rims(g, gram):
        group = [g * GROUP + i for i in range(GROUP)]
        receive(1, g)
        for l in group:
            gram = gram + sketch_level(l)
        pltpu.make_async_copy(zbuf.at[some(g)], z_hbm.at[some(g)], out_sem.at[g]).start()
        return gram

    gram = lax.fori_loop(0, nlev // GROUP, sketch_rims, jnp.zeros((2 * nprobe, 2 * nprobe), F32))

    gbuf[...] = jnp.zeros(gbuf.shape, F32)
    gbuf[:, 0 : 2 * nprobe] = gram
    full = gbuf[...]
    high, probe = full[:nprobe], full[nprobe:]
    own = high + 2.0 * roll(high, -nprobe)
    both = jnp.where(wide_lane < nprobe, own, roll(probe, nprobe) + probe)
    part = jnp.where(lane16 < 64, both[:half], roll(both[half:], 64))

    pair_part = red_a
    pair_part[0] = part
    swap = pltpu.make_async_remote_copy(
        src_ref=pair_part.at[0], dst_ref=pair_part.at[1], send_sem=red_send.at[0, 0], recv_sem=red_recv.at[0, 0],
        device_id=other, device_id_type=MESH,
    )
    swap.start()
    swap.wait_recv()
    quarter = half // 2
    mine = pl.ds(pl.multiple_of(core * quarter, quarter), quarter)
    part = pair_part[0, mine] + pair_part[1, mine]

    def finish(g, carry):
        sent(0, g)
        sent(1, g)
        pltpu.make_async_copy(zbuf.at[some(g)], z_hbm.at[some(g)], out_sem.at[g]).wait()
        return carry

    pending = [swap]
    for s, (buf, count, me, reach) in enumerate(((red_b, plane, chip, in_plane), (red_c, outer, zi, in_line))):
        buf[me] = part
        stage = []
        for o, device in enumerate(reach):
            stage.append(
                pltpu.make_async_remote_copy(
                    src_ref=buf.at[me],
                    dst_ref=buf.at[me],
                    send_sem=red_send.at[s + 1, o],
                    recv_sem=red_recv.at[s + 1, o],
                    device_id=device,
                    device_id_type=MESH,
                )
            )
            stage[-1].start()
        if s == 0:
            lax.fori_loop(0, nlev // GROUP, finish, 0)
        for copy in pending:
            copy.wait_send()
        pending = stage
        for copy in reversed(stage):
            copy.wait_recv()
        terms = [buf[o] for o in range(count)]
        while len(terms) > 1:
            terms = [sum(terms[i : i + 2][1:], terms[i]) for i in range(0, len(terms), 2)]
        part = terms[0]
    total[mine] = part
    join = pltpu.make_async_remote_copy(
        src_ref=total.at[mine], dst_ref=g_hbm.at[mine], send_sem=red_send.at[0, 1], recv_sem=red_recv.at[0, 1],
        device_id=other, device_id_type=MESH,
    )
    join.start()
    keep = pltpu.make_async_copy(total.at[mine], g_hbm.at[mine], in_sem.at[0])
    keep.start()
    for copy in pending:
        copy.wait_send()
    keep.wait()
    join.wait_send()
    join.wait_recv()


def basis_kernel(nprobe, nlev, nrow, scale, g_hbm, z_hbm, basis_hbm, factor_hbm, gbuf, zbuf, obuf, fbuf, in_sem, out_sem):
    def load(l):
        return pltpu.make_async_copy(z_hbm.at[l], zbuf.at[l], in_sem.at[l])

    def store(l):
        return pltpu.make_async_copy(obuf.at[l], basis_hbm.at[:, l], out_sem.at[l])

    sums = pltpu.make_async_copy(g_hbm, gbuf, in_sem.at[nlev])
    sums.start()
    for l in range(nlev):
        load(l).start()
    half = nprobe // 2
    sums.wait()
    g = gbuf[...]
    both = jnp.concatenate([g, roll(g, 64)], axis=0)
    flip = both.T
    lane = lanes((nprobe, 128))
    sub = lax.broadcasted_iota(jnp.int32, (nprobe, 128), 0)
    pad = jnp.zeros((nprobe, 128 - nprobe), F32)
    flip_g = jnp.concatenate([flip[:nprobe], pad], axis=1)
    flip_c = jnp.concatenate([flip[nprobe : 2 * nprobe], pad], axis=1)
    sym_g = 0.5 * (both + flip_g)
    sym_c = 0.5 * (roll(both, -nprobe) + flip_c)
    m = jnp.where(lane < nprobe, sym_g, jnp.where(jnp.logical_and(lane >= 64, lane < 64 + nprobe), roll(sym_c, 64), 0.0))
    m = jnp.where(jnp.logical_or(lane == sub + nprobe, lane == sub + 64 + nprobe), 1.0, m)
    first = lane < 64
    piv = jnp.ones((nprobe, 128), F32)
    for k0 in range(0, nprobe, WIDTH):
        cols = [
            jnp.where(
                first,
                jnp.broadcast_to(m[:, k : k + 1], (nprobe, 128)),
                jnp.broadcast_to(m[:, 64 + k : 65 + k], (nprobe, 128)),
            )
            for k in range(k0, k0 + WIDTH)
        ]
        for j in range(WIDTH):
            k = k0 + j
            p = cols[j][k : k + 1]
            inv = 1.0 / p
            piv = jnp.where(sub == k, p, piv)
            below = jnp.where(sub > k, cols[j], 0.0)
            for i in range(j + 1, WIDTH):
                cols[i] = cols[i] - below * (cols[i][k : k + 1] * inv)
            m = m - below * (m[k : k + 1] * inv)
    m = m * (1.0 / jnp.sqrt(piv))
    upper = jnp.where(jnp.logical_and(lane >= sub, lane < nprobe), m, 0.0)
    inv_g = jnp.where(lane <= sub, roll(m, -nprobe), 0.0)
    inv_c = jnp.where(lane <= sub, roll(m, -(64 + nprobe)), 0.0)
    factor = lax.dot_general(
        upper, inv_c, (((1,), (1,)), ((), ())), precision=lax.Precision.HIGHEST, preferred_element_type=F32
    )
    fbuf[...] = factor
    leave = pltpu.make_async_copy(fbuf, factor_hbm, out_sem.at[nlev])
    leave.start()
    a = inv_g * scale
    a_hi = a.astype(BF16)
    a_lo = (a - a_hi.astype(F32)).astype(BF16)
    twice = jnp.where(lane < nprobe, a_hi.astype(F32), roll(a_hi.astype(F32), nprobe))
    twice_lo = jnp.where(lane < nprobe, a_lo.astype(F32), roll(a_lo.astype(F32), nprobe))
    lhs = jnp.concatenate([twice, twice_lo], axis=0).astype(BF16)[:, : 2 * nprobe]

    def level(l, carry):
        load(l).wait()
        for r in range(0, nrow, 2):
            out = lax.dot_general(
                lhs,
                jnp.concatenate([zbuf[l, r], zbuf[l, r + 1]], axis=1),
                (((1,), (0,)), ((), ())),
                preferred_element_type=F32,
            )
            out = out[:nprobe] + out[nprobe:]
            put_row(obuf.at[l], r, out[:, :128])
            put_row(obuf.at[l], r + 1, out[:, 128:])
        store(l).start()
        return carry

    lax.fori_loop(0, nlev, level, 0)

    def finish(l, carry):
        store(l).wait()
        return carry

    lax.fori_loop(0, nlev, finish, 0)
    leave.wait()


def shards(probes, spread, adv_x, adv_y, diffusivity):
    nprobe, nlev, nrow, ncol = probes.shape
    nrd = lax.axis_size("row")
    ncd = lax.axis_size("col")
    half = nprobe // 2
    inputs = [pltpu.with_memory_space_constraint(x, pltpu.HBM) for x in (probes, spread, adv_x, adv_y, diffusivity)]
    any_spec = pl.BlockSpec(memory_space=pl.ANY)
    rows2 = pltpu.VMEM((nlev, 2, nprobe, ncol), F32)
    strip = pltpu.VMEM((nlev, half, ncol), F32)
    plane = (nrd // 2) * INNER
    most = max(2, plane, ncd // INNER)
    z, g = pl.pallas_call(
        functools.partial(halo_kernel, (nprobe, nlev, nrow, nrd, ncd)),
        out_shape=(
            jax.ShapeDtypeStruct((nlev, nrow, 2 * nprobe, ncol), BF16),
            jax.ShapeDtypeStruct((half, ncol), F32),
        ),
        in_specs=[any_spec] * 5,
        out_specs=(any_spec, any_spec),
        scratch_shapes=[
            pltpu.VMEM((nprobe, nlev, nrow, ncol), BF16),
            pltpu.VMEM((4, nlev, nrow, ncol), F32),
            pltpu.VMEM((GROUP, nprobe * nrow, ncol), F32),
            pltpu.VMEM((nlev, nrow, nprobe, ncol), BF16),
            pltpu.VMEM((nlev, nrow + 4, nprobe, ncol), F32),
            pltpu.VMEM((nlev, nrow, nprobe, ncol), F32),
            pltpu.VMEM((NF, nlev, nrow, 8, ncol), F32),
            pltpu.VMEM((2, nlev, ncol), F32),
            pltpu.VMEM((256, 256), BF16),
            pltpu.VMEM((512, 128), BF16),
            strip, strip, strip, strip, strip, strip,
            rows2, rows2, rows2, rows2,
            pltpu.VMEM((nlev, nrow, nprobe, ncol), F32),
            strip,
            pltpu.VMEM((nlev, nrow, 2 * nprobe, ncol), BF16),
            pltpu.VMEM((2 * nprobe, ncol), F32),
            pltpu.VMEM((2, half, ncol), F32),
            pltpu.VMEM((plane, half // 2, ncol), F32),
            pltpu.VMEM((ncd // INNER, half // 2, ncol), F32),
            pltpu.VMEM((half, ncol), F32),
            pltpu.SemaphoreType.DMA((5,)),
            pltpu.SemaphoreType.DMA((nlev // GROUP,)),
            pltpu.SemaphoreType.DMA((2, 4, nlev // GROUP)),
            pltpu.SemaphoreType.DMA((2, 4, nlev // GROUP)),
            pltpu.SemaphoreType.DMA((3, most)),
            pltpu.SemaphoreType.DMA((3, most)),
            pltpu.SemaphoreType.REGULAR((5,)),
        ],
        compiler_params=pltpu.CompilerParams(
            collective_id=0, has_side_effects=True, vmem_limit_bytes=40 * 1024 * 1024
        ),
        name="sketch_and_sums",
    )(*inputs)
    scale = float(nlev * nrow * ncol * nrd * ncd) ** 0.5
    basis, factor = pl.pallas_call(
        functools.partial(basis_kernel, nprobe, nlev, nrow, scale),
        out_shape=(
            jax.ShapeDtypeStruct((nprobe, nlev, nrow, ncol), F32),
            jax.ShapeDtypeStruct((nprobe, nprobe), F32),
        ),
        in_specs=[any_spec, any_spec],
        out_specs=(any_spec, any_spec),
        scratch_shapes=[
            pltpu.VMEM((half, ncol), F32),
            pltpu.VMEM((nlev, nrow, 2 * nprobe, ncol), BF16),
            pltpu.VMEM((nlev, nprobe, nrow, ncol), F32),
            pltpu.VMEM((nprobe, nprobe), F32),
            pltpu.SemaphoreType.DMA((nlev + 1,)),
            pltpu.SemaphoreType.DMA((nlev + 1,)),
        ],
        compiler_params=pltpu.CompilerParams(vmem_limit_bytes=24 * 1024 * 1024),
        name="factors_and_basis",
    )(g, z)
    return basis, factor


def solution(mesh):
    return jax.shard_map(
        shards,
        mesh=mesh,
        in_specs=(
            P(None, None, "row", "col"),
            P(None, "row", "col"),
            P(None, "row", "col"),
            P(None, "row", "col"),
            P(None, "row", "col"),
        ),
        out_specs=(P(None, None, "row", "col"), P()),
        check_vma=False,
    )
```

```python
import functools

import jax
import jax.numpy as jnp
from jax import lax
from jax.experimental import pallas as pl
from jax.experimental.pallas import tpu as pltpu
from jax.sharding import PartitionSpec as P

MESH = pl.DeviceIdType.MESH
F32 = jnp.float32
BF16 = jnp.bfloat16
INNER = 4
WIDTH = 8
CHUNK = 8
GROUP = 2
NF = 7
SPR, CEN, XP, XM, XA, YA, DIF = range(NF)
LOW, HIGH, LEFT, RIGHT = range(4)


def lanes(shape):
    return lax.broadcasted_iota(jnp.int32, shape, 1)


def roll(x, shift):
    return pltpu.roll(x, shift % 128, 1)


def put_row(ref, r, value):
    n, rows, width = ref.shape
    ref.reshape(n * rows, width)[pl.ds(r, n, stride=rows), :] = value


def wide(coef, nprobe):
    return jnp.broadcast_to(coef[None], (nprobe // 8, 8, 128)).reshape(nprobe, 128)


def halo_kernel(
    dims,
    probes_hbm, spread_hbm, advx_hbm, advy_hbm, diff_hbm,
    z_hbm, g_hbm,
    probes, coefs, turn, omega, scaled, tang, co, edge, ring, ring_t,
    pack, pack_l, pack_r, wrap, wrap_l, wrap_r,
    to_low, to_high, from_low, from_high,
    back, strip, zbuf, gbuf, red_a, red_b, red_c, total,
    in_sem, out_sem, send_sem, recv_sem, red_send, red_recv, news,
):
    nprobe, nlev, nrow, nrd, ncd = dims
    outer = ncd // INNER
    row = lax.axis_index("row")
    col = lax.axis_index("col")
    zi = col // INNER
    xi = lax.rem(col, INNER)
    half = nprobe // 2

    core = lax.rem(row, 2)
    chip = (row // 2) * INNER + xi
    plane = (nrd // 2) * INNER

    def far(o, count):
        return min(o, count - o)

    yi = row // 2
    tall = nrd // 2
    steps = [(dy, dx) for dy in range(tall) for dx in range(INNER)][1:]
    steps.sort(key=lambda st: -(far(st[0], tall) + far(st[1], INNER)))
    in_plane = [
        (lax.rem(yi + dy, tall) * 2 + core, zi * INNER + lax.rem(xi + dx, INNER)) for dy, dx in steps
    ]
    in_line = [
        (row, lax.rem(zi + o, outer) * INNER + xi) for o in sorted(range(1, outer), key=lambda o: -far(o, outer))
    ]
    other = (row + 1 - 2 * core, col)
    barrier = pltpu.get_barrier_semaphore()
    greet = [(row, lax.rem(col + o, ncd)) for o in (1, ncd - 1)]
    greet += [(lax.rem(row + o, nrd), col) for o in (1, nrd - 1)]
    next_x = [(row, zi * INNER + lax.rem(xi + o, INNER)) for o in (1, INNER - 1)]
    next_y = [(lax.rem(yi + o, tall) * 2 + core, col) for o in (1, tall - 1)]
    next_z = [(row, lax.rem(zi + o, outer) * INNER + xi) for o in (1, outer - 1)]
    skip_z = [(row, lax.rem(zi + o, outer) * INNER + xi) for o in (2, outer - 2)]
    greet += next_z + next_y + next_x + [other]
    for device in greet:
        pl.semaphore_signal(barrier, inc=1, device_id=device, device_id_type=MESH)
    signals = len(greet)

    loads = []
    for i, src in enumerate((spread_hbm, advx_hbm, advy_hbm, diff_hbm)):
        loads.append(pltpu.make_async_copy(src, coefs.at[i], in_sem.at[i]))

    gbuf[...] = jnp.zeros(gbuf.shape, F32)

    def probe_load(g):
        at = pl.ds(g * GROUP, GROUP)
        return pltpu.make_async_copy(probes_hbm.at[:, at], probes.at[:, at], in_sem.at[4 + g])

    for g in range(nlev // GROUP):
        loads.append(probe_load(g))
    for load in loads:
        load.start()

    def tell(n, devices):
        for device in devices:
            pl.semaphore_signal(news.at[n], inc=1, device_id=device, device_id_type=MESH)

    def hear(n):
        pl.semaphore_wait(news.at[n], 2)


    for load in loads[:4]:
        load.wait()

    def spread_coefs(l, carry):
        ax = coefs[1, l] * (1.0 / 12.0)
        ay = coefs[2, l] * (1.0 / 12.0)
        d = coefs[3, l]
        fields = (coefs[0, l], 0.6 - 4.0 * d, d + 8.0 * ax, d - 8.0 * ax, ax, ay, d)
        for f in range(NF):
            for r in range(nrow):
                co[f, l, r] = jnp.broadcast_to(fields[f][r : r + 1], (8, 128))
        return carry

    lax.fori_loop(0, nlev, spread_coefs, 0)

    lane16 = lanes((half, 128))
    quad = lax.rem(lane16, 4)
    lane_l = lanes((nlev, 128))
    quad_l = lax.rem(lane_l, 4)

    def packed(field):
        acc = jnp.zeros((nlev, 128), F32)
        for r in range(nrow):
            acc = jnp.where(lax.div(lane_l, 4) == r, roll(coefs[field, :, r, :], 4 * r + 2), acc)
        return jnp.where(lane_l < 64, acc, roll(acc, 64))

    pa = packed(2) * (1.0 / 12.0)
    pd = packed(3)
    near_edge = jnp.where(quad_l == 1, pd + 8.0 * pa, jnp.where(quad_l == 2, pd - 8.0 * pa, 0.0))
    for l in range(nlev):
        edge[0, l] = jnp.broadcast_to(near_edge[l : l + 1], (8, 128))
        edge[1, l] = jnp.broadcast_to(pa[l : l + 1], (8, 128))

    for k, shape in enumerate(((256, 256), (512, 128))):
        src_lane = lax.rem(lax.broadcasted_iota(jnp.int32, shape, 0), 128)
        src_part = lax.div(lax.broadcasted_iota(jnp.int32, shape, 0), 128)
        out_col = lax.broadcasted_iota(jnp.int32, shape, 1)
        step = lax.rem(src_lane - lax.rem(out_col, 128) + 128, 128)
        first = jnp.where(step == 1, 8.0, jnp.where(step == 127, -8.0, jnp.where(step == 2, -1.0, jnp.where(step == 126, 1.0, 0.0))))
        both = jnp.where(jnp.logical_or(step == 1, step == 127), 1.0, 0.0)
        if k == 0:
            ring[...] = jnp.where(out_col < 128, first, both).astype(BF16)
        else:
            ring_t[...] = jnp.where(src_part < 2, both, -first).astype(BF16)

    has = {LOW: row > 0, HIGH: row < nrd - 1, LEFT: col > 0, RIGHT: col < ncd - 1}
    target = {
        LOW: (lax.rem(row + nrd - 1, nrd), col),
        HIGH: (lax.rem(row + 1, nrd), col),
        LEFT: (row, lax.rem(col + ncd - 1, ncd)),
        RIGHT: (row, lax.rem(col + 1, ncd)),
    }
    def some(g):
        return pl.ds(g * GROUP, GROUP)

    rims = (
        {
            LOW: (lambda g: scaled.at[some(g), 2:4], lambda g: scaled.at[some(g), nrow + 2 : nrow + 4]),
            HIGH: (lambda g: scaled.at[some(g), nrow : nrow + 2], lambda g: scaled.at[some(g), 0:2]),
            LEFT: (lambda g: pack.at[some(g)], lambda g: pack_r.at[some(g)]),
            RIGHT: (lambda g: pack.at[some(g)], lambda g: pack_l.at[some(g)]),
        },
        {
            LOW: (lambda g: to_low.at[some(g)], lambda g: from_high.at[some(g)]),
            HIGH: (lambda g: to_high.at[some(g)], lambda g: from_low.at[some(g)]),
            LEFT: (lambda g: wrap.at[some(g)], lambda g: wrap_r.at[some(g)]),
            RIGHT: (lambda g: wrap.at[some(g)], lambda g: wrap_l.at[some(g)]),
        },
    )
    opposite = {LOW: HIGH, HIGH: LOW, LEFT: RIGHT, RIGHT: LEFT}

    def rim(phase, side, g):
        src, dst = rims[phase][side]
        return pltpu.make_async_remote_copy(
            src_ref=src(g),
            dst_ref=dst(g),
            send_sem=send_sem.at[phase, side, g],
            recv_sem=recv_sem.at[phase, side, g],
            device_id=target[side],
            device_id_type=MESH,
        )

    def send(phase, g):
        for side in (LEFT, RIGHT, LOW, HIGH):
            @pl.when(has[side])
            def _():
                rim(phase, side, g).start()

    def receive(phase, g):
        for side in (LEFT, RIGHT, LOW, HIGH):
            @pl.when(has[side])
            def _():
                rim(phase, opposite[side], g).wait_recv()

    def sent(phase, g):
        for side in (LOW, HIGH, LEFT, RIGHT):
            @pl.when(has[side])
            def _():
                rim(phase, side, g).wait_send()

    zero_rows = jnp.zeros((nlev, 2, nprobe, 128), F32)
    zero_pack = jnp.zeros((nlev, half, 128), F32)

    @pl.when(row == 0)
    def _():
        scaled[:, 0:2] = zero_rows
        from_low[...] = zero_rows

    @pl.when(row == nrd - 1)
    def _():
        scaled[:, nrow + 2 : nrow + 4] = zero_rows
        from_high[...] = zero_rows

    @pl.when(col == 0)
    def _():
        pack_l[...] = zero_pack
        wrap_l[...] = zero_pack

    @pl.when(col == ncd - 1)
    def _():
        pack_r[...] = zero_pack
        wrap_r[...] = zero_pack


    def put(acc, r, value):
        slot = lax.div(lane16, 4)
        acc = jnp.where(slot == r, roll(value[:half], 4 * r + 2), acc)
        return jnp.where(slot == r + 16, roll(value[half:], 4 * r + 66), acc)

    wide_lane = lanes((nprobe, 128))
    at_edge = jnp.logical_or(wide_lane < 2, wide_lane >= 126)

    def take(corr, r):
        both = jnp.concatenate([roll(corr, -(4 * r + 2)), roll(corr, -(4 * r + 66))], axis=0)
        return jnp.where(at_edge, both, 0.0)

    def scale_level(l, turn):
        for p in range(nprobe):
            turn[p * nrow : (p + 1) * nrow, :] = probes[p, l].astype(F32)
        acc = jnp.zeros((half, 128), F32)
        for r in range(nrow):
            om = turn[pl.ds(r, nprobe, stride=nrow), :]
            omega[l, r] = om.astype(BF16)
            v = om * wide(co[SPR, l, r], nprobe)
            scaled[l, r + 2] = v
            acc = put(acc, r, v)
        pack[l] = acc

    def scale_group(g):
        probe_load(g).wait()
        for i in range(GROUP):
            scale_level(g * GROUP + i, turn.at[i])

    scale_group(0)
    pl.semaphore_wait(barrier, signals)
    send(0, 0)

    def scale_next(g, carry):
        scale_group(g)
        send(0, g)
        return carry

    lax.fori_loop(1, nlev // GROUP, scale_next, 0)
    tell(0, next_x)
    tell(1, next_z)

    def halves(x):
        high = x.astype(BF16)
        return high, (x - high.astype(F32)).astype(BF16)

    def tangent_own(l, carry):
        above = jnp.minimum(l + 1, nlev - 1)
        below = jnp.maximum(l - 1, 0)
        acc = jnp.zeros((half, 128), F32)
        for r0 in range(0, nrow, CHUNK):
            v = scaled[l, r0 + 2 : r0 + 2 + CHUNK].reshape(CHUNK * nprobe, 128)
            cols = lax.dot_general(
                jnp.concatenate(halves(v), axis=1), ring[...], (((1,), (0,)), ((), ())), preferred_element_type=F32
            )
            for r in range(r0, r0 + CHUNK):
                at = slice((r - r0) * nprobe, (r - r0 + 1) * nprobe)
                c = [wide(co[f, l, r], nprobe) for f in range(NF)]
                t = c[CEN] * scaled[l, r + 2] + 0.2 * (scaled[above, r + 2] + scaled[below, r + 2])
                if r + 1 < nrow:
                    t = t + c[XP] * scaled[l, r + 3]
                if r >= 1:
                    t = t + c[XM] * scaled[l, r + 1]
                if r >= 2 and r + 2 < nrow:
                    t = t + c[XA] * (scaled[l, r] - scaled[l, r + 4])
                elif r >= 2:
                    t = t + c[XA] * scaled[l, r]
                else:
                    t = t - c[XA] * scaled[l, r + 4]
                t = t + c[YA] * cols[at, :128] + c[DIF] * cols[at, 128:]
                tang[l, r] = t
                if 2 <= r < nrow - 2:
                    acc = put(acc, r, t)
        strip[l] = acc
        return carry

    lax.fori_loop(0, nlev, tangent_own, 0, unroll=2)
    hear(0)
    hear(1)
    tell(2, next_y)
    tell(3, skip_z)

    def tangent_outer(l):
        e1 = wide(edge[0, l], half)
        ea = wide(edge[1, l], half)
        diff = jnp.where(quad < 2, pack_l[l], pack_r[l]) - pack[l]
        near = jnp.where(quad == 1, roll(diff, -1), roll(diff, 1))
        far = jnp.where(quad < 2, -roll(diff, -2), roll(diff, 2))
        corr = e1 * near + ea * far
        acc = strip[l] + corr
        ends = {}
        last = nrow - 1

        def coef(f, r):
            return wide(co[f, l, r], nprobe)

        rim_terms = {
            0: coef(XM, 0) * scaled[l, 1] + coef(XA, 0) * scaled[l, 0],
            1: coef(XA, 1) * scaled[l, 1],
            last - 1: -(coef(XA, last - 1) * scaled[l, nrow + 2]),
            last: coef(XP, last) * scaled[l, nrow + 2] - coef(XA, last) * scaled[l, nrow + 3],
        }
        for r in rim_terms:
            t = tang[l, r] + rim_terms[r] + take(corr, r)
            tang[l, r] = t
            ends[r] = t
            acc = put(acc, r, t)

        to_low[l, 0] = coef(XA, 0) * ends[0]
        to_low[l, 1] = coef(XM, 0) * ends[0] + coef(XA, 1) * ends[1]
        to_high[l, 0] = coef(XP, last) * ends[last] - coef(XA, last - 1) * ends[last - 1]
        to_high[l, 1] = -(coef(XA, last) * ends[last])
        u = ea * acc
        w = e1 * acc
        wrap[l] = jnp.where(quad < 2, roll(u, -2), -roll(u, 2)) + jnp.where(
            quad == 1, roll(w, -1), jnp.where(quad == 2, roll(w, 1), 0.0)
        )
        for r in range(2, nrow - 2):
            tang[l, r] = tang[l, r] + take(corr, r)

    def tangent_rims(g, carry):
        group = [g * GROUP + i for i in range(GROUP)]
        receive(0, g)
        for l in group:
            tangent_outer(l)
        send(1, g)
        return carry

    lax.fori_loop(0, nlev // GROUP, tangent_rims, 0)
    hear(2)
    hear(3)
    tell(4, next_y)

    def adjoint_own(l, carry):
        above = jnp.minimum(l + 1, nlev - 1)
        below = jnp.maximum(l - 1, 0)
        for r0 in range(0, nrow, CHUNK):
            parts = []
            for r in range(r0, r0 + CHUNK):
                w = tang[l, r]
                parts.append(
                    jnp.concatenate(
                        halves(wide(co[DIF, l, r], nprobe) * w) + halves(wide(co[YA, l, r], nprobe) * w), axis=1
                    )
                )
            cols = lax.dot_general(
                jnp.concatenate(parts, axis=0), ring_t[...], (((1,), (0,)), ((), ())), preferred_element_type=F32
            )
            for r in range(r0, r0 + CHUNK):
                b = cols[(r - r0) * nprobe : (r - r0 + 1) * nprobe]
                b = b + wide(co[CEN, l, r], nprobe) * tang[l, r] + 0.2 * (tang[above, r] + tang[below, r])
                if r + 1 < nrow:
                    b = b + wide(co[XM, l, r + 1], nprobe) * tang[l, r + 1]
                if r >= 1:
                    b = b + wide(co[XP, l, r - 1], nprobe) * tang[l, r - 1]
                if r + 2 < nrow:
                    b = b + wide(co[XA, l, r + 2], nprobe) * tang[l, r + 2]
                if r >= 2:
                    b = b - wide(co[XA, l, r - 2], nprobe) * tang[l, r - 2]
                back[l, r] = b
        return carry

    lax.fori_loop(0, nlev, adjoint_own, 0, unroll=2)
    hear(4)

    def sketch_level(l):
        corr = jnp.where(quad < 2, wrap_r[l], wrap_l[l]) - wrap[l]
        left, right = [], []
        for r in range(nrow):
            b = back[l, r] + take(corr, r)
            if r < 2:
                b = b + from_low[l, r]
            if r >= nrow - 2:
                b = b + from_high[l, r - (nrow - 2)]
            om = omega[l, r]
            sk = om.astype(F32) + wide(co[SPR, l, r], nprobe) * b
            hi = sk.astype(BF16)
            lo = (sk - hi.astype(F32)).astype(BF16)
            z = jnp.concatenate([hi, lo], axis=0)
            zbuf[l, r] = z
            right.append(z)
            left.append(jnp.concatenate([hi, om], axis=0))
        return lax.dot_general(
            jnp.concatenate(left, axis=1),
            jnp.concatenate(right, axis=1),
            (((1,), (1,)), ((), ())),
            preferred_element_type=F32,
        )

    def sketch_rims(g, gram):
        group = [g * GROUP + i for i in range(GROUP)]
        receive(1, g)
        for l in group:
            gram = gram + sketch_level(l)
        pltpu.make_async_copy(zbuf.at[some(g)], z_hbm.at[some(g)], out_sem.at[g]).start()
        return gram

    gram = lax.fori_loop(0, nlev // GROUP, sketch_rims, jnp.zeros((2 * nprobe, 2 * nprobe), F32))

    gbuf[:, 0 : 2 * nprobe] = gram
    full = gbuf[...]
    high, probe = full[:nprobe], full[nprobe:]
    own = high + 2.0 * roll(high, -nprobe)
    both = jnp.where(wide_lane < nprobe, own, roll(probe, nprobe) + probe)
    part = jnp.where(lane16 < 64, both[:half], roll(both[half:], 64))

    pair_part = red_a
    pair_part[0] = part
    swap = pltpu.make_async_remote_copy(
        src_ref=pair_part.at[0], dst_ref=pair_part.at[1], send_sem=red_send.at[0, 0], recv_sem=red_recv.at[0, 0],
        device_id=other, device_id_type=MESH,
    )
    swap.start()
    swap.wait_recv()
    quarter = half // 2
    mine = pl.ds(pl.multiple_of(core * quarter, quarter), quarter)
    part = pair_part[0, mine] + pair_part[1, mine]

    def finish(g, carry):
        sent(0, g)
        sent(1, g)
        pltpu.make_async_copy(zbuf.at[some(g)], z_hbm.at[some(g)], out_sem.at[g]).wait()
        return carry

    pending = [swap]
    for s, (buf, count, me, reach) in enumerate(((red_c, outer, zi, in_line), (red_b, plane, chip, in_plane))):
        buf[me] = part
        stage = []
        for o, device in enumerate(reach):
            stage.append(
                pltpu.make_async_remote_copy(
                    src_ref=buf.at[me],
                    dst_ref=buf.at[me],
                    send_sem=red_send.at[s + 1, o],
                    recv_sem=red_recv.at[s + 1, o],
                    device_id=device,
                    device_id_type=MESH,
                )
            )
            stage[-1].start()
        if s == 0:
            lax.fori_loop(0, nlev // GROUP, finish, 0)
        for copy in pending:
            copy.wait_send()
        pending = stage
        for copy in reversed(stage):
            copy.wait_recv()
        terms = [buf[o] for o in range(count)]
        while len(terms) > 1:
            terms = [sum(terms[i : i + 2][1:], terms[i]) for i in range(0, len(terms), 2)]
        part = terms[0]
    total[mine] = part
    join = pltpu.make_async_remote_copy(
        src_ref=total.at[mine], dst_ref=g_hbm.at[mine], send_sem=red_send.at[0, 1], recv_sem=red_recv.at[0, 1],
        device_id=other, device_id_type=MESH,
    )
    join.start()
    keep = pltpu.make_async_copy(total.at[mine], g_hbm.at[mine], in_sem.at[0])
    keep.start()
    for copy in pending:
        copy.wait_send()
    keep.wait()
    join.wait_send()
    join.wait_recv()


def basis_kernel(nprobe, nlev, nrow, scale, g_hbm, z_hbm, basis_hbm, factor_hbm, gbuf, zbuf, obuf, fbuf, in_sem, out_sem):
    def load(l):
        return pltpu.make_async_copy(z_hbm.at[l], zbuf.at[l], in_sem.at[l])

    def store(l):
        return pltpu.make_async_copy(obuf.at[l], basis_hbm.at[:, l], out_sem.at[l])

    sums = pltpu.make_async_copy(g_hbm, gbuf, in_sem.at[nlev])
    sums.start()
    for l in range(nlev):
        load(l).start()
    half = nprobe // 2
    sums.wait()
    g = gbuf[...]
    both = jnp.concatenate([g, roll(g, 64)], axis=0)
    flip = both.T
    lane = lanes((nprobe, 128))
    sub = lax.broadcasted_iota(jnp.int32, (nprobe, 128), 0)
    pad = jnp.zeros((nprobe, 128 - nprobe), F32)
    flip_g = jnp.concatenate([flip[:nprobe], pad], axis=1)
    flip_c = jnp.concatenate([flip[nprobe : 2 * nprobe], pad], axis=1)
    sym_g = 0.5 * (both + flip_g)
    sym_c = 0.5 * (roll(both, -nprobe) + flip_c)
    m = jnp.where(lane < nprobe, sym_g, jnp.where(jnp.logical_and(lane >= 64, lane < 64 + nprobe), roll(sym_c, 64), 0.0))
    m = jnp.where(jnp.logical_or(lane == sub + nprobe, lane == sub + 64 + nprobe), 1.0, m)
    first = lane < 64
    piv = jnp.ones((nprobe, 128), F32)
    for k0 in range(0, nprobe, WIDTH):
        cols = [
            jnp.where(
                first,
                jnp.broadcast_to(m[:, k : k + 1], (nprobe, 128)),
                jnp.broadcast_to(m[:, 64 + k : 65 + k], (nprobe, 128)),
            )
            for k in range(k0, k0 + WIDTH)
        ]
        for j in range(WIDTH):
            k = k0 + j
            p = cols[j][k : k + 1]
            inv = 1.0 / p
            piv = jnp.where(sub == k, p, piv)
            below = jnp.where(sub > k, cols[j], 0.0)
            for i in range(j + 1, WIDTH):
                cols[i] = cols[i] - below * (cols[i][k : k + 1] * inv)
            m = m - below * (m[k : k + 1] * inv)
    m = m * (1.0 / jnp.sqrt(piv))
    upper = jnp.where(jnp.logical_and(lane >= sub, lane < nprobe), m, 0.0)
    inv_g = jnp.where(lane <= sub, roll(m, -nprobe), 0.0)
    inv_c = jnp.where(lane <= sub, roll(m, -(64 + nprobe)), 0.0)
    factor = lax.dot_general(
        upper, inv_c, (((1,), (1,)), ((), ())), precision=lax.Precision.HIGHEST, preferred_element_type=F32
    )
    fbuf[...] = factor
    leave = pltpu.make_async_copy(fbuf, factor_hbm, out_sem.at[nlev])
    leave.start()
    a = inv_g * scale
    a_hi = a.astype(BF16)
    a_lo = (a - a_hi.astype(F32)).astype(BF16)
    twice = jnp.where(lane < nprobe, a_hi.astype(F32), roll(a_hi.astype(F32), nprobe))
    twice_lo = jnp.where(lane < nprobe, a_lo.astype(F32), roll(a_lo.astype(F32), nprobe))
    lhs = jnp.concatenate([twice, twice_lo], axis=0).astype(BF16)[:, : 2 * nprobe]

    def level(l, carry):
        load(l).wait()
        for r in range(0, nrow, 2):
            out = lax.dot_general(
                lhs,
                jnp.concatenate([zbuf[l, r], zbuf[l, r + 1]], axis=1),
                (((1,), (0,)), ((), ())),
                preferred_element_type=F32,
            )
            out = out[:nprobe] + out[nprobe:]
            put_row(obuf.at[l], r, out[:, :128])
            put_row(obuf.at[l], r + 1, out[:, 128:])
        store(l).start()
        return carry

    lax.fori_loop(0, nlev, level, 0)

    def finish(l, carry):
        store(l).wait()
        return carry

    lax.fori_loop(0, nlev, finish, 0)
    leave.wait()


def shards(probes, spread, adv_x, adv_y, diffusivity):
    nprobe, nlev, nrow, ncol = probes.shape
    nrd = lax.axis_size("row")
    ncd = lax.axis_size("col")
    half = nprobe // 2
    inputs = [pltpu.with_memory_space_constraint(x, pltpu.HBM) for x in (probes, spread, adv_x, adv_y, diffusivity)]
    any_spec = pl.BlockSpec(memory_space=pl.ANY)
    rows2 = pltpu.VMEM((nlev, 2, nprobe, ncol), F32)
    strip = pltpu.VMEM((nlev, half, ncol), F32)
    plane = (nrd // 2) * INNER
    most = max(2, plane, ncd // INNER)
    z, g = pl.pallas_call(
        functools.partial(halo_kernel, (nprobe, nlev, nrow, nrd, ncd)),
        out_shape=(
            jax.ShapeDtypeStruct((nlev, nrow, 2 * nprobe, ncol), BF16),
            jax.ShapeDtypeStruct((half, ncol), F32),
        ),
        in_specs=[any_spec] * 5,
        out_specs=(any_spec, any_spec),
        scratch_shapes=[
            pltpu.VMEM((nprobe, nlev, nrow, ncol), BF16),
            pltpu.VMEM((4, nlev, nrow, ncol), F32),
            pltpu.VMEM((GROUP, nprobe * nrow, ncol), F32),
            pltpu.VMEM((nlev, nrow, nprobe, ncol), BF16),
            pltpu.VMEM((nlev, nrow + 4, nprobe, ncol), F32),
            pltpu.VMEM((nlev, nrow, nprobe, ncol), F32),
            pltpu.VMEM((NF, nlev, nrow, 8, ncol), F32),
            pltpu.VMEM((2, nlev, 8, ncol), F32),
            pltpu.VMEM((256, 256), BF16),
            pltpu.VMEM((512, 128), BF16),
            strip, strip, strip, strip, strip, strip,
            rows2, rows2, rows2, rows2,
            pltpu.VMEM((nlev, nrow, nprobe, ncol), F32),
            strip,
            pltpu.VMEM((nlev, nrow, 2 * nprobe, ncol), BF16),
            pltpu.VMEM((2 * nprobe, ncol), F32),
            pltpu.VMEM((2, half, ncol), F32),
            pltpu.VMEM((plane, half // 2, ncol), F32),
            pltpu.VMEM((ncd // INNER, half // 2, ncol), F32),
            pltpu.VMEM((half, ncol), F32),
            pltpu.SemaphoreType.DMA((4 + nlev // GROUP,)),
            pltpu.SemaphoreType.DMA((nlev // GROUP,)),
            pltpu.SemaphoreType.DMA((2, 4, nlev // GROUP)),
            pltpu.SemaphoreType.DMA((2, 4, nlev // GROUP)),
            pltpu.SemaphoreType.DMA((3, most)),
            pltpu.SemaphoreType.DMA((3, most)),
            pltpu.SemaphoreType.REGULAR((5,)),
        ],
        compiler_params=pltpu.CompilerParams(
            collective_id=0, has_side_effects=True, vmem_limit_bytes=40 * 1024 * 1024
        ),
        name="sketch_and_sums",
    )(*inputs)
    scale = float(nlev * nrow * ncol * nrd * ncd) ** 0.5
    basis, factor = pl.pallas_call(
        functools.partial(basis_kernel, nprobe, nlev, nrow, scale),
        out_shape=(
            jax.ShapeDtypeStruct((nprobe, nlev, nrow, ncol), F32),
            jax.ShapeDtypeStruct((nprobe, nprobe), F32),
        ),
        in_specs=[any_spec, any_spec],
        out_specs=(any_spec, any_spec),
        scratch_shapes=[
            pltpu.VMEM((half, ncol), F32),
            pltpu.VMEM((nlev, nrow, 2 * nprobe, ncol), BF16),
            pltpu.VMEM((nlev, nprobe, nrow, ncol), F32),
            pltpu.VMEM((nprobe, nprobe), F32),
            pltpu.SemaphoreType.DMA((nlev + 1,)),
            pltpu.SemaphoreType.DMA((nlev + 1,)),
        ],
        compiler_params=pltpu.CompilerParams(vmem_limit_bytes=24 * 1024 * 1024),
        name="factors_and_basis",
    )(g, z)
    return basis, factor


def solution(mesh):
    return jax.shard_map(
        shards,
        mesh=mesh,
        in_specs=(
            P(None, None, "row", "col"),
            P(None, "row", "col"),
            P(None, "row", "col"),
            P(None, "row", "col"),
            P(None, "row", "col"),
        ),
        out_specs=(P(None, None, "row", "col"), P()),
        check_vma=False,
    )
```

```python
import functools

import jax
import jax.numpy as jnp
from jax import lax
from jax.experimental import pallas as pl
from jax.experimental.pallas import tpu as pltpu
from jax.sharding import PartitionSpec as P

MESH = pl.DeviceIdType.MESH
F32 = jnp.float32
BF16 = jnp.bfloat16
INNER = 4
WIDTH = 8
CHUNK = 8
GROUP = 2
NF = 7
SPR, CEN, XP, XM, XA, YA, DIF = range(NF)
LOW, HIGH, LEFT, RIGHT = range(4)


def lanes(shape):
    return lax.broadcasted_iota(jnp.int32, shape, 1)


def roll(x, shift):
    return pltpu.roll(x, shift % 128, 1)


def put_row(ref, r, value):
    n, rows, width = ref.shape
    ref.reshape(n * rows, width)[pl.ds(r, n, stride=rows), :] = value


def wide(coef, nprobe):
    return jnp.broadcast_to(coef[None], (nprobe // 8, 8, 128)).reshape(nprobe, 128)


def halo_kernel(
    dims,
    probes_hbm, spread_hbm, advx_hbm, advy_hbm, diff_hbm,
    z_hbm, g_hbm,
    probes, coefs, turn, omega, scaled, tang, co, edge, ring, ring_t,
    pack, pack_l, pack_r, wrap, wrap_l, wrap_r,
    to_low, to_high, from_low, from_high,
    back, strip, zbuf, gbuf, red_a, red_b, red_c, total,
    in_sem, out_sem, send_sem, recv_sem, red_send, red_recv, news,
):
    nprobe, nlev, nrow, nrd, ncd = dims
    outer = ncd // INNER
    row = lax.axis_index("row")
    col = lax.axis_index("col")
    zi = col // INNER
    xi = lax.rem(col, INNER)
    half = nprobe // 2

    core = lax.rem(row, 2)
    chip = (row // 2) * INNER + xi
    plane = (nrd // 2) * INNER

    def far(o, count):
        return min(o, count - o)

    yi = row // 2
    tall = nrd // 2
    steps = [(dy, dx) for dy in range(tall) for dx in range(INNER)][1:]
    steps.sort(key=lambda st: -(far(st[0], tall) + far(st[1], INNER)))
    in_plane = [
        (lax.rem(yi + dy, tall) * 2 + core, zi * INNER + lax.rem(xi + dx, INNER)) for dy, dx in steps
    ]
    in_line = [
        (row, lax.rem(zi + o, outer) * INNER + xi) for o in sorted(range(1, outer), key=lambda o: -far(o, outer))
    ]
    other = (row + 1 - 2 * core, col)
    barrier = pltpu.get_barrier_semaphore()
    greet = [(row, lax.rem(col + o, ncd)) for o in (1, ncd - 1)]
    greet += [(lax.rem(row + o, nrd), col) for o in (1, nrd - 1)]
    next_x = [(row, zi * INNER + lax.rem(xi + o, INNER)) for o in (1, INNER - 1)]
    next_y = [(lax.rem(yi + o, tall) * 2 + core, col) for o in (1, tall - 1)]
    next_z = [(row, lax.rem(zi + o, outer) * INNER + xi) for o in (1, outer - 1)]
    skip_z = [(row, lax.rem(zi + o, outer) * INNER + xi) for o in (2, outer - 2)]
    greet += next_z + next_y + next_x + [other]
    for device in greet:
        pl.semaphore_signal(barrier, inc=1, device_id=device, device_id_type=MESH)
    signals = len(greet)

    loads = []
    for i, src in enumerate((spread_hbm, advx_hbm, advy_hbm, diff_hbm)):
        loads.append(pltpu.make_async_copy(src, coefs.at[i], in_sem.at[i]))

    gbuf[...] = jnp.zeros(gbuf.shape, F32)

    def probe_load(g):
        at = pl.ds(g * GROUP, GROUP)
        return pltpu.make_async_copy(probes_hbm.at[:, at], probes.at[:, at], in_sem.at[4 + g])

    for g in range(nlev // GROUP):
        loads.append(probe_load(g))
    for load in loads:
        load.start()

    def tell(n, devices):
        for device in devices:
            pl.semaphore_signal(news.at[n], inc=1, device_id=device, device_id_type=MESH)

    def hear(n):
        pl.semaphore_wait(news.at[n], 2)


    for load in loads[:4]:
        load.wait()

    def spread_coefs(l, carry):
        ax = coefs[1, l] * (1.0 / 12.0)
        ay = coefs[2, l] * (1.0 / 12.0)
        d = coefs[3, l]
        fields = (coefs[0, l], 0.6 - 4.0 * d, d + 8.0 * ax, d - 8.0 * ax, ax, ay, d)
        for f in range(NF):
            for r in range(nrow):
                co[f, l, r] = jnp.broadcast_to(fields[f][r : r + 1], (8, 128))
        return carry

    lax.fori_loop(0, nlev, spread_coefs, 0)

    lane16 = lanes((half, 128))
    quad = lax.rem(lane16, 4)
    lane_l = lanes((nlev, 128))
    quad_l = lax.rem(lane_l, 4)

    def packed(field):
        acc = jnp.zeros((nlev, 128), F32)
        for r in range(nrow):
            acc = jnp.where(lax.div(lane_l, 4) == r, roll(coefs[field, :, r, :], 4 * r + 2), acc)
        return jnp.where(lane_l < 64, acc, roll(acc, 64))

    pa = packed(2) * (1.0 / 12.0)
    pd = packed(3)
    near_edge = jnp.where(quad_l == 1, pd + 8.0 * pa, jnp.where(quad_l == 2, pd - 8.0 * pa, 0.0))
    for l in range(nlev):
        edge[0, l] = jnp.broadcast_to(near_edge[l : l + 1], (8, 128))
        edge[1, l] = jnp.broadcast_to(pa[l : l + 1], (8, 128))

    for k, shape in enumerate(((256, 256), (512, 128))):
        src_lane = lax.rem(lax.broadcasted_iota(jnp.int32, shape, 0), 128)
        src_part = lax.div(lax.broadcasted_iota(jnp.int32, shape, 0), 128)
        out_col = lax.broadcasted_iota(jnp.int32, shape, 1)
        step = lax.rem(src_lane - lax.rem(out_col, 128) + 128, 128)
        first = jnp.where(step == 1, 8.0, jnp.where(step == 127, -8.0, jnp.where(step == 2, -1.0, jnp.where(step == 126, 1.0, 0.0))))
        both = jnp.where(jnp.logical_or(step == 1, step == 127), 1.0, 0.0)
        if k == 0:
            ring[...] = jnp.where(out_col < 128, first, both).astype(BF16)
        else:
            ring_t[...] = jnp.where(src_part < 2, both, -first).astype(BF16)

    has = {LOW: row > 0, HIGH: row < nrd - 1, LEFT: col > 0, RIGHT: col < ncd - 1}
    target = {
        LOW: (lax.rem(row + nrd - 1, nrd), col),
        HIGH: (lax.rem(row + 1, nrd), col),
        LEFT: (row, lax.rem(col + ncd - 1, ncd)),
        RIGHT: (row, lax.rem(col + 1, ncd)),
    }
    def some(g):
        return pl.ds(g * GROUP, GROUP)

    rims = (
        {
            LOW: (lambda g: scaled.at[some(g), 2:4], lambda g: scaled.at[some(g), nrow + 2 : nrow + 4]),
            HIGH: (lambda g: scaled.at[some(g), nrow : nrow + 2], lambda g: scaled.at[some(g), 0:2]),
            LEFT: (lambda g: pack.at[some(g)], lambda g: pack_r.at[some(g)]),
            RIGHT: (lambda g: pack.at[some(g)], lambda g: pack_l.at[some(g)]),
        },
        {
            LOW: (lambda g: to_low.at[some(g)], lambda g: from_high.at[some(g)]),
            HIGH: (lambda g: to_high.at[some(g)], lambda g: from_low.at[some(g)]),
            LEFT: (lambda g: wrap.at[some(g)], lambda g: wrap_r.at[some(g)]),
            RIGHT: (lambda g: wrap.at[some(g)], lambda g: wrap_l.at[some(g)]),
        },
    )
    opposite = {LOW: HIGH, HIGH: LOW, LEFT: RIGHT, RIGHT: LEFT}

    def rim(phase, side, g):
        src, dst = rims[phase][side]
        return pltpu.make_async_remote_copy(
            src_ref=src(g),
            dst_ref=dst(g),
            send_sem=send_sem.at[phase, side, g],
            recv_sem=recv_sem.at[phase, side, g],
            device_id=target[side],
            device_id_type=MESH,
        )

    def send(phase, g):
        for side in (LEFT, RIGHT, LOW, HIGH):
            @pl.when(has[side])
            def _():
                rim(phase, side, g).start()

    def receive(phase, g):
        for side in (LEFT, RIGHT, LOW, HIGH):
            @pl.when(has[side])
            def _():
                rim(phase, opposite[side], g).wait_recv()

    def sent(phase, g):
        for side in (LOW, HIGH, LEFT, RIGHT):
            @pl.when(has[side])
            def _():
                rim(phase, side, g).wait_send()

    zero_rows = jnp.zeros((nlev, 2, nprobe, 128), F32)
    zero_pack = jnp.zeros((nlev, half, 128), F32)

    @pl.when(row == 0)
    def _():
        scaled[:, 0:2] = zero_rows
        from_low[...] = zero_rows

    @pl.when(row == nrd - 1)
    def _():
        scaled[:, nrow + 2 : nrow + 4] = zero_rows
        from_high[...] = zero_rows

    @pl.when(col == 0)
    def _():
        pack_l[...] = zero_pack
        wrap_l[...] = zero_pack

    @pl.when(col == ncd - 1)
    def _():
        pack_r[...] = zero_pack
        wrap_r[...] = zero_pack


    def put(acc, r, value):
        slot = lax.div(lane16, 4)
        acc = jnp.where(slot == r, roll(value[:half], 4 * r + 2), acc)
        return jnp.where(slot == r + 16, roll(value[half:], 4 * r + 66), acc)

    wide_lane = lanes((nprobe, 128))
    at_edge = jnp.logical_or(wide_lane < 2, wide_lane >= 126)

    def take(corr, r):
        both = jnp.concatenate([roll(corr, -(4 * r + 2)), roll(corr, -(4 * r + 66))], axis=0)
        return jnp.where(at_edge, both, 0.0)

    def scale_level(l, turn):
        for p in range(nprobe):
            turn[p * nrow : (p + 1) * nrow, :] = probes[p, l].astype(F32)
        acc = jnp.zeros((half, 128), F32)
        for r in range(nrow):
            om = turn[pl.ds(r, nprobe, stride=nrow), :]
            omega[l, r] = om.astype(BF16)
            v = om * wide(co[SPR, l, r], nprobe)
            scaled[l, r + 2] = v
            acc = put(acc, r, v)
        pack[l] = acc

    def scale_group(g):
        probe_load(g).wait()
        for i in range(GROUP):
            scale_level(g * GROUP + i, turn.at[i])

    scale_group(0)
    pl.semaphore_wait(barrier, signals)
    send(0, 0)

    def scale_next(g, carry):
        scale_group(g)
        send(0, g)
        return carry

    lax.fori_loop(1, nlev // GROUP, scale_next, 0)
    tell(0, next_x)
    tell(1, next_z)

    def halves(x):
        high = x.astype(BF16)
        return high, (x - high.astype(F32)).astype(BF16)

    def tangent_own(l, carry):
        above = jnp.minimum(l + 1, nlev - 1)
        below = jnp.maximum(l - 1, 0)
        acc = jnp.zeros((half, 128), F32)
        for r0 in range(0, nrow, CHUNK):
            v = scaled[l, r0 + 2 : r0 + 2 + CHUNK].reshape(CHUNK * nprobe, 128)
            cols = lax.dot_general(
                jnp.concatenate(halves(v), axis=1), ring[...], (((1,), (0,)), ((), ())), preferred_element_type=F32
            )
            for r in range(r0, r0 + CHUNK):
                at = slice((r - r0) * nprobe, (r - r0 + 1) * nprobe)
                c = [wide(co[f, l, r], nprobe) for f in range(NF)]
                t = c[CEN] * scaled[l, r + 2] + 0.2 * (scaled[above, r + 2] + scaled[below, r + 2])
                if r + 1 < nrow:
                    t = t + c[XP] * scaled[l, r + 3]
                if r >= 1:
                    t = t + c[XM] * scaled[l, r + 1]
                if r >= 2 and r + 2 < nrow:
                    t = t + c[XA] * (scaled[l, r] - scaled[l, r + 4])
                elif r >= 2:
                    t = t + c[XA] * scaled[l, r]
                else:
                    t = t - c[XA] * scaled[l, r + 4]
                t = t + c[YA] * cols[at, :128] + c[DIF] * cols[at, 128:]
                tang[l, r] = t
                if 2 <= r < nrow - 2:
                    acc = put(acc, r, t)
        strip[l] = acc
        return carry

    lax.fori_loop(0, nlev, tangent_own, 0, unroll=2)
    hear(0)
    hear(1)
    tell(2, next_y)
    tell(3, skip_z)

    def tangent_outer(l):
        e1 = wide(edge[0, l], half)
        ea = wide(edge[1, l], half)
        diff = jnp.where(quad < 2, pack_l[l], pack_r[l]) - pack[l]
        near = jnp.where(quad == 1, roll(diff, -1), roll(diff, 1))
        far = jnp.where(quad < 2, -roll(diff, -2), roll(diff, 2))
        corr = e1 * near + ea * far
        acc = strip[l] + corr
        ends = {}
        last = nrow - 1

        def coef(f, r):
            return wide(co[f, l, r], nprobe)

        rim_terms = {
            0: coef(XM, 0) * scaled[l, 1] + coef(XA, 0) * scaled[l, 0],
            1: coef(XA, 1) * scaled[l, 1],
            last - 1: -(coef(XA, last - 1) * scaled[l, nrow + 2]),
            last: coef(XP, last) * scaled[l, nrow + 2] - coef(XA, last) * scaled[l, nrow + 3],
        }
        for r in rim_terms:
            t = tang[l, r] + rim_terms[r] + take(corr, r)
            tang[l, r] = t
            ends[r] = t
            acc = put(acc, r, t)

        to_low[l, 0] = coef(XA, 0) * ends[0]
        to_low[l, 1] = coef(XM, 0) * ends[0] + coef(XA, 1) * ends[1]
        to_high[l, 0] = coef(XP, last) * ends[last] - coef(XA, last - 1) * ends[last - 1]
        to_high[l, 1] = -(coef(XA, last) * ends[last])
        u = ea * acc
        w = e1 * acc
        wrap[l] = jnp.where(quad < 2, roll(u, -2), -roll(u, 2)) + jnp.where(
            quad == 1, roll(w, -1), jnp.where(quad == 2, roll(w, 1), 0.0)
        )
        return corr

    def tangent_rims(g, carry):
        group = [g * GROUP + i for i in range(GROUP)]
        receive(0, g)
        corrs = [tangent_outer(l) for l in group]
        send(1, g)
        for l, corr in zip(group, corrs):
            for r in range(2, nrow - 2):
                tang[l, r] = tang[l, r] + take(corr, r)
        return carry

    lax.fori_loop(0, nlev // GROUP, tangent_rims, 0)
    hear(2)
    hear(3)
    tell(4, next_y)

    def adjoint_own(l, carry):
        above = jnp.minimum(l + 1, nlev - 1)
        below = jnp.maximum(l - 1, 0)
        for r0 in range(0, nrow, CHUNK):
            parts = []
            for r in range(r0, r0 + CHUNK):
                w = tang[l, r]
                parts.append(
                    jnp.concatenate(
                        halves(wide(co[DIF, l, r], nprobe) * w) + halves(wide(co[YA, l, r], nprobe) * w), axis=1
                    )
                )
            cols = lax.dot_general(
                jnp.concatenate(parts, axis=0), ring_t[...], (((1,), (0,)), ((), ())), preferred_element_type=F32
            )
            for r in range(r0, r0 + CHUNK):
                b = cols[(r - r0) * nprobe : (r - r0 + 1) * nprobe]
                b = b + wide(co[CEN, l, r], nprobe) * tang[l, r] + 0.2 * (tang[above, r] + tang[below, r])
                if r + 1 < nrow:
                    b = b + wide(co[XM, l, r + 1], nprobe) * tang[l, r + 1]
                if r >= 1:
                    b = b + wide(co[XP, l, r - 1], nprobe) * tang[l, r - 1]
                if r + 2 < nrow:
                    b = b + wide(co[XA, l, r + 2], nprobe) * tang[l, r + 2]
                if r >= 2:
                    b = b - wide(co[XA, l, r - 2], nprobe) * tang[l, r - 2]
                back[l, r] = b
        return carry

    lax.fori_loop(0, nlev, adjoint_own, 0, unroll=2)
    hear(4)

    def sketch_level(l):
        corr = jnp.where(quad < 2, wrap_r[l], wrap_l[l]) - wrap[l]
        left, right = [], []
        for r in range(nrow):
            b = back[l, r] + take(corr, r)
            if r < 2:
                b = b + from_low[l, r]
            if r >= nrow - 2:
                b = b + from_high[l, r - (nrow - 2)]
            om = omega[l, r]
            sk = om.astype(F32) + wide(co[SPR, l, r], nprobe) * b
            hi = sk.astype(BF16)
            lo = (sk - hi.astype(F32)).astype(BF16)
            z = jnp.concatenate([hi, lo], axis=0)
            zbuf[l, r] = z
            right.append(z)
            left.append(jnp.concatenate([hi, om], axis=0))
        return lax.dot_general(
            jnp.concatenate(left, axis=1),
            jnp.concatenate(right, axis=1),
            (((1,), (1,)), ((), ())),
            preferred_element_type=F32,
        )

    def sketch_rims(g, gram):
        group = [g * GROUP + i for i in range(GROUP)]
        receive(1, g)
        for l in group:
            gram = gram + sketch_level(l)
        pltpu.make_async_copy(zbuf.at[some(g)], z_hbm.at[some(g)], out_sem.at[g]).start()
        return gram

    gram = lax.fori_loop(0, nlev // GROUP, sketch_rims, jnp.zeros((2 * nprobe, 2 * nprobe), F32))

    gbuf[:, 0 : 2 * nprobe] = gram
    full = gbuf[...]
    high, probe = full[:nprobe], full[nprobe:]
    own = high + 2.0 * roll(high, -nprobe)
    both = jnp.where(wide_lane < nprobe, own, roll(probe, nprobe) + probe)
    part = jnp.where(lane16 < 64, both[:half], roll(both[half:], 64))

    pair_part = red_a
    pair_part[0] = part
    swap = pltpu.make_async_remote_copy(
        src_ref=pair_part.at[0], dst_ref=pair_part.at[1], send_sem=red_send.at[0, 0], recv_sem=red_recv.at[0, 0],
        device_id=other, device_id_type=MESH,
    )
    swap.start()
    swap.wait_recv()
    quarter = half // 2
    mine = pl.ds(pl.multiple_of(core * quarter, quarter), quarter)
    part = pair_part[0, mine] + pair_part[1, mine]

    def finish(g, carry):
        sent(0, g)
        sent(1, g)
        pltpu.make_async_copy(zbuf.at[some(g)], z_hbm.at[some(g)], out_sem.at[g]).wait()
        return carry

    pending = [swap]
    for s, (buf, count, me, reach) in enumerate(((red_c, outer, zi, in_line), (red_b, plane, chip, in_plane))):
        buf[me] = part
        stage = []
        for o, device in enumerate(reach):
            stage.append(
                pltpu.make_async_remote_copy(
                    src_ref=buf.at[me],
                    dst_ref=buf.at[me],
                    send_sem=red_send.at[s + 1, o],
                    recv_sem=red_recv.at[s + 1, o],
                    device_id=device,
                    device_id_type=MESH,
                )
            )
            stage[-1].start()
        if s == 0:
            lax.fori_loop(0, nlev // GROUP, finish, 0)
        for copy in pending:
            copy.wait_send()
        pending = stage
        for copy in reversed(stage):
            copy.wait_recv()
        terms = [buf[o] for o in range(count)]
        while len(terms) > 1:
            terms = [sum(terms[i : i + 2][1:], terms[i]) for i in range(0, len(terms), 2)]
        part = terms[0]
    total[mine] = part
    join = pltpu.make_async_remote_copy(
        src_ref=total.at[mine], dst_ref=g_hbm.at[mine], send_sem=red_send.at[0, 1], recv_sem=red_recv.at[0, 1],
        device_id=other, device_id_type=MESH,
    )
    join.start()
    keep = pltpu.make_async_copy(total.at[mine], g_hbm.at[mine], in_sem.at[0])
    keep.start()
    for copy in pending:
        copy.wait_send()
    keep.wait()
    join.wait_send()
    join.wait_recv()


def basis_kernel(nprobe, nlev, nrow, scale, g_hbm, z_hbm, basis_hbm, factor_hbm, gbuf, zbuf, obuf, fbuf, in_sem, out_sem):
    def load(l):
        return pltpu.make_async_copy(z_hbm.at[l], zbuf.at[l], in_sem.at[l])

    def store(l):
        return pltpu.make_async_copy(obuf.at[l], basis_hbm.at[:, l], out_sem.at[l])

    sums = pltpu.make_async_copy(g_hbm, gbuf, in_sem.at[nlev])
    sums.start()
    for l in range(nlev):
        load(l).start()
    half = nprobe // 2
    sums.wait()
    g = gbuf[...]
    both = jnp.concatenate([g, roll(g, 64)], axis=0)
    flip = both.T
    lane = lanes((nprobe, 128))
    sub = lax.broadcasted_iota(jnp.int32, (nprobe, 128), 0)
    pad = jnp.zeros((nprobe, 128 - nprobe), F32)
    flip_g = jnp.concatenate([flip[:nprobe], pad], axis=1)
    flip_c = jnp.concatenate([flip[nprobe : 2 * nprobe], pad], axis=1)
    sym_g = 0.5 * (both + flip_g)
    sym_c = 0.5 * (roll(both, -nprobe) + flip_c)
    m = jnp.where(lane < nprobe, sym_g, jnp.where(jnp.logical_and(lane >= 64, lane < 64 + nprobe), roll(sym_c, 64), 0.0))
    m = jnp.where(jnp.logical_or(lane == sub + nprobe, lane == sub + 64 + nprobe), 1.0, m)
    first = lane < 64
    piv = jnp.ones((nprobe, 128), F32)
    for k0 in range(0, nprobe, WIDTH):
        cols = [
            jnp.where(
                first,
                jnp.broadcast_to(m[:, k : k + 1], (nprobe, 128)),
                jnp.broadcast_to(m[:, 64 + k : 65 + k], (nprobe, 128)),
            )
            for k in range(k0, k0 + WIDTH)
        ]
        for j in range(WIDTH):
            k = k0 + j
            p = cols[j][k : k + 1]
            inv = 1.0 / p
            piv = jnp.where(sub == k, p, piv)
            below = jnp.where(sub > k, cols[j], 0.0)
            for i in range(j + 1, WIDTH):
                cols[i] = cols[i] - below * (cols[i][k : k + 1] * inv)
            m = m - below * (m[k : k + 1] * inv)
    m = m * (1.0 / jnp.sqrt(piv))
    upper = jnp.where(jnp.logical_and(lane >= sub, lane < nprobe), m, 0.0)
    inv_g = jnp.where(lane <= sub, roll(m, -nprobe), 0.0)
    inv_c = jnp.where(lane <= sub, roll(m, -(64 + nprobe)), 0.0)
    factor = lax.dot_general(
        upper, inv_c, (((1,), (1,)), ((), ())), precision=lax.Precision.HIGHEST, preferred_element_type=F32
    )
    fbuf[...] = factor
    leave = pltpu.make_async_copy(fbuf, factor_hbm, out_sem.at[nlev])
    leave.start()
    a = inv_g * scale
    a_hi = a.astype(BF16)
    a_lo = (a - a_hi.astype(F32)).astype(BF16)
    twice = jnp.where(lane < nprobe, a_hi.astype(F32), roll(a_hi.astype(F32), nprobe))
    twice_lo = jnp.where(lane < nprobe, a_lo.astype(F32), roll(a_lo.astype(F32), nprobe))
    lhs = jnp.concatenate([twice, twice_lo], axis=0).astype(BF16)[:, : 2 * nprobe]

    def level(l, carry):
        load(l).wait()
        for r in range(0, nrow, 2):
            out = lax.dot_general(
                lhs,
                jnp.concatenate([zbuf[l, r], zbuf[l, r + 1]], axis=1),
                (((1,), (0,)), ((), ())),
                preferred_element_type=F32,
            )
            out = out[:nprobe] + out[nprobe:]
            put_row(obuf.at[l], r, out[:, :128])
            put_row(obuf.at[l], r + 1, out[:, 128:])
        store(l).start()
        return carry

    lax.fori_loop(0, nlev, level, 0)

    def finish(l, carry):
        store(l).wait()
        return carry

    lax.fori_loop(0, nlev, finish, 0)
    leave.wait()


def shards(probes, spread, adv_x, adv_y, diffusivity):
    nprobe, nlev, nrow, ncol = probes.shape
    nrd = lax.axis_size("row")
    ncd = lax.axis_size("col")
    half = nprobe // 2
    inputs = [pltpu.with_memory_space_constraint(x, pltpu.HBM) for x in (probes, spread, adv_x, adv_y, diffusivity)]
    any_spec = pl.BlockSpec(memory_space=pl.ANY)
    rows2 = pltpu.VMEM((nlev, 2, nprobe, ncol), F32)
    strip = pltpu.VMEM((nlev, half, ncol), F32)
    plane = (nrd // 2) * INNER
    most = max(2, plane, ncd // INNER)
    z, g = pl.pallas_call(
        functools.partial(halo_kernel, (nprobe, nlev, nrow, nrd, ncd)),
        out_shape=(
            jax.ShapeDtypeStruct((nlev, nrow, 2 * nprobe, ncol), BF16),
            jax.ShapeDtypeStruct((half, ncol), F32),
        ),
        in_specs=[any_spec] * 5,
        out_specs=(any_spec, any_spec),
        scratch_shapes=[
            pltpu.VMEM((nprobe, nlev, nrow, ncol), BF16),
            pltpu.VMEM((4, nlev, nrow, ncol), F32),
            pltpu.VMEM((GROUP, nprobe * nrow, ncol), F32),
            pltpu.VMEM((nlev, nrow, nprobe, ncol), BF16),
            pltpu.VMEM((nlev, nrow + 4, nprobe, ncol), F32),
            pltpu.VMEM((nlev, nrow, nprobe, ncol), F32),
            pltpu.VMEM((NF, nlev, nrow, 8, ncol), F32),
            pltpu.VMEM((2, nlev, 8, ncol), F32),
            pltpu.VMEM((256, 256), BF16),
            pltpu.VMEM((512, 128), BF16),
            strip, strip, strip, strip, strip, strip,
            rows2, rows2, rows2, rows2,
            pltpu.VMEM((nlev, nrow, nprobe, ncol), F32),
            strip,
            pltpu.VMEM((nlev, nrow, 2 * nprobe, ncol), BF16),
            pltpu.VMEM((2 * nprobe, ncol), F32),
            pltpu.VMEM((2, half, ncol), F32),
            pltpu.VMEM((plane, half // 2, ncol), F32),
            pltpu.VMEM((ncd // INNER, half // 2, ncol), F32),
            pltpu.VMEM((half, ncol), F32),
            pltpu.SemaphoreType.DMA((4 + nlev // GROUP,)),
            pltpu.SemaphoreType.DMA((nlev // GROUP,)),
            pltpu.SemaphoreType.DMA((2, 4, nlev // GROUP)),
            pltpu.SemaphoreType.DMA((2, 4, nlev // GROUP)),
            pltpu.SemaphoreType.DMA((3, most)),
            pltpu.SemaphoreType.DMA((3, most)),
            pltpu.SemaphoreType.REGULAR((5,)),
        ],
        compiler_params=pltpu.CompilerParams(
            collective_id=0, has_side_effects=True, vmem_limit_bytes=40 * 1024 * 1024
        ),
        name="sketch_and_sums",
    )(*inputs)
    scale = float(nlev * nrow * ncol * nrd * ncd) ** 0.5
    basis, factor = pl.pallas_call(
        functools.partial(basis_kernel, nprobe, nlev, nrow, scale),
        out_shape=(
            jax.ShapeDtypeStruct((nprobe, nlev, nrow, ncol), F32),
            jax.ShapeDtypeStruct((nprobe, nprobe), F32),
        ),
        in_specs=[any_spec, any_spec],
        out_specs=(any_spec, any_spec),
        scratch_shapes=[
            pltpu.VMEM((half, ncol), F32),
            pltpu.VMEM((nlev, nrow, 2 * nprobe, ncol), BF16),
            pltpu.VMEM((nlev, nprobe, nrow, ncol), F32),
            pltpu.VMEM((nprobe, nprobe), F32),
            pltpu.SemaphoreType.DMA((nlev + 1,)),
            pltpu.SemaphoreType.DMA((nlev + 1,)),
        ],
        compiler_params=pltpu.CompilerParams(vmem_limit_bytes=24 * 1024 * 1024),
        name="factors_and_basis",
    )(g, z)
    return basis, factor


def solution(mesh):
    return jax.shard_map(
        shards,
        mesh=mesh,
        in_specs=(
            P(None, None, "row", "col"),
            P(None, "row", "col"),
            P(None, "row", "col"),
            P(None, "row", "col"),
            P(None, "row", "col"),
        ),
        out_specs=(P(None, None, "row", "col"), P()),
        check_vma=False,
    )
```
